32 devices in a mesh: rep: 16 (over z, x, core), shard: 2 (over y).
Axes of the slice: x: 2, y: 2, z: 4, core: 2. Of those that a mesh axis runs over, the one named last changes fastest.
Arguments:
- tokens: bfloat16 [4096, 1024], P(('rep', 'shard')), may hold values from -6 to 6
- cotangent: bfloat16 [4096, 1024], P(('rep', 'shard')), may hold values from -6 to 6
- lengths: int32 [32], P(('rep', 'shard')), may hold values from 16 to 128, as said below
- qkv_weight: bfloat16 [1024, 3072], P('shard'), may hold values from -0.1875 to 0.1875
- qkv_bias: bfloat16 [3072], P('shard'), may hold values from -1 to 1
- dense_weight: bfloat16 [1024, 1024], P('shard'), may hold values from -1 to 1
- dense_bias: bfloat16 [1024], P('shard'), may hold values from -1 to 1
- in_weight: bfloat16 [1024, 4096], P('shard'), may hold values from -0.1875 to 0.1875
- in_bias: bfloat16 [4096], P('shard'), may hold values from -1 to 1
- out_weight: bfloat16 [4096, 1024], P('shard'), may hold values from -0.09375 to 0.09375
- out_bias: bfloat16 [1024], P('shard'), may hold values from -1 to 1
- norm1_gain: bfloat16 [1024], P('shard'), may hold values from 0.5 to 1.5
- norm1_bias: bfloat16 [1024], P('shard'), may hold values from -1 to 1
- norm2_gain: bfloat16 [1024], P('shard'), may hold values from 0.5 to 1.5
- norm2_bias: bfloat16 [1024], P('shard'), may hold values from -1 to 1
Outputs:
- result: bfloat16 [4096, 1024], P(('rep', 'shard'))
- grad_tokens: bfloat16 [4096, 1024], P(('rep', 'shard'))
- grad_qkv_weight: float32 [1024, 3072], P('shard')
- grad_qkv_bias: float32 [3072], P('shard')
- grad_dense_weight: float32 [1024, 1024], P('shard')
- grad_dense_bias: float32 [1024], P('shard')
- grad_in_weight: float32 [1024, 4096], P('shard')
- grad_in_bias: float32 [4096], P('shard')
- grad_out_weight: float32 [4096, 1024], P('shard')
- grad_out_bias: float32 [1024], P('shard')
- grad_norm1_gain: float32 [1024], P('shard')
- grad_norm1_bias: float32 [1024], P('shard')
- grad_norm2_gain: float32 [1024], P('shard')
- grad_norm2_bias: float32 [1024], P('shard')
The draws below stay inside these ranges and needn't reach their ends.
Inputs may be any that keep to these rules, and one draw needn't show every extreme that they name: `lengths`: each device's sequence has a length of its own; in every draw some device's sequence fills all 128 slots.
All inputs are finite; a program needn't handle non-finite values.
Results may differ from the reference program's by a relative error of at most 0.0084.
Values may be sent and summed in bfloat16 or wider, within the bound.
No kernel may reach another device: no remote copies, remote signals or barrier semaphores. Data moves between devices by JAX's collectives and lax.ppermute only.
A program may use at most 192 MiB of HBM per device.

```python
import math
import jax
import jax.numpy as jnp
from jax import lax

D = 1024
HEADS = 16
HEAD_DIM = 64
ROT = 16
FF = 4096
TOK_DEV = 128
SEQS = 32
TOKENS = 4096


def draw_lengths(key, part):
    key = jax.random.fold_in(key, 7)
    first_key, second_key = jax.random.split(key)
    drawn = jax.random.randint(first_key, (SEQS,), TOK_DEV // 8, TOK_DEV + 1)
    chosen = jax.random.randint(second_key, (), 0, SEQS)
    return jnp.where(jnp.arange(SEQS) == chosen, TOK_DEV, drawn).astype(jnp.int32)


def levels(key, extent, pieces, least, largest):
    loudness = 1.0
    for axis_at, shards_of in pieces:
        steps = jax.random.uniform(jax.random.fold_in(jax.random.fold_in(key, 6), axis_at), (shards_of,), jnp.float32, least / len(pieces), largest / len(pieces))
        loudness = loudness * jnp.repeat(jnp.exp(steps), extent[axis_at] // shards_of).reshape((-1,) + (1,) * (len(extent) - 1 - axis_at))
    return loudness


def noise(rng, extent, scale, limit, pieces=(), kind=jnp.bfloat16):
    factor_of = levels(rng, extent, pieces, -0.22, 0.18) if pieces else 1.0
    array = jax.random.normal(rng, extent, jnp.float32) * scale * factor_of
    return jnp.minimum(jnp.maximum(array, -limit), limit).astype(kind)


def setup_inputs(seed: int = 0) -> dict:
    keys = jax.random.split(jax.random.key(seed), 16)
    tokens = noise(keys[0], (TOKENS, D), 1.0, 6.0, ((0, 32),))
    cotangent = noise(keys[1], (TOKENS, D), 1.0, 6.0, ((0, 32),))
    lengths = draw_lengths(jax.random.fold_in(keys[15], 71), 0)
    qkv_weight = noise(keys[3], (D, 3 * D), D ** -0.5, 0.1875, ((0, 2),))
    qkv_bias = noise(keys[4], (3 * D,), 0.2, 1.0, ((0, 2),))
    dense_weight = noise(keys[5], (D, D), (D // 32) ** -0.5, 1.0, ((0, 2),))
    dense_bias = noise(keys[6], (D,), 0.2, 1.0, ((0, 2),))
    in_weight = noise(keys[7], (D, FF), D ** -0.5, 0.1875, ((0, 2),))
    in_bias = noise(keys[8], (FF,), 0.2, 1.0, ((0, 2),))
    out_weight = noise(keys[9], (FF, D), FF ** -0.5, 0.09375, ((0, 2),))
    out_bias = noise(keys[10], (D,), 0.2, 1.0, ((0, 2),))
    norm1_gain = jnp.clip(1.0 + 0.1 * jax.random.normal(keys[11], (D,), jnp.float32), 0.5, 1.5).astype(jnp.bfloat16)
    norm1_bias = noise(keys[12], (D,), 0.2, 1.0, ((0, 2),))
    norm2_gain = jnp.clip(1.0 + 0.1 * jax.random.normal(keys[13], (D,), jnp.float32), 0.5, 1.5).astype(jnp.bfloat16)
    norm2_bias = noise(keys[14], (D,), 0.2, 1.0, ((0, 2),))
    return {"tokens": tokens, "cotangent": cotangent, "lengths": lengths, "qkv_weight": qkv_weight, "qkv_bias": qkv_bias, "dense_weight": dense_weight, "dense_bias": dense_bias, "in_weight": in_weight, "in_bias": in_bias, "out_weight": out_weight, "out_bias": out_bias, "norm1_gain": norm1_gain, "norm1_bias": norm1_bias, "norm2_gain": norm2_gain, "norm2_bias": norm2_bias}


@jax.custom_vjp
def low(v):
    return lax.optimization_barrier(v.astype(jnp.bfloat16)).astype(jnp.float32)

@jax.custom_vjp
def low_back(v):
    return v

def low_keep(v):
    return (low(v), None)

def low_pass(kept, grad):
    return (grad,)

def back_keep(v):
    return (v, None)

def back_low(kept, grad):
    return (low(grad),)
low.defvjp(low_keep, low_pass)
low_back.defvjp(back_keep, back_low)

def layer_norm(values, gain, shift):
    centre = values - lax.optimization_barrier(jnp.mean(values, axis=-1, keepdims=True))
    spread = lax.optimization_barrier(jnp.mean(centre * centre, axis=-1, keepdims=True))
    return centre * lax.rsqrt(spread + 1e-05) * gain + shift

def rotary(values):
    seq_rows = values.shape[0]
    half_dims = ROT // 2
    inverse = 10000.0 ** (-(2.0 * jnp.arange(half_dims).astype(values.dtype)) / ROT)
    angles = jnp.arange(seq_rows).astype(values.dtype)[:, None] * inverse[None, :]
    cosine_table = jnp.cos(angles)[:, None, :]
    sine_table = jnp.sin(angles)[:, None, :]
    first_half = values[..., :half_dims]
    second_half = values[..., half_dims:ROT]
    return jnp.concatenate([first_half * cosine_table - second_half * sine_table, second_half * cosine_table + first_half * sine_table, values[..., ROT:]], axis=-1)

def sequence_forward(params, values, length):
    qkv_w, qkv_b, dense_w, dense_b, in_w, in_b, out_w, out_b, gain_one, shift_one, gain_two, shift_two = params
    highest = lax.Precision.HIGHEST
    seq_rows = values.shape[0]
    position = jnp.arange(seq_rows).astype(jnp.int32)
    live_rows = (position < length).astype(values.dtype)[:, None]
    normed = low(layer_norm(values, gain_one, shift_one))
    joint = low_back(jnp.dot(normed, qkv_w, precision=highest) + qkv_b)
    query = low(rotary(joint[:, :D].reshape(seq_rows, HEADS, HEAD_DIM)))
    key_rows = low(rotary(joint[:, D:2 * D].reshape(seq_rows, HEADS, HEAD_DIM)))
    value_rows = low(joint[:, 2 * D:].reshape(seq_rows, HEADS, HEAD_DIM))
    scores = low_back(jnp.einsum('thd,shd->hts', query, key_rows, precision=highest) * HEAD_DIM ** (-0.5))
    allowed = (position[None, :] <= position[:, None]) & (position[None, :] < length)
    scores = jnp.where(allowed[None], scores, -1e+30)
    probs = low(jax.nn.softmax(scores, axis=-1))
    context = low(low_back(jnp.einsum('hts,shd->thd', probs, value_rows, precision=highest))).reshape(seq_rows, D)
    attention = jnp.dot(context, dense_w, precision=highest) + dense_b
    normed_two = low(layer_norm(values, gain_two, shift_two))
    before = low_back(jnp.dot(normed_two, in_w, precision=highest) + in_b)
    active = low(jax.nn.gelu(before, approximate=False))
    mixed = jnp.dot(active, out_w, precision=highest) + out_b
    return values + live_rows * (attention + mixed)

def reference(tokens, cotangent, lengths, qkv_weight, qkv_bias, dense_weight, dense_bias, in_weight, in_bias, out_weight, out_bias, norm1_gain, norm1_bias, norm2_gain, norm2_bias):
    params = (qkv_weight.astype(jnp.float32), qkv_bias.astype(jnp.float32), dense_weight.astype(jnp.float32), dense_bias.astype(jnp.float32), in_weight.astype(jnp.float32), in_bias.astype(jnp.float32), out_weight.astype(jnp.float32), out_bias.astype(jnp.float32), norm1_gain.astype(jnp.float32), norm1_bias.astype(jnp.float32), norm2_gain.astype(jnp.float32), norm2_bias.astype(jnp.float32))
    seq_count = lengths.shape[0]
    seq_rows = tokens.shape[0] // seq_count
    group_size = math.gcd(seq_count, 16)

    def group_forward(params, block_values, block_lengths):
        return jax.vmap(sequence_forward, in_axes=(None, 0, 0))(params, block_values, block_lengths)
    checked = jax.checkpoint(group_forward)

    def whole(params, values):
        blocks = values.reshape(seq_count // group_size, group_size, seq_rows, D)
        block_lengths = lengths.reshape(seq_count // group_size, group_size)
        outputs = lax.map(lambda entry_pair: checked(params, entry_pair[0], entry_pair[1]), (blocks, block_lengths))
        return outputs.reshape(seq_count * seq_rows, D)
    output, backward = jax.vjp(whole, params, tokens.astype(jnp.float32))
    grad_params, grad_values = backward(cotangent.astype(jnp.float32))
    return (output.astype(jnp.bfloat16), grad_values.astype(jnp.bfloat16), grad_params[0], grad_params[1], grad_params[2], grad_params[3], grad_params[4], grad_params[5], grad_params[6], grad_params[7], grad_params[8], grad_params[9], grad_params[10], grad_params[11])
```

```python
import jax
import jax.numpy as jnp
from jax import lax
from jax.sharding import PartitionSpec as P

HEAD_DIM = 64
ROT = 16
F32 = jnp.float32
BF16 = jnp.bfloat16
EXTRA = 16


def rotary(values, turn):
    seq_rows = values.shape[-2]
    half = ROT // 2
    inverse = 10000.0 ** (-(2.0 * jnp.arange(half).astype(F32)) / ROT)
    angles = jnp.arange(seq_rows).astype(F32)[:, None] * inverse[None, :]
    cosine = jnp.cos(angles)
    sine = jnp.sin(angles) * turn
    first = values[..., :half]
    second = values[..., half:ROT]
    return jnp.concatenate(
        [first * cosine - second * sine, second * cosine + first * sine, values[..., ROT:]],
        axis=-1,
    )


def dot(left, right):
    return jnp.dot(left, right, preferred_element_type=F32)


def dot_nt(left, right):
    return lax.dot_general(left, right, (((1,), (1,)), ((), ())), preferred_element_type=F32)


def dot_tn(left, right):
    return lax.dot_general(left, right, (((0,), (0,)), ((), ())), preferred_element_type=F32)


def plan(mesh_shape, heads):
    shards, reps = mesh_shape["shard"], mesh_shape["rep"]
    split = 1
    while split < 4 and reps % (2 * split) == 0 and heads % (2 * split * shards) == 0:
        split *= 2
    return shards, reps, split


def make(mesh):
    def on_device(
        tokens,
        cotangent,
        lengths,
        qkv_weight,
        qkv_bias,
        dense_weight,
        dense_bias,
        in_weight,
        in_bias,
        out_weight,
        out_bias,
        norm1_gain,
        norm1_bias,
        norm2_gain,
        norm2_bias,
    ):
        seq_rows, width = tokens.shape
        heads = width // HEAD_DIM
        shards, reps, split = plan(dict(mesh.shape), heads)
        lines = reps // split
        group = shards * split
        owned = width // shards
        hidden = in_weight.shape[1]
        part_f = hidden // group
        part_h = width // group
        own_heads = part_h // HEAD_DIM
        shard = lax.axis_index("shard")
        rep = lax.axis_index("rep")
        slot = lax.rem(rep, split)
        line = rep // split
        block = shard * split + slot
        bits = []
        bit = split // 2
        while bit:
            bits.append(bit)
            bit //= 2

        def swap_rep(values, bit):
            return lax.ppermute(values, "rep", [(i, i ^ bit) for i in range(reps)])

        def swap_shard(values):
            return lax.ppermute(values, "shard", [(0, 1), (1, 0)])

        def gather_shard(values):
            if shards == 1:
                return values
            if shards == 2:
                return jnp.concatenate([values, swap_shard(values)], axis=0)
            return lax.all_gather(values, "shard", axis=0, tiled=True)

        def gather_rep(values):
            for bit in bits:
                values = jnp.concatenate([values, swap_rep(values, bit)], axis=0)
            return values

        def scatter_sum(values):
            for bit in reversed(bits):
                half = values.shape[0] // 2
                values = values[:half] + swap_rep(values[half:].astype(BF16), bit).astype(F32)
            if shards == 2:
                half = values.shape[0] // 2
                values = values[:half] + swap_shard(values[half:].astype(BF16)).astype(F32)
            elif shards > 2:
                values = lax.psum_scatter(
                    values.astype(BF16), "shard", scatter_dimension=0, tiled=True
                ).astype(F32)
            return values

        def ordered(mine, other, flag, axis):
            first = jnp.where(flag, other, mine)
            second = jnp.where(flag, mine, other)
            return jnp.concatenate([first, second], axis=axis)

        def columns_of(weight, parts, size):
            rows = weight.shape[0]
            cut = weight.reshape(rows, parts, group, size)

            def piece(at):
                return lax.dynamic_slice_in_dim(cut, at, 1, 2).reshape(rows, parts * size)

            if shards == 1:
                return piece(block)
            if shards == 2:
                other = swap_shard(piece((1 - shard) * split + slot))
                return ordered(piece(block), other, shard == 1, 0)
            picked = jnp.stack([piece(s * split + slot) for s in range(shards)], axis=0)
            return lax.all_to_all(picked, "shard", 0, 0, tiled=True).reshape(
                rows * shards, parts * size
            )

        def rows_exchange(grad):
            if shards == 1:
                return [grad]
            if shards == 2:
                mine = lax.dynamic_slice_in_dim(grad, shard * owned, owned, 0)
                other = swap_shard(lax.dynamic_slice_in_dim(grad, (1 - shard) * owned, owned, 0))
                return [jnp.where(shard == 1, other, mine), jnp.where(shard == 1, mine, other)]
            got = lax.all_to_all(grad, "shard", 0, 0, tiled=True)
            return [got[s * owned : (s + 1) * owned] for s in range(shards)]

        length = lengths[0]
        live = (jnp.arange(seq_rows) < length).astype(F32)[:, None]
        branch = (live * cotangent.astype(F32)).astype(BF16)
        halves = [dense_bias, out_bias, norm1_gain, norm1_bias, norm2_gain, norm2_bias]
        params = jnp.concatenate([qkv_bias] + halves)
        params = jnp.pad(params, (0, 8 * width - params.shape[0])).reshape(8, width)
        length_rows = jnp.broadcast_to(length.astype(BF16), (EXTRA - 8, width))
        packed = jnp.concatenate([tokens, params, length_rows], axis=0)
        packed = gather_shard(packed)
        branch_all = gather_shard(branch)
        in_w = columns_of(in_weight, 1, part_f)
        packed_all = gather_rep(packed).reshape(group, seq_rows + EXTRA, width)
        branch_all = gather_rep(branch_all)
        qkv_w = columns_of(qkv_weight, 3, part_h)

        by_shard = packed.reshape(shards, seq_rows + EXTRA, width)[:, seq_rows : seq_rows + 8]
        by_shard = by_shard.reshape(shards, 8 * width)
        if shards == 2:
            by_shard = jnp.where(shard == 1, by_shard[::-1], by_shard)

        def whole(at, size):
            return by_shard[:, at : at + size].reshape(shards * size).astype(F32)

        qkv_b = whole(0, 3 * owned)
        at = 3 * owned
        full = []
        for _ in halves:
            full.append(whole(at, owned))
            at += owned
        dense_b, out_b, gain_one, shift_one, gain_two, shift_two = full
        all_lengths = packed_all[:, seq_rows + 8, 0].astype(jnp.int32)
        rows = group * seq_rows
        values = packed_all[:, :seq_rows].reshape(rows, width).astype(F32)

        centre = values - jnp.mean(values, axis=-1, keepdims=True)
        spread = jnp.mean(centre * centre, axis=-1, keepdims=True)
        root = lax.rsqrt(spread + 1e-05)
        xhat = centre * root
        normed = (xhat * gain_one + shift_one).astype(BF16)
        normed_two = (xhat * gain_two + shift_two).astype(BF16)

        out_w = lax.dynamic_slice_in_dim(out_weight, slot * part_f, part_f, 0)
        in_b = lax.dynamic_slice_in_dim(in_bias, slot * part_f, part_f, 0).astype(F32)
        before = dot(normed_two, in_w) + in_b
        cdf = 0.5 * (1.0 + lax.erf(before * (0.5**0.5)))
        active = (before * cdf).astype(BF16)
        slope = cdf + before * jnp.exp(-0.5 * before * before) * 0.3989422804014327
        grad_before = (dot_nt(branch_all, out_w) * slope).astype(BF16)
        grad_out_w = dot_tn(active, branch_all).astype(BF16)
        grad_in_w = dot_tn(normed_two, grad_before).astype(BF16)
        grad_two = dot_nt(grad_before, in_w)

        scaling = HEAD_DIM ** (-0.5)
        bias = lax.dynamic_slice_in_dim(qkv_b.reshape(3, group, part_h), block, 1, 1)
        joint = dot(normed, qkv_w) + bias.reshape(3 * part_h)
        split_joint = joint.reshape(group, seq_rows, 3, own_heads, HEAD_DIM).transpose(2, 0, 3, 1, 4)
        query = rotary(split_joint[0], 1.0).astype(BF16)
        keys = rotary(split_joint[1], 1.0).astype(BF16)
        vals = split_joint[2].astype(BF16)
        position = jnp.arange(seq_rows)
        allowed = (position[None, :] <= position[:, None])[None] & (
            position[None, None, :] < all_lengths[:, None, None]
        )
        scores = jnp.einsum("bhpd,bhqd->bhpq", query, keys, preferred_element_type=F32) * scaling
        scores = jnp.where(allowed[:, None], scores, -1e30)
        raised = jnp.exp(scores - jnp.max(scores, axis=-1, keepdims=True))
        exact = raised / jnp.sum(raised, axis=-1, keepdims=True)
        probs = exact.astype(BF16)
        context = jnp.einsum("bhpq,bhqd->bhpd", probs, vals, preferred_element_type=F32)
        context = context.astype(BF16).transpose(0, 2, 1, 3).reshape(rows, part_h)
        dense_w = lax.dynamic_slice_in_dim(dense_weight, slot * part_h, part_h, 0)
        mixed = scatter_sum(dot(active, out_w) + dot(context, dense_w))
        result = (tokens.astype(F32) + live * (mixed + dense_b + out_b)).astype(BF16)

        grad_context = dot_nt(branch_all, dense_w).astype(BF16)
        grad_dense_w = dot_tn(context, branch_all).astype(BF16)
        grad_context = grad_context.reshape(group, seq_rows, own_heads, HEAD_DIM).transpose(0, 2, 1, 3)
        grad_probs = jnp.einsum(
            "bhpd,bhqd->bhpq", grad_context, vals, preferred_element_type=F32
        )
        grad_vals = jnp.einsum("bhpq,bhpd->bhqd", probs, grad_context, preferred_element_type=F32)
        grad_scores = (
            exact * (grad_probs - jnp.sum(grad_probs * exact, axis=-1, keepdims=True))
        ).astype(BF16)
        grad_query = jnp.einsum("bhpq,bhqd->bhpd", grad_scores, keys, preferred_element_type=F32)
        grad_keys = jnp.einsum("bhpq,bhpd->bhqd", grad_scores, query, preferred_element_type=F32)
        grad_joint = jnp.stack(
            [rotary(grad_query * scaling, -1.0), rotary(grad_keys * scaling, -1.0), grad_vals]
        ).astype(BF16)
        grad_joint = grad_joint.transpose(1, 3, 0, 2, 4).reshape(rows, 3 * part_h)
        grad_qkv_w = dot_tn(normed, grad_joint).astype(BF16)
        grad_one = dot_nt(grad_joint, qkv_w)

        inner = scatter_sum(grad_one * gain_one + grad_two * gain_two)
        own_xhat = xhat[:seq_rows] if shards <= 2 else None
        if own_xhat is None:
            own_xhat = lax.dynamic_slice_in_dim(xhat, shard * seq_rows, seq_rows, 0)
            own_root = lax.dynamic_slice_in_dim(root, shard * seq_rows, seq_rows, 0)
        else:
            own_root = root[:seq_rows]
        inner = (
            inner
            - jnp.mean(inner, axis=-1, keepdims=True)
            - own_xhat * jnp.mean(inner * own_xhat, axis=-1, keepdims=True)
        ) * own_root
        grad_tokens = (cotangent.astype(F32) + inner).astype(BF16)

        in_sum = jnp.sum(grad_before.astype(F32), axis=0)
        qkv_sum = jnp.sum(grad_joint.astype(F32), axis=0).reshape(3, 1, part_h)
        vectors = jnp.concatenate(
            [
                jnp.sum(grad_one * xhat, axis=0),
                jnp.sum(grad_one, axis=0),
                jnp.sum(grad_two * xhat, axis=0),
                jnp.sum(grad_two, axis=0),
                jnp.sum(branch.astype(F32), axis=0),
                lax.dynamic_update_slice_in_dim(jnp.zeros((hidden,), F32), in_sum, block * part_f, 0),
                lax.dynamic_update_slice_in_dim(
                    jnp.zeros((3, group, part_h), F32), qkv_sum, block, 1
                ).reshape(3 * width),
            ]
        )
        vectors = lax.psum(vectors, ("rep", "shard"))

        def own_part(at, size):
            piece = size // shards
            return lax.dynamic_slice_in_dim(vectors, at + shard * piece, piece, 0)

        in_parts = rows_exchange(grad_in_w)
        qkv_parts = rows_exchange(grad_qkv_w)
        chunks = [grad_out_w] + in_parts + [grad_dense_w] + qkv_parts
        if lines == 4:
            inner_line = (line == 1) | (line == 2)

            def line_permute(values, pairs):
                return lax.ppermute(
                    values,
                    "rep",
                    [(a * split + i, b * split + i) for a, b in pairs for i in range(split)],
                )

            summed = []
            for chunk in chunks:
                got = line_permute(chunk, [(0, 1), (3, 2)])
                near = lax.optimization_barrier((chunk.astype(F32) + got.astype(F32)).astype(BF16))
                got = line_permute(near, [(1, 2), (2, 1)])
                both = lax.optimization_barrier((near.astype(F32) + got.astype(F32)).astype(BF16))
                got = line_permute(both, [(1, 0), (2, 3)])
                summed.append(jnp.where(inner_line, both, got))
        else:
            groups = [[a * split + i for a in range(lines)] for i in range(split)]
            summed = [lax.psum(c, "rep", axis_index_groups=groups) for c in chunks]

        def gather_slots(values):
            values = values[None]
            for bit in reversed(bits):
                values = ordered(values, swap_rep(values, bit), (slot & bit) != 0, 0)
            return values

        summed = [gather_slots(c) for c in summed]
        total_out = summed[0].reshape(split * part_f, width).astype(F32)
        total_in = jnp.stack(summed[1 : 1 + shards])
        total_in = total_in.transpose(2, 0, 1, 3).reshape(owned, hidden).astype(F32)
        total_dense = summed[1 + shards].reshape(split * part_h, width).astype(F32)
        total_qkv = jnp.stack(summed[2 + shards :]).reshape(shards, split, owned, 3, part_h)
        total_qkv = total_qkv.transpose(2, 3, 0, 1, 4).reshape(owned, 3 * width).astype(F32)
        at_in = 5 * width
        at_qkv = at_in + hidden
        out_sum = own_part(4 * width, width)
        return (
            result,
            grad_tokens,
            total_qkv,
            own_part(at_qkv, 3 * width),
            total_dense,
            out_sum,
            total_in,
            own_part(at_in, hidden),
            total_out,
            out_sum,
            own_part(0, width),
            own_part(width, width),
            own_part(2 * width, width),
            own_part(3 * width, width),
        )

    return on_device


def solution(mesh):
    rows = P(("rep", "shard"), None)
    vector = P("shard")
    matrix = P("shard", None)
    weights = (matrix, vector)
    in_specs = (rows, rows, P(("rep", "shard"))) + 4 * weights + 4 * (vector,)
    out_specs = (rows, rows) + 4 * weights + 4 * (vector,)
    return jax.shard_map(
        make(mesh), mesh=mesh, in_specs=in_specs, out_specs=out_specs, check_vma=False
    )
```

```python
import jax
import jax.numpy as jnp
import numpy as np
from jax import lax
from jax.experimental import pallas as pl
from jax.experimental.pallas import tpu as pltpu
from jax.sharding import PartitionSpec as P

HEAD_DIM = 64
ROT = 16
F32 = jnp.float32
BF16 = jnp.bfloat16
EXTRA = 16


def rotary(values, turn):
    seq_rows = values.shape[-2]
    half = ROT // 2
    inverse = 10000.0 ** (-(2.0 * jnp.arange(half).astype(F32)) / ROT)
    angles = jnp.arange(seq_rows).astype(F32)[:, None] * inverse[None, :]
    cosine = jnp.cos(angles)
    sine = jnp.sin(angles) * turn
    first = values[..., :half]
    second = values[..., half:ROT]
    return jnp.concatenate(
        [first * cosine - second * sine, second * cosine + first * sine, values[..., ROT:]],
        axis=-1,
    )


def dot(left, right):
    return jnp.dot(left, right, preferred_element_type=F32)


def dot_nt(left, right):
    return lax.dot_general(left, right, (((1,), (1,)), ((), ())), preferred_element_type=F32)


def dot_tn(left, right):
    return lax.dot_general(left, right, (((0,), (0,)), ((), ())), preferred_element_type=F32)


def plan(mesh_shape, heads):
    shards, reps = mesh_shape["shard"], mesh_shape["rep"]
    split = 1
    while split < 4 and reps % (2 * split) == 0 and heads % (2 * split * shards) == 0:
        split *= 2
    return shards, reps, split


def make(mesh):
    def on_device(
        tokens,
        cotangent,
        lengths,
        qkv_weight,
        qkv_bias,
        dense_weight,
        dense_bias,
        in_weight,
        in_bias,
        out_weight,
        out_bias,
        norm1_gain,
        norm1_bias,
        norm2_gain,
        norm2_bias,
    ):
        seq_rows, width = tokens.shape
        heads = width // HEAD_DIM
        shards, reps, split = plan(dict(mesh.shape), heads)
        lines = reps // split
        group = shards * split
        owned = width // shards
        hidden = in_weight.shape[1]
        part_f = hidden // group
        part_h = width // group
        own_heads = part_h // HEAD_DIM
        shard = lax.axis_index("shard")
        rep = lax.axis_index("rep")
        slot = lax.rem(rep, split)
        line = rep // split
        block = shard * split + slot
        bits = []
        bit = split // 2
        while bit:
            bits.append(bit)
            bit //= 2

        def swap_rep(values, bit):
            return lax.ppermute(values, "rep", [(i, i ^ bit) for i in range(reps)])

        def swap_shard(values):
            return lax.ppermute(values, "shard", [(0, 1), (1, 0)])

        def gather_shard(values):
            if shards == 1:
                return values
            if shards == 2:
                return jnp.concatenate([values, swap_shard(values)], axis=0)
            return lax.all_gather(values, "shard", axis=0, tiled=True)

        def gather_rep(values):
            for bit in bits:
                values = jnp.concatenate([values, swap_rep(values, bit)], axis=0)
            return values

        def scatter_sum(values):
            for bit in reversed(bits):
                half = values.shape[0] // 2
                values = values[:half] + swap_rep(values[half:].astype(BF16), bit).astype(F32)
            if shards == 2:
                half = values.shape[0] // 2
                values = values[:half] + swap_shard(values[half:].astype(BF16)).astype(F32)
            elif shards > 2:
                values = lax.psum_scatter(
                    values.astype(BF16), "shard", scatter_dimension=0, tiled=True
                ).astype(F32)
            return values

        def ordered(mine, other, flag, axis):
            first = jnp.where(flag, other, mine)
            second = jnp.where(flag, mine, other)
            return jnp.concatenate([first, second], axis=axis)

        def columns_of(weight, parts, size):
            rows = weight.shape[0]
            cut = weight.reshape(rows, parts, group, size)

            def piece(at):
                return lax.dynamic_slice_in_dim(cut, at, 1, 2).reshape(rows, parts * size)

            if shards == 1:
                return piece(block)
            if shards == 2:
                other = swap_shard(piece((1 - shard) * split + slot))
                return ordered(piece(block), other, shard == 1, 0)
            picked = jnp.stack([piece(s * split + slot) for s in range(shards)], axis=0)
            return lax.all_to_all(picked, "shard", 0, 0, tiled=True).reshape(
                rows * shards, parts * size
            )

        def rows_exchange(grad):
            if shards == 1:
                return [grad]
            if shards == 2:
                mine = lax.dynamic_slice_in_dim(grad, shard * owned, owned, 0)
                other = swap_shard(lax.dynamic_slice_in_dim(grad, (1 - shard) * owned, owned, 0))
                return [jnp.where(shard == 1, other, mine), jnp.where(shard == 1, mine, other)]
            got = lax.all_to_all(grad, "shard", 0, 0, tiled=True)
            return [got[s * owned : (s + 1) * owned] for s in range(shards)]

        length = lengths[0]
        live = (jnp.arange(seq_rows) < length).astype(F32)[:, None]
        branch = (live * cotangent.astype(F32)).astype(BF16)
        halves = [dense_bias, out_bias, norm1_gain, norm1_bias, norm2_gain, norm2_bias]
        params = jnp.concatenate([qkv_bias] + halves)
        params = jnp.pad(params, (0, 8 * width - params.shape[0])).reshape(8, width)
        length_rows = jnp.broadcast_to(length.astype(BF16), (EXTRA - 8, width))
        packed = jnp.concatenate([tokens, params, length_rows], axis=0)
        packed = gather_shard(packed)
        branch_all = gather_shard(branch)
        in_w = columns_of(in_weight, 1, part_f)
        packed_all = gather_rep(packed).reshape(group, seq_rows + EXTRA, width)
        branch_all = gather_rep(branch_all)
        qkv_w = columns_of(qkv_weight, 3, part_h)

        by_shard = packed.reshape(shards, seq_rows + EXTRA, width)[:, seq_rows : seq_rows + 8]
        by_shard = by_shard.reshape(shards, 8 * width)
        if shards == 2:
            by_shard = jnp.where(shard == 1, by_shard[::-1], by_shard)

        def whole(at, size):
            return by_shard[:, at : at + size].reshape(shards * size).astype(F32)

        qkv_b = whole(0, 3 * owned)
        at = 3 * owned
        full = []
        for _ in halves:
            full.append(whole(at, owned))
            at += owned
        dense_b, out_b, gain_one, shift_one, gain_two, shift_two = full
        all_lengths = packed_all[:, seq_rows + 8, 0].astype(jnp.int32)
        rows = group * seq_rows
        values = packed_all[:, :seq_rows].reshape(rows, width).astype(F32)

        centre = values - jnp.mean(values, axis=-1, keepdims=True)
        spread = jnp.mean(centre * centre, axis=-1, keepdims=True)
        root = lax.rsqrt(spread + 1e-05)
        xhat = centre * root
        normed = (xhat * gain_one + shift_one).astype(BF16)
        normed_two = (xhat * gain_two + shift_two).astype(BF16)

        out_w = lax.dynamic_slice_in_dim(out_weight, slot * part_f, part_f, 0)
        in_b = lax.dynamic_slice_in_dim(in_bias, slot * part_f, part_f, 0).astype(F32)
        before = dot(normed_two, in_w) + in_b
        cdf = 0.5 * (1.0 + lax.erf(before * (0.5**0.5)))
        active = (before * cdf).astype(BF16)
        slope = cdf + before * jnp.exp(-0.5 * before * before) * 0.3989422804014327
        grad_before = (dot_nt(branch_all, out_w) * slope).astype(BF16)
        grad_out_w = dot_tn(active, branch_all).astype(BF16)
        grad_in_w = dot_tn(normed_two, grad_before).astype(BF16)
        grad_two = dot_nt(grad_before, in_w)

        scaling = HEAD_DIM ** (-0.5)
        bias = lax.dynamic_slice_in_dim(qkv_b.reshape(3, group, part_h), block, 1, 1)
        joint = dot(normed, qkv_w) + bias.reshape(3 * part_h)
        split_joint = joint.reshape(group, seq_rows, 3, own_heads, HEAD_DIM).transpose(2, 0, 3, 1, 4)
        query = rotary(split_joint[0], 1.0).astype(BF16)
        keys = rotary(split_joint[1], 1.0).astype(BF16)
        vals = split_joint[2].astype(BF16)
        position = jnp.arange(seq_rows)
        allowed = (position[None, :] <= position[:, None])[None] & (
            position[None, None, :] < all_lengths[:, None, None]
        )
        scores = jnp.einsum("bhpd,bhqd->bhpq", query, keys, preferred_element_type=F32) * scaling
        scores = jnp.where(allowed[:, None], scores, -1e30)
        raised = jnp.exp(scores - jnp.max(scores, axis=-1, keepdims=True))
        exact = raised / jnp.sum(raised, axis=-1, keepdims=True)
        probs = exact.astype(BF16)
        context = jnp.einsum("bhpq,bhqd->bhpd", probs, vals, preferred_element_type=F32)
        context = context.astype(BF16).transpose(0, 2, 1, 3).reshape(rows, part_h)
        dense_w = lax.dynamic_slice_in_dim(dense_weight, slot * part_h, part_h, 0)
        mixed = scatter_sum(dot(active, out_w) + dot(context, dense_w))
        result = (tokens.astype(F32) + live * (mixed + dense_b + out_b)).astype(BF16)

        grad_context = dot_nt(branch_all, dense_w).astype(BF16)
        grad_dense_w = dot_tn(context, branch_all).astype(BF16)
        grad_context = grad_context.reshape(group, seq_rows, own_heads, HEAD_DIM).transpose(0, 2, 1, 3)
        grad_probs = jnp.einsum(
            "bhpd,bhqd->bhpq", grad_context, vals, preferred_element_type=F32
        )
        grad_vals = jnp.einsum("bhpq,bhpd->bhqd", probs, grad_context, preferred_element_type=F32)
        grad_scores = (
            exact * (grad_probs - jnp.sum(grad_probs * exact, axis=-1, keepdims=True))
        ).astype(BF16)
        grad_query = jnp.einsum("bhpq,bhqd->bhpd", grad_scores, keys, preferred_element_type=F32)
        grad_keys = jnp.einsum("bhpq,bhpd->bhqd", grad_scores, query, preferred_element_type=F32)
        grad_joint = jnp.stack(
            [rotary(grad_query * scaling, -1.0), rotary(grad_keys * scaling, -1.0), grad_vals]
        ).astype(BF16)
        grad_joint = grad_joint.transpose(1, 3, 0, 2, 4).reshape(rows, 3 * part_h)
        grad_qkv_w = dot_tn(normed, grad_joint).astype(BF16)
        grad_one = dot_nt(grad_joint, qkv_w)

        inner = scatter_sum(grad_one * gain_one + grad_two * gain_two)
        own_xhat = xhat[:seq_rows] if shards <= 2 else None
        if own_xhat is None:
            own_xhat = lax.dynamic_slice_in_dim(xhat, shard * seq_rows, seq_rows, 0)
            own_root = lax.dynamic_slice_in_dim(root, shard * seq_rows, seq_rows, 0)
        else:
            own_root = root[:seq_rows]
        inner = (
            inner
            - jnp.mean(inner, axis=-1, keepdims=True)
            - own_xhat * jnp.mean(inner * own_xhat, axis=-1, keepdims=True)
        ) * own_root
        grad_tokens = (cotangent.astype(F32) + inner).astype(BF16)

        in_sum = jnp.sum(grad_before.astype(F32), axis=0)
        qkv_sum = jnp.sum(grad_joint.astype(F32), axis=0).reshape(3, 1, part_h)
        vectors = jnp.concatenate(
            [
                jnp.sum(grad_one * xhat, axis=0),
                jnp.sum(grad_one, axis=0),
                jnp.sum(grad_two * xhat, axis=0),
                jnp.sum(grad_two, axis=0),
                jnp.sum(branch.astype(F32), axis=0),
                lax.dynamic_update_slice_in_dim(jnp.zeros((hidden,), F32), in_sum, block * part_f, 0),
                lax.dynamic_update_slice_in_dim(
                    jnp.zeros((3, group, part_h), F32), qkv_sum, block, 1
                ).reshape(3 * width),
            ]
        )
        vectors = lax.psum(vectors, ("rep", "shard"))

        def own_part(at, size):
            piece = size // shards
            return lax.dynamic_slice_in_dim(vectors, at + shard * piece, piece, 0)

        in_parts = rows_exchange(grad_in_w)
        qkv_parts = rows_exchange(grad_qkv_w)
        chunks = [grad_out_w] + in_parts + [grad_dense_w] + qkv_parts
        if lines == 4:
            inner_line = (line == 1) | (line == 2)

            def line_permute(values, pairs):
                return lax.ppermute(
                    values,
                    "rep",
                    [(a * split + i, b * split + i) for a, b in pairs for i in range(split)],
                )

            summed = []
            for chunk in chunks:
                got = line_permute(chunk, [(0, 1), (3, 2)])
                near = lax.optimization_barrier((chunk.astype(F32) + got.astype(F32)).astype(BF16))
                got = line_permute(near, [(1, 2), (2, 1)])
                both = lax.optimization_barrier((near.astype(F32) + got.astype(F32)).astype(BF16))
                got = line_permute(both, [(1, 0), (2, 3)])
                summed.append(jnp.where(inner_line, both, got))
        else:
            groups = [[a * split + i for a in range(lines)] for i in range(split)]
            summed = [lax.psum(c, "rep", axis_index_groups=groups) for c in chunks]

        def gather_slots(values):
            values = values[None]
            for bit in reversed(bits):
                values = ordered(values, swap_rep(values, bit), (slot & bit) != 0, 0)
            return values

        summed = [gather_slots(c) for c in summed]
        total_out = summed[0].reshape(split * part_f, width).astype(F32)
        total_in = jnp.stack(summed[1 : 1 + shards])
        total_in = total_in.transpose(2, 0, 1, 3).reshape(owned, hidden).astype(F32)
        total_dense = summed[1 + shards].reshape(split * part_h, width).astype(F32)
        total_qkv = jnp.stack(summed[2 + shards :]).reshape(shards, split, owned, 3, part_h)
        total_qkv = total_qkv.transpose(2, 3, 0, 1, 4).reshape(owned, 3 * width).astype(F32)
        at_in = 5 * width
        at_qkv = at_in + hidden
        out_sum = own_part(4 * width, width)
        return (
            result,
            grad_tokens,
            total_qkv,
            own_part(at_qkv, 3 * width),
            total_dense,
            out_sum,
            total_in,
            own_part(at_in, hidden),
            total_out,
            out_sum,
            own_part(0, width),
            own_part(width, width),
            own_part(2 * width, width),
            own_part(3 * width, width),
        )

    return on_device


GROUP = 8
SPLIT = 4
LINES = 4
TAIL = 16
ANY = pl.BlockSpec(memory_space=pl.ANY)
SCALAR = pl.BlockSpec(memory_space=pltpu.SMEM)
WHOLE = pl.BlockSpec(memory_space=pltpu.VMEM)
LIMIT = 48 * 2**20
COST = pl.CostEstimate(flops=1024, bytes_accessed=1024, transcendentals=0)


def shaped(shape, dtype=BF16):
    return jax.ShapeDtypeStruct(shape, dtype)


def call(kernel, name, ins, outs, scratch=()):
    return pl.pallas_call(
        kernel,
        out_shape=[shape for shape, _ in outs],
        in_specs=[spec for _, spec in ins],
        out_specs=[spec for _, spec in outs],
        scratch_shapes=list(scratch),
        compiler_params=pltpu.CompilerParams(vmem_limit_bytes=LIMIT),
        cost_estimate=COST,
        name=name,
    )(*[array for array, _ in ins])


class Copies:
    def __init__(self, sems):
        self.sems, self.used = sems, 0

    def start(self, source, target):
        copy = pltpu.make_async_copy(source, target, self.sems.at[self.used])
        self.used += 1
        copy.start()
        return copy


def place_of():
    shard = lax.axis_index("shard")
    slot = lax.rem(lax.axis_index("rep"), SPLIT)
    return shard, slot, shard * SPLIT + slot


def span(at, size):
    return pl.ds(pl.multiple_of(at * size, size), size)


def pack_kernel(length, tok, cot, in_bias, qb, db, ob, g1, b1, g2, b2, in_weight, qkv_weight,
                packed, total, in_b, in_give, qkv_give, tok_v, cot_v, ib_v, qb_v, *rest):
    vecs, sems = rest[:-1], rest[-1]
    shard, slot, _ = place_of()
    twin = (1 - shard) * SPLIT + slot
    rows, width = tok_v.shape
    owned = vecs[0].shape[0]
    part_f, part_h = in_give.shape[1], qkv_give.shape[1] // 3
    copies = Copies(sems)
    first = [copies.start(tok, tok_v), copies.start(cot, cot_v), copies.start(in_bias, ib_v)]
    first.append(copies.start(qb, qb_v))
    first += [copies.start(a, b) for a, b in zip((db, ob, g1, b1, g2, b2), vecs)]
    given = [copies.start(in_weight.at[:, span(twin, part_f)], in_give)]
    for i in range(3):
        cols = pl.ds(pl.multiple_of(i * width + twin * part_h, part_h), part_h)
        target = qkv_give.at[:, i * part_h : (i + 1) * part_h]
        given.append(copies.start(qkv_weight.at[:, cols], target))
    for copy in first:
        copy.wait()
    live = lax.broadcasted_iota(jnp.int32, (rows, width), 0) < length[0]
    kept = jnp.where(live, cot_v[...].astype(F32), 0.0)
    packed[rows + TAIL :, :] = kept.astype(BF16)
    total[...] = jnp.sum(kept, axis=0, keepdims=True)
    packed[0:rows, :] = tok_v[...]
    whole = qb_v[...].astype(F32).reshape(1, 3 * owned)
    lines = [whole[:, i * owned : (i + 1) * owned] for i in range(3)]
    lines += [ref[...].astype(F32).reshape(1, owned) for ref in vecs]
    lines.append(jnp.full((TAIL - 9, owned), length[0].astype(F32)))
    packed[rows : rows + TAIL, 0:owned] = jnp.concatenate(lines, axis=0).astype(BF16)
    packed[rows : rows + TAIL, owned:width] = jnp.zeros((TAIL, width - owned), BF16)
    bias = ib_v[...].astype(F32).reshape(1, SPLIT * part_f)
    in_b[...] = sum(
        jnp.where(slot == i, bias[:, i * part_f : (i + 1) * part_f], 0.0) for i in range(SPLIT)
    )
    for copy in given:
        copy.wait()


def hidden_kernel(*refs):
    pieces, refs = refs[:GROUP], refs[GROUP:]
    (in_weight, in_got, out_weight, in_b, normed_o, xhat_o, active_o, grad_o, branch_o, out_a, out_b,
     own_o, other_o, params, lens, in_sum, every, branch, tails, w_full, out_w, normed, normed_two,
     xhat, active, slope, grad_before, grad_out, own, other, sems) = refs
    shard, slot, block = place_of()
    rows = pieces[0].shape[0] - TAIL >> 1
    owned, part = in_got.shape
    copies = Copies(sems)
    edge = [copies.start(p.at[rows : rows + TAIL, :], tails.at[i]) for i, p in enumerate(pieces)]
    first = [copies.start(p.at[0:rows, :], every.at[i * rows : (i + 1) * rows, :]) for i, p in enumerate(pieces)]
    first.append(copies.start(in_weight.at[:, span(block, part)], w_full.at[span(shard, owned), :]))
    first.append(copies.start(in_got, w_full.at[span(1 - shard, owned), :]))
    late = [copies.start(p.at[rows + TAIL :, :], branch.at[i * rows : (i + 1) * rows, :]) for i, p in enumerate(pieces)]
    late.append(copies.start(out_weight.at[span(slot, part), :], out_w))
    for copy in edge:
        copy.wait()
    params[:, span(shard, owned)] = tails[0, :, 0:owned].astype(F32)
    params[:, span(1 - shard, owned)] = tails[1, :, 0:owned].astype(F32)
    for i in range(GROUP):
        lens[i * 8 : (i + 1) * 8, :] = tails[i, :, 0:128].astype(F32)[8:]
    g1, b1, g2, b2 = (params[i : i + 1, :] for i in range(5, 9))
    for copy in first:
        copy.wait()
    step = 256

    def forward(i, carry):
        at = span(i, step)
        values = every[at, :].astype(F32)
        centre = values - jnp.mean(values, axis=-1, keepdims=True)
        spread = jnp.mean(centre * centre, axis=-1, keepdims=True)
        hat = centre * lax.rsqrt(spread + 1e-05)
        xhat[at, :] = hat.astype(BF16)
        normed[at, :] = (hat * g1 + b1).astype(BF16)
        two = (hat * g2 + b2).astype(BF16)
        normed_two[at, :] = two
        before = dot(two, w_full[...]) + in_b[...]
        cdf = 0.5 * (1.0 + lax.erf(before * (0.5**0.5)))
        active[at, :] = (before * cdf).astype(BF16)
        slope[at, :] = cdf + before * jnp.exp(-0.5 * before * before) * 0.3989422804014327
        return carry

    lax.fori_loop(0, GROUP * rows // step, forward, 0)
    done = [copies.start(normed, normed_o), copies.start(xhat, xhat_o), copies.start(active, active_o)]
    for copy in late:
        copy.wait()
    done.append(copies.start(branch, branch_o))

    def out_grad(j, carry):
        grad_out[span(j, step), :] = dot_tn(active[:, span(j, step)], branch[...]).astype(BF16)
        return carry

    lax.fori_loop(0, part // step, out_grad, 0)
    done.append(copies.start(grad_out.at[0 : part // 2, :], out_a))
    done.append(copies.start(grad_out.at[part // 2 :, :], out_b))
    in_sum[...] = jnp.zeros_like(in_sum)

    def back(i, carry):
        at = span(i, step)
        grad = (dot_nt(branch[at, :], out_w[...]) * slope[at, :]).astype(BF16)
        grad_before[at, :] = grad
        in_sum[...] += jnp.sum(grad.astype(F32), axis=0, keepdims=True)
        return carry

    lax.fori_loop(0, GROUP * rows // step, back, 0)
    done.append(copies.start(grad_before, grad_o))
    for ref, target, where in ((other, other_o, 1 - shard), (own, own_o, shard)):

        def weight(j, carry, ref=ref, where=where):
            cols = span(where * (owned // step) + j, step)
            ref[span(j, step), :] = dot_tn(normed_two[:, cols], grad_before[...]).astype(BF16)
            return carry

        lax.fori_loop(0, owned // step, weight, 0)
        done.append(copies.start(ref, target))
    for copy in done:
        copy.wait()


def turn(values, tables, back):
    cosine, low, high = tables
    width = values.shape[1]
    ahead = pltpu.roll(values, width - ROT // 2, 1)
    behind = pltpu.roll(values, ROT // 2, 1)
    moved = ahead * low + behind * high
    return values * cosine - moved if back else values * cosine + moved


def attention_kernel(last, *refs):
    (normed, branch, active, grad_before, xhat, lens, qkv_weight, qkv_got, dense_weight, out_weight,
     in_weight, in_got, params, cosine, low, high), refs = refs[:16], refs[16:]
    if last:
        (joint_held, dense_held, sums_held, jsum_held, in_sum, own_sum), refs = refs[:6], refs[6:]
        both, own, other, dense_o, vectors, acc, dense, sums, jsum, *refs = refs
    else:
        both, acc, dense, sums, jsum, *refs = refs
    w_full, dense_w, out_w, in_w, sems = refs
    shard, slot, block = place_of()
    rows, width = normed.shape
    part = dense_w.shape[0]
    owned, hidden = in_got.shape
    step = pl.program_id(0)

    @pl.when(step == 0)
    def _():
        copies = Copies(sems)
        mine, theirs = span(shard, owned), span(1 - shard, owned)
        started = [copies.start(qkv_got, w_full.at[theirs, :])]
        for i in range(3):
            cols = pl.ds(pl.multiple_of(i * width + block * part, part), part)
            target = w_full.at[mine, i * part : (i + 1) * part]
            started.append(copies.start(qkv_weight.at[:, cols], target))
        started.append(copies.start(dense_weight.at[span(slot, part), :], dense_w))
        started.append(copies.start(out_weight.at[span(slot, hidden), :], out_w))
        started.append(copies.start(in_weight.at[:, span(block, hidden)], in_w.at[mine, :]))
        started.append(copies.start(in_got, in_w.at[theirs, :]))
        if last:
            pairs = ((joint_held, acc), (dense_held, dense), (sums_held, sums), (jsum_held, jsum))
            started += [copies.start(a, b) for a, b in pairs]
        else:
            for ref in (acc, dense, sums, jsum):
                ref[...] = jnp.zeros_like(ref)
        for copy in started:
            copy.wait()

    scaling = HEAD_DIM**-0.5
    biases = []
    for i in range(3):
        at = i * width + block * part
        inside = lax.rem(at, 3 * owned)
        col = at // (3 * owned) * owned + lax.rem(inside, owned)
        cols = pl.ds(pl.multiple_of(col, part), part)
        biases.append(
            sum(jnp.where(inside // owned == r, params[r : r + 1, cols], 0.0) for r in range(3))
        )
    joint = dot(normed[...], w_full[...]) + jnp.concatenate(biases, axis=1)
    grad_context = dot_nt(branch[...], dense_w[...]).astype(BF16)
    seq = cosine.shape[0]
    tables = (cosine[...], low[...], high[...])
    at_p = lax.broadcasted_iota(jnp.int32, (seq, seq), 0)
    at_q = lax.broadcasted_iota(jnp.int32, (seq, seq), 1)
    contexts, grads = [], []
    for one in range(rows // seq):
        at = slice(one * seq, (one + 1) * seq)
        query = turn(joint[at, 0:part], tables, False).astype(BF16)
        keys = turn(joint[at, part : 2 * part], tables, False).astype(BF16)
        vals = joint[at, 2 * part :].astype(BF16)
        allowed = (at_q <= at_p) & (at_q.astype(F32) < lens[8 * one + 7 : 8 * one + 8, :])
        ctxs, queries, keyss, valss = [], [], [], []
        for head in range(part // HEAD_DIM):
            cols = slice(head * HEAD_DIM, (head + 1) * HEAD_DIM)
            q, k, v, gc = query[:, cols], keys[:, cols], vals[:, cols], grad_context[at, cols]
            scores = jnp.where(allowed, dot_nt(q, k) * scaling, -1e30)
            raised = jnp.exp(scores - jnp.max(scores, axis=-1, keepdims=True))
            exact = raised / jnp.sum(raised, axis=-1, keepdims=True)
            probs = exact.astype(BF16)
            ctxs.append(dot(probs, v))
            grad_probs = dot_nt(gc, v)
            valss.append(dot_tn(probs, gc))
            grad_scores = exact * (grad_probs - jnp.sum(grad_probs * exact, axis=-1, keepdims=True))
            grad_scores = grad_scores.astype(BF16)
            queries.append(dot(grad_scores, k) * scaling)
            keyss.append(dot_tn(grad_scores, q) * scaling)
        contexts.append(jnp.concatenate(ctxs, axis=1).astype(BF16))
        grad_query = turn(jnp.concatenate(queries, axis=1), tables, True)
        grad_keys = turn(jnp.concatenate(keyss, axis=1), tables, True)
        grads.append(jnp.concatenate([grad_query, grad_keys] + valss, axis=1).astype(BF16))
    ctx = jnp.concatenate(contexts, axis=0)
    grad = jnp.concatenate(grads, axis=0)
    jsum[...] += jnp.sum(grad.astype(F32), axis=0, keepdims=True)
    acc[...] += dot_tn(normed[...], grad)
    dense[...] += dot_tn(ctx, branch[...])
    both[:, 0:width] = (dot(active[...], out_w[...]) + dot(ctx, dense_w[...])).astype(BF16)
    hat = xhat[...].astype(F32)
    one = dot_nt(grad, w_full[...])
    sums[0:1, :] += jnp.sum(one * hat, axis=0, keepdims=True)
    sums[1:2, :] += jnp.sum(one, axis=0, keepdims=True)
    two = dot_nt(grad_before[...], in_w[...])
    sums[2:3, :] += jnp.sum(two * hat, axis=0, keepdims=True)
    sums[3:4, :] += jnp.sum(two, axis=0, keepdims=True)
    both[:, width:] = (one * params[5:6, :] + two * params[7:8, :]).astype(BF16)
    if not last:
        return

    @pl.when(step == pl.num_programs(0) - 1)
    def _():
        own[...] = acc[span(shard, owned), :].astype(BF16)
        other[...] = acc[span(1 - shard, owned), :].astype(BF16)
        dense_o[...] = dense[...].astype(BF16)
        vectors[...] = jnp.zeros_like(vectors)
        vectors[0:4, :] = sums[0:4, :]
        vectors[4:5, :] = own_sum[...]
        per_row = width // hidden
        vectors[pl.ds(5 + block // per_row, 1), span(lax.rem(block, per_row), hidden)] = in_sum[...]
        for i in range(3):
            row = 5 + GROUP // per_row + i
            vectors[row : row + 1, span(block, part)] = jsum[:, i * part : (i + 1) * part]


def attention(first, blocks, whole, tables, seq_rows, sizes, held=None):
    width, part, hidden = sizes
    rows, steps = 2 * seq_rows, 2
    owned = width // 2
    last = held is not None

    def block(array, height):
        return pl.BlockSpec((height, array.shape[1]), lambda i: (i + first, 0))

    def full(shape):
        return pl.BlockSpec(shape, lambda i: (0, 0))

    sums = [(width, 3 * part), (part, width), (8, width), (1, 3 * part)]
    out = [(shaped((steps * rows, 2 * width)), pl.BlockSpec((rows, 2 * width), lambda i: (i, 0)))]
    if last:
        shapes = [(owned, 3 * part), (owned, 3 * part), (part, width)]
        out += [(shaped(s), full(s)) for s in shapes]
        out.append((shaped((TAIL, width), F32), full((TAIL, width))))
    else:
        out += [(shaped(s, F32), full(s)) for s in sums]
    args = [*blocks, *whole, *tables] + list(held or ())
    specs = [block(a, h) for a, h in zip(blocks, [rows] * 5 + [16])]
    specs += [ANY] * 6 + [full(whole[6].shape)] + [full(t.shape) for t in tables]
    if last:
        specs += [ANY] * 4 + [full(a.shape) for a in held[4:]]
    scratch = [pltpu.VMEM(s, F32) for s in sums] if last else []
    scratch += [pltpu.VMEM(s, BF16) for s in ((width, 3 * part), (part, width), (hidden, width), (width, hidden))]
    return pl.pallas_call(
        lambda *refs: attention_kernel(last, *refs),
        grid=(steps,),
        out_shape=[shape for shape, _ in out],
        in_specs=specs,
        out_specs=[spec for _, spec in out],
        scratch_shapes=scratch + [pltpu.SemaphoreType.DMA((12,))],
        compiler_params=pltpu.CompilerParams(vmem_limit_bytes=LIMIT),
        cost_estimate=COST,
        name="attention",
    )(*args)


def placed(held, pieces, shape, size, where, parts=1):
    count = len(pieces)
    per = shape[1] // max(parts, 1)

    def kernel(*refs):
        ins, (out, raw, wide, sems) = refs[:count], refs[-4:]
        shard, slot, _ = place_of()
        copies = Copies(sems)
        loads = [copies.start(ref, raw.at[j]) for j, ref in enumerate(ins)]
        stores = []
        for j in range(count):
            loads[j].wait()
            wide[j] = raw[j].astype(F32)
            at = where(slot ^ (0, 2, 1, 3)[j], shard)
            if parts == 0:
                stores.append(copies.start(wide.at[j], out.at[span(at, size), :]))
            for i in range(parts):
                cols = pl.ds(pl.multiple_of(i * per + at * size, size), size)
                source = wide.at[j, :, i * size : (i + 1) * size]
                stores.append(copies.start(source, out.at[:, cols]))
        for copy in stores:
            copy.wait()

    args = list(pieces) + ([] if held is None else [held])
    return pl.pallas_call(
        kernel,
        in_specs=[ANY] * len(args),
        out_specs=ANY,
        out_shape=shaped(shape, F32),
        scratch_shapes=[
            pltpu.VMEM((count,) + pieces[0].shape, BF16),
            pltpu.VMEM((count,) + pieces[0].shape, F32),
            pltpu.SemaphoreType.DMA((count * (1 + max(parts, 1)),)),
        ],
        input_output_aliases={} if held is None else {count: 0},
        compiler_params=pltpu.CompilerParams(vmem_limit_bytes=LIMIT),
        cost_estimate=COST,
        name="place",
    )(*args)


def finish_kernel(length, tok, cot, own, got, params, result, grad_tokens):
    rows, width = tok.shape
    live = lax.broadcasted_iota(jnp.int32, (rows, width), 0) < length[0]
    values = tok[...].astype(F32)
    mixed = own[:, 0:width] + got[:, 0:width].astype(F32) + params[3:4, :] + params[4:5, :]
    result[...] = (values + jnp.where(live, mixed, 0.0)).astype(BF16)
    centre = values - jnp.mean(values, axis=-1, keepdims=True)
    root = lax.rsqrt(jnp.mean(centre * centre, axis=-1, keepdims=True) + 1e-05)
    hat = centre * root
    inner = own[:, width:] + got[:, width:].astype(F32)
    inner = inner - jnp.mean(inner, axis=-1, keepdims=True) - hat * jnp.mean(inner * hat, axis=-1, keepdims=True)
    grad_tokens[...] = (cot[...].astype(F32) + inner * root).astype(BF16)


def turn_tables(seq_rows, columns):
    half = ROT // 2
    inverse = np.float32(10000.0) ** (-(2.0 * np.arange(half, dtype=np.float32)) / np.float32(ROT))
    angles = np.arange(seq_rows, dtype=np.float32)[:, None] * inverse.astype(np.float32)[None, :]
    cosine = np.ones((seq_rows, HEAD_DIM), np.float32)
    low = np.zeros((seq_rows, HEAD_DIM), np.float32)
    high = np.zeros((seq_rows, HEAD_DIM), np.float32)
    cosine[:, :half] = cosine[:, half:ROT] = np.cos(angles)
    low[:, :half] = -np.sin(angles)
    high[:, half:ROT] = np.sin(angles)
    return [jnp.asarray(np.tile(t, (1, columns // HEAD_DIM))) for t in (cosine, low, high)]


def make_pairs(mesh):
    reps = mesh.shape["rep"]

    def swap_rep(values, bit):
        return lax.ppermute(values, "rep", [(i, i ^ bit) for i in range(reps)])

    def swap_shard(values):
        return lax.ppermute(values, "shard", [(0, 1), (1, 0)])

    def line_permute(values, pairs):
        pairs = [(a * SPLIT + i, b * SPLIT + i) for a, b in pairs for i in range(SPLIT)]
        return lax.ppermute(values, "rep", pairs)

    def added(left, right):
        return (left.astype(F32) + right.astype(F32)).astype(BF16)

    def after(value, other):
        return lax.optimization_barrier((value, other))[0]

    def on_device(
        tokens, cotangent, lengths, qkv_weight, qkv_bias, dense_weight, dense_bias, in_weight,
        in_bias, out_weight, out_bias, norm1_gain, norm1_bias, norm2_gain, norm2_bias,
    ):
        seq_rows, width = tokens.shape
        owned = width // 2
        hidden = in_weight.shape[1]
        part_f, part_h = hidden // GROUP, width // GROUP
        rows = GROUP * seq_rows
        line = lax.axis_index("rep") // SPLIT

        halves = [qkv_bias, dense_bias, out_bias, norm1_gain, norm1_bias, norm2_gain, norm2_bias]
        packed, branch_sum, in_b, in_give, qkv_give = call(
            pack_kernel,
            "pack",
            [(lengths, SCALAR)]
            + [(a, ANY) for a in [tokens, cotangent, in_bias, *halves, in_weight, qkv_weight]],
            [
                (shaped((2 * seq_rows + TAIL, width)), WHOLE),
                (shaped((1, width), F32), WHOLE),
                (shaped((1, part_f), F32), WHOLE),
                (shaped((owned, part_f)), ANY),
                (shaped((owned, 3 * part_h)), ANY),
            ],
            [pltpu.VMEM((seq_rows, width), BF16)] * 2
            + [pltpu.VMEM(v.shape, BF16) for v in [in_bias, *halves]]
            + [pltpu.SemaphoreType.DMA((14,))],
        )
        beside = swap_rep(packed, 2)
        across = swap_shard(packed)
        beyond = swap_rep(after(across, beside), 2)
        pieces = [packed, across, beside, beyond]
        pieces += [swap_rep(v, 1) for v in pieces]
        in_got = swap_shard(in_give)
        qkv_got = swap_shard(qkv_give)

        normed, xhat, active, grad_before, branch, out_a, out_b, in_mine, in_theirs, params, lens, in_sum = call(
            hidden_kernel,
            "hidden",
            [(p, ANY) for p in pieces]
            + [(in_weight, ANY), (in_got, ANY), (out_weight, ANY), (in_b, WHOLE)],
            [
                (shaped((rows, width)), ANY),
                (shaped((rows, width)), ANY),
                (shaped((rows, part_f)), ANY),
                (shaped((rows, part_f)), ANY),
                (shaped((rows, width)), ANY),
                (shaped((part_f // 2, width)), ANY),
                (shaped((part_f // 2, width)), ANY),
                (shaped((owned, part_f)), ANY),
                (shaped((owned, part_f)), ANY),
                (shaped((TAIL, width), F32), WHOLE),
                (shaped((GROUP * 8, 128), F32), WHOLE),
                (shaped((1, part_f), F32), WHOLE),
            ],
            [
                pltpu.VMEM((rows, width), BF16),
                pltpu.VMEM((rows, width), BF16),
                pltpu.VMEM((GROUP, TAIL, width), BF16),
                pltpu.VMEM((width, part_f), BF16),
                pltpu.VMEM((part_f, width), BF16),
                pltpu.VMEM((rows, width), BF16),
                pltpu.VMEM((rows, width), BF16),
                pltpu.VMEM((rows, width), BF16),
                pltpu.VMEM((rows, part_f), BF16),
                pltpu.VMEM((rows, part_f), F32),
                pltpu.VMEM((rows, part_f), BF16),
                pltpu.VMEM((part_f, width), BF16),
                pltpu.VMEM((owned, part_f), BF16),
                pltpu.VMEM((owned, part_f), BF16),
                pltpu.SemaphoreType.DMA((3 * GROUP + 3 + 9,)),
            ],
        )
        in_other = swap_shard(in_theirs)

        blocks = [normed, branch, active, grad_before, xhat, lens]
        whole = [qkv_weight, qkv_got, dense_weight, out_weight, in_weight, in_got, params]
        tables = turn_tables(seq_rows, part_h)
        sizes = (width, part_h, part_f)
        inner_line = (line == 1) | (line == 2)
        last = [params]

        def then(value):
            return after(value, last[0])

        def did(value):
            last[0] = value
            return value

        def meet(chunk):
            got = line_permute(chunk, [(0, 1), (3, 2)])
            return did(lax.optimization_barrier(added(then(chunk), got)))

        def cross(near):
            got = line_permute(near, [(1, 2), (2, 1)])
            return did(lax.optimization_barrier(added(then(near), got)))

        def spread(both):
            got = line_permute(both, [(1, 0), (2, 3)])
            return did(jnp.where(inner_line, then(both), got))

        def slots(chunk):
            two = [chunk, swap_rep(chunk, 2)]
            return two + [swap_rep(v, 1) for v in two]

        def place(held, pieces, *how):
            return did(placed(held, [then(pieces[0])] + pieces[1:], *how))

        far, *sums = attention(2, blocks, whole, tables, seq_rows, sizes)
        did(sums[3])
        far = swap_rep(far, 1)
        out_a = meet(out_a)
        near, qkv_mine, qkv_theirs, dense_mine, vectors = attention(
            0, [then(normed)] + blocks[1:], whole, tables, seq_rows, sizes, sums + [in_sum, branch_sum]
        )
        did(vectors)
        qkv_other = swap_shard(qkv_theirs)
        out_b = meet(out_b)
        out_a = cross(out_a)
        in_mine = meet(in_mine)
        half = 2 * seq_rows
        give = did(added(then(near[half:]), far[half:]))
        give = swap_rep(give, 2)
        vectors = did(then(vectors) + swap_rep(vectors, 1))
        out_b = cross(out_b)
        in_other = meet(in_other)
        out_a = spread(out_a)
        vectors = did(then(vectors) + swap_rep(vectors, 2))
        in_mine = cross(in_mine)
        qkv_mine = meet(qkv_mine)
        out_b = spread(out_b)
        out_a = slots(out_a)
        vectors = did(then(vectors) + swap_shard(vectors))
        dense_mine = did(jnp.concatenate([dense_mine, then(vectors).astype(BF16)], axis=0))
        in_other = cross(in_other)
        qkv_other = meet(qkv_other)
        in_mine = spread(in_mine)
        out_b = slots(out_b)
        half_f = (hidden // 2, width)
        total_out = place(None, out_a, half_f, part_f // 2, lambda slot, shard: 2 * slot, 0)
        qkv_mine = cross(qkv_mine)
        dense_mine = meet(dense_mine)
        in_other = spread(in_other)
        in_mine = slots(in_mine)
        keep = did(then(near[:half]).astype(F32) + far[:half].astype(F32) + give.astype(F32))
        give = swap_shard(keep[seq_rows:].astype(BF16))
        total_out = place(total_out, out_b, half_f, part_f // 2, lambda slot, shard: 2 * slot + 1, 0)
        qkv_other = cross(qkv_other)
        qkv_mine = spread(qkv_mine)
        in_other = slots(in_other)
        here = lambda slot, shard: shard * SPLIT + slot
        there = lambda slot, shard: (1 - shard) * SPLIT + slot
        dense_mine = cross(dense_mine)
        total_in = place(None, in_mine, (owned, hidden), part_f, here, 1)
        qkv_other = spread(qkv_other)
        qkv_mine = slots(qkv_mine)
        dense_mine = spread(dense_mine)
        qkv_other = slots(qkv_other)
        dense_four = slots(dense_mine[:part_h])
        total_in = place(total_in, in_other, (owned, hidden), part_f, there, 1)
        result, grad_tokens = call(
            finish_kernel,
            "finish",
            [(then(lengths), SCALAR)]
            + [(a, WHOLE) for a in (tokens, cotangent, keep[:seq_rows], give, params)],
            [(shaped((seq_rows, width)), WHOLE)] * 2,
        )
        did(result)
        total_qkv = place(None, qkv_mine, (owned, 3 * width), part_h, here, 3)
        vectors = did(then(dense_mine)[part_h:].astype(F32))
        total_qkv = place(total_qkv, qkv_other, (owned, 3 * width), part_h, there, 3)
        total_dense = place(None, dense_four, (owned, width), part_h, lambda slot, shard: slot, 0)
        shard = lax.axis_index("shard")

        def own_part(first, count):
            piece = vectors[first : first + count].reshape(-1)
            return lax.dynamic_slice_in_dim(piece, shard * (piece.shape[0] // 2), piece.shape[0] // 2, 0)

        hidden_rows = hidden // width
        out_sum = own_part(4, 1)
        return (
            result,
            grad_tokens,
            total_qkv,
            own_part(5 + hidden_rows, 3),
            total_dense,
            out_sum,
            total_in,
            own_part(5, hidden_rows),
            total_out,
            out_sum,
            own_part(0, 1),
            own_part(1, 1),
            own_part(2, 1),
            own_part(3, 1),
        )

    return on_device


def solution(mesh):
    rows = P(("rep", "shard"), None)
    vector = P("shard")
    matrix = P("shard", None)
    weights = (matrix, vector)
    in_specs = (rows, rows, P(("rep", "shard"))) + 4 * weights + 4 * (vector,)
    out_specs = (rows, rows) + 4 * weights + 4 * (vector,)
    paired = mesh.shape["shard"] == 2 and mesh.shape["rep"] == SPLIT * LINES
    body = make_pairs(mesh) if paired else make(mesh)
    return jax.shard_map(body, mesh=mesh, in_specs=in_specs, out_specs=out_specs, check_vma=False)
```

```python
import jax
import jax.numpy as jnp
import numpy as np
from jax import lax
from jax.experimental import pallas as pl
from jax.experimental.pallas import tpu as pltpu
from jax.sharding import PartitionSpec as P

HEAD_DIM = 64
ROT = 16
F32 = jnp.float32
BF16 = jnp.bfloat16
EXTRA = 16


def rotary(values, turn):
    seq_rows = values.shape[-2]
    half = ROT // 2
    inverse = 10000.0 ** (-(2.0 * jnp.arange(half).astype(F32)) / ROT)
    angles = jnp.arange(seq_rows).astype(F32)[:, None] * inverse[None, :]
    cosine = jnp.cos(angles)
    sine = jnp.sin(angles) * turn
    first = values[..., :half]
    second = values[..., half:ROT]
    return jnp.concatenate(
        [first * cosine - second * sine, second * cosine + first * sine, values[..., ROT:]],
        axis=-1,
    )


def dot(left, right):
    return jnp.dot(left, right, preferred_element_type=F32)


def dot_nt(left, right):
    return lax.dot_general(left, right, (((1,), (1,)), ((), ())), preferred_element_type=F32)


def dot_tn(left, right):
    return lax.dot_general(left, right, (((0,), (0,)), ((), ())), preferred_element_type=F32)


def plan(mesh_shape, heads):
    shards, reps = mesh_shape["shard"], mesh_shape["rep"]
    split = 1
    while split < 4 and reps % (2 * split) == 0 and heads % (2 * split * shards) == 0:
        split *= 2
    return shards, reps, split


def make(mesh):
    def on_device(
        tokens,
        cotangent,
        lengths,
        qkv_weight,
        qkv_bias,
        dense_weight,
        dense_bias,
        in_weight,
        in_bias,
        out_weight,
        out_bias,
        norm1_gain,
        norm1_bias,
        norm2_gain,
        norm2_bias,
    ):
        seq_rows, width = tokens.shape
        heads = width // HEAD_DIM
        shards, reps, split = plan(dict(mesh.shape), heads)
        lines = reps // split
        group = shards * split
        owned = width // shards
        hidden = in_weight.shape[1]
        part_f = hidden // group
        part_h = width // group
        own_heads = part_h // HEAD_DIM
        shard = lax.axis_index("shard")
        rep = lax.axis_index("rep")
        slot = lax.rem(rep, split)
        line = rep // split
        block = shard * split + slot
        bits = []
        bit = split // 2
        while bit:
            bits.append(bit)
            bit //= 2

        def swap_rep(values, bit):
            return lax.ppermute(values, "rep", [(i, i ^ bit) for i in range(reps)])

        def swap_shard(values):
            return lax.ppermute(values, "shard", [(0, 1), (1, 0)])

        def gather_shard(values):
            if shards == 1:
                return values
            if shards == 2:
                return jnp.concatenate([values, swap_shard(values)], axis=0)
            return lax.all_gather(values, "shard", axis=0, tiled=True)

        def gather_rep(values):
            for bit in bits:
                values = jnp.concatenate([values, swap_rep(values, bit)], axis=0)
            return values

        def scatter_sum(values):
            for bit in reversed(bits):
                half = values.shape[0] // 2
                values = values[:half] + swap_rep(values[half:].astype(BF16), bit).astype(F32)
            if shards == 2:
                half = values.shape[0] // 2
                values = values[:half] + swap_shard(values[half:].astype(BF16)).astype(F32)
            elif shards > 2:
                values = lax.psum_scatter(
                    values.astype(BF16), "shard", scatter_dimension=0, tiled=True
                ).astype(F32)
            return values

        def ordered(mine, other, flag, axis):
            first = jnp.where(flag, other, mine)
            second = jnp.where(flag, mine, other)
            return jnp.concatenate([first, second], axis=axis)

        def columns_of(weight, parts, size):
            rows = weight.shape[0]
            cut = weight.reshape(rows, parts, group, size)

            def piece(at):
                return lax.dynamic_slice_in_dim(cut, at, 1, 2).reshape(rows, parts * size)

            if shards == 1:
                return piece(block)
            if shards == 2:
                other = swap_shard(piece((1 - shard) * split + slot))
                return ordered(piece(block), other, shard == 1, 0)
            picked = jnp.stack([piece(s * split + slot) for s in range(shards)], axis=0)
            return lax.all_to_all(picked, "shard", 0, 0, tiled=True).reshape(
                rows * shards, parts * size
            )

        def rows_exchange(grad):
            if shards == 1:
                return [grad]
            if shards == 2:
                mine = lax.dynamic_slice_in_dim(grad, shard * owned, owned, 0)
                other = swap_shard(lax.dynamic_slice_in_dim(grad, (1 - shard) * owned, owned, 0))
                return [jnp.where(shard == 1, other, mine), jnp.where(shard == 1, mine, other)]
            got = lax.all_to_all(grad, "shard", 0, 0, tiled=True)
            return [got[s * owned : (s + 1) * owned] for s in range(shards)]

        length = lengths[0]
        live = (jnp.arange(seq_rows) < length).astype(F32)[:, None]
        branch = (live * cotangent.astype(F32)).astype(BF16)
        halves = [dense_bias, out_bias, norm1_gain, norm1_bias, norm2_gain, norm2_bias]
        params = jnp.concatenate([qkv_bias] + halves)
        params = jnp.pad(params, (0, 8 * width - params.shape[0])).reshape(8, width)
        length_rows = jnp.broadcast_to(length.astype(BF16), (EXTRA - 8, width))
        packed = jnp.concatenate([tokens, params, length_rows], axis=0)
        packed = gather_shard(packed)
        branch_all = gather_shard(branch)
        in_w = columns_of(in_weight, 1, part_f)
        packed_all = gather_rep(packed).reshape(group, seq_rows + EXTRA, width)
        branch_all = gather_rep(branch_all)
        qkv_w = columns_of(qkv_weight, 3, part_h)

        by_shard = packed.reshape(shards, seq_rows + EXTRA, width)[:, seq_rows : seq_rows + 8]
        by_shard = by_shard.reshape(shards, 8 * width)
        if shards == 2:
            by_shard = jnp.where(shard == 1, by_shard[::-1], by_shard)

        def whole(at, size):
            return by_shard[:, at : at + size].reshape(shards * size).astype(F32)

        qkv_b = whole(0, 3 * owned)
        at = 3 * owned
        full = []
        for _ in halves:
            full.append(whole(at, owned))
            at += owned
        dense_b, out_b, gain_one, shift_one, gain_two, shift_two = full
        all_lengths = packed_all[:, seq_rows + 8, 0].astype(jnp.int32)
        rows = group * seq_rows
        values = packed_all[:, :seq_rows].reshape(rows, width).astype(F32)

        centre = values - jnp.mean(values, axis=-1, keepdims=True)
        spread = jnp.mean(centre * centre, axis=-1, keepdims=True)
        root = lax.rsqrt(spread + 1e-05)
        xhat = centre * root
        normed = (xhat * gain_one + shift_one).astype(BF16)
        normed_two = (xhat * gain_two + shift_two).astype(BF16)

        out_w = lax.dynamic_slice_in_dim(out_weight, slot * part_f, part_f, 0)
        in_b = lax.dynamic_slice_in_dim(in_bias, slot * part_f, part_f, 0).astype(F32)
        before = dot(normed_two, in_w) + in_b
        cdf = 0.5 * (1.0 + lax.erf(before * (0.5**0.5)))
        active = (before * cdf).astype(BF16)
        slope = cdf + before * jnp.exp(-0.5 * before * before) * 0.3989422804014327
        grad_before = (dot_nt(branch_all, out_w) * slope).astype(BF16)
        grad_out_w = dot_tn(active, branch_all).astype(BF16)
        grad_in_w = dot_tn(normed_two, grad_before).astype(BF16)
        grad_two = dot_nt(grad_before, in_w)

        scaling = HEAD_DIM ** (-0.5)
        bias = lax.dynamic_slice_in_dim(qkv_b.reshape(3, group, part_h), block, 1, 1)
        joint = dot(normed, qkv_w) + bias.reshape(3 * part_h)
        split_joint = joint.reshape(group, seq_rows, 3, own_heads, HEAD_DIM).transpose(2, 0, 3, 1, 4)
        query = rotary(split_joint[0], 1.0).astype(BF16)
        keys = rotary(split_joint[1], 1.0).astype(BF16)
        vals = split_joint[2].astype(BF16)
        position = jnp.arange(seq_rows)
        allowed = (position[None, :] <= position[:, None])[None] & (
            position[None, None, :] < all_lengths[:, None, None]
        )
        scores = jnp.einsum("bhpd,bhqd->bhpq", query, keys, preferred_element_type=F32) * scaling
        scores = jnp.where(allowed[:, None], scores, -1e30)
        raised = jnp.exp(scores - jnp.max(scores, axis=-1, keepdims=True))
        exact = raised / jnp.sum(raised, axis=-1, keepdims=True)
        probs = exact.astype(BF16)
        context = jnp.einsum("bhpq,bhqd->bhpd", probs, vals, preferred_element_type=F32)
        context = context.astype(BF16).transpose(0, 2, 1, 3).reshape(rows, part_h)
        dense_w = lax.dynamic_slice_in_dim(dense_weight, slot * part_h, part_h, 0)
        mixed = scatter_sum(dot(active, out_w) + dot(context, dense_w))
        result = (tokens.astype(F32) + live * (mixed + dense_b + out_b)).astype(BF16)

        grad_context = dot_nt(branch_all, dense_w).astype(BF16)
        grad_dense_w = dot_tn(context, branch_all).astype(BF16)
        grad_context = grad_context.reshape(group, seq_rows, own_heads, HEAD_DIM).transpose(0, 2, 1, 3)
        grad_probs = jnp.einsum(
            "bhpd,bhqd->bhpq", grad_context, vals, preferred_element_type=F32
        )
        grad_vals = jnp.einsum("bhpq,bhpd->bhqd", probs, grad_context, preferred_element_type=F32)
        grad_scores = (
            exact * (grad_probs - jnp.sum(grad_probs * exact, axis=-1, keepdims=True))
        ).astype(BF16)
        grad_query = jnp.einsum("bhpq,bhqd->bhpd", grad_scores, keys, preferred_element_type=F32)
        grad_keys = jnp.einsum("bhpq,bhpd->bhqd", grad_scores, query, preferred_element_type=F32)
        grad_joint = jnp.stack(
            [rotary(grad_query * scaling, -1.0), rotary(grad_keys * scaling, -1.0), grad_vals]
        ).astype(BF16)
        grad_joint = grad_joint.transpose(1, 3, 0, 2, 4).reshape(rows, 3 * part_h)
        grad_qkv_w = dot_tn(normed, grad_joint).astype(BF16)
        grad_one = dot_nt(grad_joint, qkv_w)

        inner = scatter_sum(grad_one * gain_one + grad_two * gain_two)
        own_xhat = xhat[:seq_rows] if shards <= 2 else None
        if own_xhat is None:
            own_xhat = lax.dynamic_slice_in_dim(xhat, shard * seq_rows, seq_rows, 0)
            own_root = lax.dynamic_slice_in_dim(root, shard * seq_rows, seq_rows, 0)
        else:
            own_root = root[:seq_rows]
        inner = (
            inner
            - jnp.mean(inner, axis=-1, keepdims=True)
            - own_xhat * jnp.mean(inner * own_xhat, axis=-1, keepdims=True)
        ) * own_root
        grad_tokens = (cotangent.astype(F32) + inner).astype(BF16)

        in_sum = jnp.sum(grad_before.astype(F32), axis=0)
        qkv_sum = jnp.sum(grad_joint.astype(F32), axis=0).reshape(3, 1, part_h)
        vectors = jnp.concatenate(
            [
                jnp.sum(grad_one * xhat, axis=0),
                jnp.sum(grad_one, axis=0),
                jnp.sum(grad_two * xhat, axis=0),
                jnp.sum(grad_two, axis=0),
                jnp.sum(branch.astype(F32), axis=0),
                lax.dynamic_update_slice_in_dim(jnp.zeros((hidden,), F32), in_sum, block * part_f, 0),
                lax.dynamic_update_slice_in_dim(
                    jnp.zeros((3, group, part_h), F32), qkv_sum, block, 1
                ).reshape(3 * width),
            ]
        )
        vectors = lax.psum(vectors, ("rep", "shard"))

        def own_part(at, size):
            piece = size // shards
            return lax.dynamic_slice_in_dim(vectors, at + shard * piece, piece, 0)

        in_parts = rows_exchange(grad_in_w)
        qkv_parts = rows_exchange(grad_qkv_w)
        chunks = [grad_out_w] + in_parts + [grad_dense_w] + qkv_parts
        if lines == 4:
            inner_line = (line == 1) | (line == 2)

            def line_permute(values, pairs):
                return lax.ppermute(
                    values,
                    "rep",
                    [(a * split + i, b * split + i) for a, b in pairs for i in range(split)],
                )

            summed = []
            for chunk in chunks:
                got = line_permute(chunk, [(0, 1), (3, 2)])
                near = lax.optimization_barrier((chunk.astype(F32) + got.astype(F32)).astype(BF16))
                got = line_permute(near, [(1, 2), (2, 1)])
                both = lax.optimization_barrier((near.astype(F32) + got.astype(F32)).astype(BF16))
                got = line_permute(both, [(1, 0), (2, 3)])
                summed.append(jnp.where(inner_line, both, got))
        else:
            groups = [[a * split + i for a in range(lines)] for i in range(split)]
            summed = [lax.psum(c, "rep", axis_index_groups=groups) for c in chunks]

        def gather_slots(values):
            values = values[None]
            for bit in reversed(bits):
                values = ordered(values, swap_rep(values, bit), (slot & bit) != 0, 0)
            return values

        summed = [gather_slots(c) for c in summed]
        total_out = summed[0].reshape(split * part_f, width).astype(F32)
        total_in = jnp.stack(summed[1 : 1 + shards])
        total_in = total_in.transpose(2, 0, 1, 3).reshape(owned, hidden).astype(F32)
        total_dense = summed[1 + shards].reshape(split * part_h, width).astype(F32)
        total_qkv = jnp.stack(summed[2 + shards :]).reshape(shards, split, owned, 3, part_h)
        total_qkv = total_qkv.transpose(2, 3, 0, 1, 4).reshape(owned, 3 * width).astype(F32)
        at_in = 5 * width
        at_qkv = at_in + hidden
        out_sum = own_part(4 * width, width)
        return (
            result,
            grad_tokens,
            total_qkv,
            own_part(at_qkv, 3 * width),
            total_dense,
            out_sum,
            total_in,
            own_part(at_in, hidden),
            total_out,
            out_sum,
            own_part(0, width),
            own_part(width, width),
            own_part(2 * width, width),
            own_part(3 * width, width),
        )

    return on_device


GROUP = 8
SPLIT = 4
LINES = 4
TAIL = 16
VECTORS = 32
ANY = pl.BlockSpec(memory_space=pltpu.HBM)
SCALAR = pl.BlockSpec(memory_space=pltpu.SMEM)
WHOLE = pl.BlockSpec(memory_space=pltpu.VMEM)
LIMIT = 63 * 2**20
COST = pl.CostEstimate(flops=10**12, bytes_accessed=10**9, transcendentals=0)
SMALL = pl.CostEstimate(flops=10**6, bytes_accessed=0, transcendentals=0)


def shaped(shape, dtype=BF16):
    return jax.ShapeDtypeStruct(shape, dtype)


def call(kernel, name, ins, outs, scratch=()):
    return pl.pallas_call(
        kernel,
        out_shape=[shape for shape, _ in outs],
        in_specs=[spec for _, spec in ins],
        out_specs=[spec for _, spec in outs],
        scratch_shapes=list(scratch),
        compiler_params=pltpu.CompilerParams(vmem_limit_bytes=LIMIT),
        cost_estimate=COST if name == "hidden" else SMALL,
        name=name,
    )(*[array for array, _ in ins])


class Copies:
    def __init__(self, sems):
        self.sems, self.used = sems, 0

    def make(self, source, target):
        self.used += 1
        return pltpu.make_async_copy(source, target, self.sems.at[self.used - 1])

    def start(self, source, target):
        copy = self.make(source, target)
        copy.start()
        return copy


def place_of():
    shard = lax.axis_index("shard")
    slot = lax.rem(lax.axis_index("rep"), SPLIT)
    return shard, slot, shard * SPLIT + slot


def span(at, size):
    if isinstance(at, int):
        return pl.ds(at * size, size)
    return pl.ds(pl.multiple_of(at * size, size), size)


def pack_kernel(length, tok, cot, in_bias, qb, db, ob, g1, b1, g2, b2, in_weight, qkv_weight,
                packed, total, in_b, in_give, qkv_give, tok_v, cot_v, ib_v, qb_v, *rest):
    vecs, sems = rest[:-1], rest[-1]
    shard, slot, _ = place_of()
    twin = (1 - shard) * SPLIT + slot
    rows, width = tok_v.shape
    owned = vecs[0].shape[0]
    part_f, part_h = in_give.shape[1], qkv_give.shape[1] // 3
    copies = Copies(sems)
    first = [copies.start(tok, tok_v), copies.start(cot, cot_v), copies.start(in_bias, ib_v)]
    first.append(copies.start(qb, qb_v))
    first += [copies.start(a, b) for a, b in zip((db, ob, g1, b1, g2, b2), vecs)]
    given = [copies.start(in_weight.at[:, span(twin, part_f)], in_give)]
    for i in range(3):
        cols = pl.ds(pl.multiple_of(i * width + twin * part_h, part_h), part_h)
        target = qkv_give.at[:, i * part_h : (i + 1) * part_h]
        given.append(copies.start(qkv_weight.at[:, cols], target))
    for copy in first:
        copy.wait()
    live = lax.broadcasted_iota(jnp.int32, (rows, width), 0) < length[0]
    kept = jnp.where(live, cot_v[...].astype(F32), 0.0)
    packed[rows + TAIL :, :] = kept.astype(BF16)
    total[...] = jnp.sum(kept, axis=0, keepdims=True)
    packed[0:rows, :] = tok_v[...]
    whole = qb_v[...].astype(F32).reshape(1, 3 * owned)
    lines = [whole[:, i * owned : (i + 1) * owned] for i in range(3)]
    lines += [ref[...].astype(F32).reshape(1, owned) for ref in vecs]
    lines.append(jnp.full((TAIL - 9, owned), length[0].astype(F32)))
    packed[rows : rows + TAIL, 0:owned] = jnp.concatenate(lines, axis=0).astype(BF16)
    packed[rows : rows + TAIL, owned:width] = jnp.zeros((TAIL, width - owned), BF16)
    bias = ib_v[...].astype(F32).reshape(1, SPLIT * part_f)
    in_b[...] = sum(
        jnp.where(slot == i, bias[:, i * part_f : (i + 1) * part_f], 0.0) for i in range(SPLIT)
    )
    for copy in given:
        copy.wait()


def hidden_kernel(*refs):
    pieces, refs = refs[:GROUP], refs[GROUP:]
    (in_weight, in_got, out_weight, in_b, normed_o, xhat_o, active_o, grad_o, branch_o, out_o,
     own_o, other_o, params, lens, in_sum, every, branch, tails, w_full, out_w, normed, normed_two,
     xhat, active, slope, grad_before, grad_out, own, other, sems) = refs
    shard, slot, block = place_of()
    rows = pieces[0].shape[0] - TAIL >> 1
    owned, part = in_got.shape
    copies = Copies(sems)
    edge = [copies.start(p.at[rows : rows + TAIL, :], tails.at[i]) for i, p in enumerate(pieces)]
    first = [copies.start(p.at[0:rows, :], every.at[i * rows : (i + 1) * rows, :]) for i, p in enumerate(pieces)]
    first.append(copies.start(in_weight.at[:, span(block, part)], w_full.at[span(shard, owned), :]))
    first.append(copies.start(in_got, w_full.at[span(1 - shard, owned), :]))
    late = [copies.start(p.at[rows + TAIL :, :], branch.at[i * rows : (i + 1) * rows, :]) for i, p in enumerate(pieces)]
    late.append(copies.start(out_weight.at[span(slot, part), :], out_w))
    for copy in edge:
        copy.wait()
    params[:, span(shard, owned)] = tails[0, :, 0:owned].astype(F32)
    params[:, span(1 - shard, owned)] = tails[1, :, 0:owned].astype(F32)
    for i in range(GROUP):
        lens[i * 8 : (i + 1) * 8, :] = tails[i, :, 0:128].astype(F32)[8:]
    g1, b1, g2, b2 = (params[i : i + 1, :] for i in range(5, 9))
    for copy in first:
        copy.wait()
    step = 256

    def forward(i, carry):
        at = span(i, step)
        values = every[at, :].astype(F32)
        centre = values - jnp.mean(values, axis=-1, keepdims=True)
        spread = jnp.mean(centre * centre, axis=-1, keepdims=True)
        hat = centre * lax.rsqrt(spread + 1e-05)
        xhat[at, :] = hat.astype(BF16)
        normed[at, :] = (hat * g1 + b1).astype(BF16)
        two = (hat * g2 + b2).astype(BF16)
        normed_two[at, :] = two
        before = dot(two, w_full[...]) + in_b[...]
        cdf = 0.5 * (1.0 + lax.erf(before * (0.5**0.5)))
        active[at, :] = (before * cdf).astype(BF16)
        slope[at, :] = cdf + before * jnp.exp(-0.5 * before * before) * 0.3989422804014327
        return carry

    for i in range(GROUP * rows // step):
        forward(i, 0)
    done = [copies.start(normed, normed_o), copies.start(xhat, xhat_o), copies.start(active, active_o)]
    for copy in late:
        copy.wait()
    done.append(copies.start(branch, branch_o))

    def out_grad(j, carry):
        grad_out[span(j, step), :] = dot_tn(active[:, span(j, step)], branch[...]).astype(BF16)
        return carry

    lax.fori_loop(0, part // step, out_grad, 0)
    done.append(copies.start(grad_out, out_o))
    in_sum[...] = jnp.zeros_like(in_sum)

    def back(i, carry):
        at = span(i, step)
        grad = (dot_nt(branch[at, :], out_w[...]) * slope[at, :]).astype(BF16)
        grad_before[at, :] = grad
        in_sum[...] += jnp.sum(grad.astype(F32), axis=0, keepdims=True)
        return carry

    for i in range(GROUP * rows // step):
        back(i, 0)
    done.append(copies.start(grad_before, grad_o))
    for ref, target, where in ((other, other_o, 1 - shard), (own, own_o, shard)):

        def weight(j, carry, ref=ref, where=where):
            cols = span(where * (owned // step) + j, step)
            ref[span(j, step), :] = dot_tn(normed_two[:, cols], grad_before[...]).astype(BF16)
            return carry

        lax.fori_loop(0, owned // step, weight, 0)
        done.append(copies.start(ref, target))
    for copy in done:
        copy.wait()


def turn(values, tables, back):
    cosine, low, high = tables
    width = values.shape[1]
    ahead = pltpu.roll(values, width - ROT // 2, 1)
    behind = pltpu.roll(values, ROT // 2, 1)
    moved = ahead * low + behind * high
    return values * cosine - moved if back else values * cosine + moved


def attention_kernel(
    normed, branch, active, grad_before, xhat, lens, qkv_weight, qkv_got, dense_weight, out_weight,
    in_weight, in_got, params, cosine, low, high, in_sum, own_sum, far, near, mine_o, theirs_o,
    acc, dense, sums, jsum, vectors, w_full, dense_w, out_w, in_w, sems,
):
    shard, slot, block = place_of()
    rows, width = normed.shape
    part = dense_w.shape[0]
    owned, hidden = in_got.shape
    step = pl.program_id(0)

    copies = Copies(sems)
    mine, theirs = span(shard, owned), span(1 - shard, owned)
    early = [copies.make(qkv_got, w_full.at[theirs, :])]
    for i in range(3):
        cols = pl.ds(pl.multiple_of(i * width + block * part, part), part)
        target = w_full.at[mine, i * part : (i + 1) * part]
        early.append(copies.make(qkv_weight.at[:, cols], target))
    early.append(copies.make(dense_weight.at[span(slot, part), :], dense_w))
    late = [copies.make(out_weight.at[span(slot, hidden), :], out_w)]
    late.append(copies.make(in_weight.at[:, span(block, hidden)], in_w.at[mine, :]))
    late.append(copies.make(in_got, in_w.at[theirs, :]))

    @pl.when(step == 0)
    def _():
        for copy in early + late:
            copy.start()
        for ref in (acc, dense, sums, jsum):
            ref[...] = jnp.zeros_like(ref)
        for copy in early:
            copy.wait()

    scaling = HEAD_DIM**-0.5
    biases = []
    for i in range(3):
        at = i * width + block * part
        inside = lax.rem(at, 3 * owned)
        col = at // (3 * owned) * owned + lax.rem(inside, owned)
        cols = pl.ds(pl.multiple_of(col, part), part)
        biases.append(
            sum(jnp.where(inside // owned == r, params[r : r + 1, cols], 0.0) for r in range(3))
        )
    joint = dot(normed[...], w_full[...]) + jnp.concatenate(biases, axis=1)
    grad_context = dot_nt(branch[...], dense_w[...]).astype(BF16)
    seq = cosine.shape[0]
    tables = (cosine[...], low[...], high[...])
    at_p = lax.broadcasted_iota(jnp.int32, (seq, seq), 0)
    at_q = lax.broadcasted_iota(jnp.int32, (seq, seq), 1)
    head_of = lax.broadcasted_iota(jnp.int32, (seq, part), 1) // HEAD_DIM

    def apart(values):
        zero = jnp.zeros_like(values)
        return jnp.concatenate(
            [jnp.where(head_of == h, values, zero) for h in range(part // HEAD_DIM)], axis=0
        )

    def together(values):
        total = values[0:seq]
        for h in range(1, part // HEAD_DIM):
            total = jnp.where(head_of == h, values[h * seq : (h + 1) * seq], total)
        return total

    contexts, grads = [], []
    for one in range(rows // seq):
        at = slice(one * seq, (one + 1) * seq)
        query = turn(joint[at, 0:part], tables, False).astype(BF16)
        keys = turn(joint[at, part : 2 * part], tables, False).astype(BF16)
        vals = joint[at, 2 * part :].astype(BF16)
        allowed = (at_q <= at_p) & (at_q.astype(F32) < lens[8 * one + 7 : 8 * one + 8, :])
        gc = grad_context[at, :]
        keys_apart, vals_apart = apart(keys), apart(vals)
        scores = dot_nt(query, keys_apart) * scaling
        heads = range(part // HEAD_DIM)
        exact = []
        for head in heads:
            masked = jnp.where(allowed, scores[:, head * seq : (head + 1) * seq], -1e30)
            raised = jnp.exp(masked - jnp.max(masked, axis=-1, keepdims=True))
            exact.append(raised / jnp.sum(raised, axis=-1, keepdims=True))
        probs = jnp.concatenate(exact, axis=1).astype(BF16)
        contexts.append(dot(probs, vals_apart).astype(BF16))
        grad_probs = dot_nt(gc, vals_apart)
        grad_vals = together(dot_tn(probs, gc))
        grad_scores = []
        for head in heads:
            grad = grad_probs[:, head * seq : (head + 1) * seq]
            mean = jnp.sum(grad * exact[head], axis=-1, keepdims=True)
            grad_scores.append((exact[head] * (grad - mean)).astype(BF16))
        grad_scores = jnp.concatenate(grad_scores, axis=1)
        grad_query = turn(dot(grad_scores, keys_apart) * scaling, tables, True)
        grad_keys = turn(together(dot_tn(grad_scores, query)) * scaling, tables, True)
        grads.append(jnp.concatenate([grad_query, grad_keys, grad_vals], axis=1).astype(BF16))
    ctx = jnp.concatenate(contexts, axis=0)
    grad = jnp.concatenate(grads, axis=0)
    jsum[...] += jnp.sum(grad.astype(F32), axis=0, keepdims=True)
    acc[...] += dot_tn(normed[...], grad)
    dense[...] += dot_tn(ctx, branch[...])

    @pl.when(step == 0)
    def _():
        for copy in late:
            copy.wait()

    mixed = (dot(active[...], out_w[...]) + dot(ctx, dense_w[...])).astype(BF16)
    hat = xhat[...].astype(F32)
    one = dot_nt(grad, w_full[...])
    sums[0:1, :] += jnp.sum(one * hat, axis=0, keepdims=True)
    sums[1:2, :] += jnp.sum(one, axis=0, keepdims=True)
    two = dot_nt(grad_before[...], in_w[...])
    sums[2:3, :] += jnp.sum(two * hat, axis=0, keepdims=True)
    sums[3:4, :] += jnp.sum(two, axis=0, keepdims=True)
    inner = (one * params[5:6, :] + two * params[7:8, :]).astype(BF16)
    for ref, here in ((far, step < 2), (near, step >= 2)):

        @pl.when(here)
        def _(ref=ref):
            ref[:, 0:width] = mixed
            ref[:, width:] = inner

    @pl.when(step == pl.num_programs(0) - 1)
    def _():
        wide = 3 * part
        vectors[...] = jnp.zeros_like(vectors)
        row = 0
        for source in [sums[i : i + 1, :] for i in range(4)] + [own_sum[...], in_sum[...], jsum[...]]:
            for at in range(0, source.shape[1], wide):
                piece = source[:, at : at + wide]
                vectors[row : row + 1, 0 : piece.shape[1]] = piece
                row += 1
        for ref, which in ((mine_o, shard), (theirs_o, 1 - shard)):
            ref[0:owned, 0:wide] = acc[span(which, owned), :].astype(BF16)
            ref[owned:, 0:wide] = vectors[...].astype(BF16)
        each = width * part // owned
        for i in range(owned // part):
            cols = slice(i * each, (i + 1) * each)
            mine_o[i * part : (i + 1) * part, wide:] = dense[:, cols].astype(BF16)
        mine_o[owned:, wide:] = jnp.zeros((VECTORS, each), BF16)


def attention(blocks, whole, tables, small, seq_rows, sizes):
    width, part, hidden = sizes
    rows, steps = 2 * seq_rows, 4
    owned, wide = width // 2, 3 * part

    def block(array, height):
        return pl.BlockSpec((height, array.shape[1]), lambda i: ((i + 2) % 4, 0))

    def full(shape):
        return pl.BlockSpec(shape, lambda i: (0, 0))

    outer = pl.BlockSpec((rows, 2 * width), lambda i: (jnp.minimum(i, 1), 0))
    inner = pl.BlockSpec((rows, 2 * width), lambda i: (jnp.maximum(i - 2, 0), 0))
    mine = (owned + VECTORS, wide + width * part // owned)
    theirs = (owned + VECTORS, wide)
    half = shaped((2 * rows, 2 * width))
    args = [*blocks, *whole, *tables, *small]
    specs = [block(a, h) for a, h in zip(blocks, [rows] * 5 + [16])]
    specs += [ANY] * 6 + [full(a.shape) for a in [whole[6], *tables, *small]]
    sums = [(width, wide), (part, width), (8, width), (1, wide), (VECTORS, wide)]
    weights = [(width, wide), (part, width), (hidden, width), (width, hidden)]
    return pl.pallas_call(
        attention_kernel,
        grid=(steps,),
        out_shape=[half, half, shaped(mine), shaped(theirs)],
        in_specs=specs,
        out_specs=[outer, inner, full(mine), full(theirs)],
        scratch_shapes=[pltpu.VMEM(s, F32) for s in sums]
        + [pltpu.VMEM(s, BF16) for s in weights]
        + [pltpu.SemaphoreType.DMA((8,))],
        compiler_params=pltpu.CompilerParams(vmem_limit_bytes=LIMIT),
        cost_estimate=COST,
        name="attention",
    )(*args)


def placed(held, pieces, shape, size, where, parts=1):
    count = len(pieces)
    per = shape[1] // max(parts, 1)
    height = pieces[0].shape[0] if parts else size
    held_shape = (count, height, pieces[0].shape[1])

    def kernel(*refs):
        ins, (out, raw, wide, sems) = refs[:count], refs[-4:]
        shard, slot, _ = place_of()
        copies = Copies(sems)
        loads = [copies.start(ref.at[0:height, :], raw.at[j]) for j, ref in enumerate(ins)]
        stores = []
        for j in range(count):
            loads[j].wait()
            wide[j] = raw[j].astype(F32)
            at = where(slot ^ (0, 2, 1, 3)[j], shard)
            if parts == 0:
                stores.append(copies.start(wide.at[j], out.at[span(at, size), :]))
            for i in range(parts):
                cols = pl.ds(pl.multiple_of(i * per + at * size, size), size)
                source = wide.at[j, :, i * size : (i + 1) * size]
                stores.append(copies.start(source, out.at[:, cols]))
        for copy in stores:
            copy.wait()

    args = list(pieces) + ([] if held is None else [held])
    return pl.pallas_call(
        kernel,
        in_specs=[pl.BlockSpec(memory_space=pl.ANY)] * len(args),
        out_specs=pl.BlockSpec(memory_space=pl.ANY),
        out_shape=shaped(shape, F32),
        scratch_shapes=[
            pltpu.VMEM(held_shape, BF16),
            pltpu.VMEM(held_shape, F32),
            pltpu.SemaphoreType.DMA((count * (1 + max(parts, 1)),)),
        ],
        input_output_aliases={} if held is None else {count: 0},
        compiler_params=pltpu.CompilerParams(vmem_limit_bytes=LIMIT // 2),
        cost_estimate=SMALL,
        name="place",
    )(*args)


def fold(left, right, rows=None, name="fold"):
    count = rows or left.shape[0]
    shape = (count, left.shape[1])

    def kernel(a, b, out, a_v, b_v, sems):
        copies = Copies(sems)
        first = copies.start(a.at[a.shape[0] - count :, :], a_v)
        second = copies.start(b.at[b.shape[0] - count :, :], b_v)
        first.wait()
        second.wait()
        a_v[...] = (a_v[...].astype(F32) + b_v[...].astype(F32)).astype(BF16)
        copies.start(a_v, out).wait()

    scratch = [pltpu.VMEM(shape, BF16)] * 2 + [pltpu.SemaphoreType.DMA((3,))]
    return call(kernel, name, [(left, ANY), (right, ANY)], [(shaped(shape), ANY)], scratch)[0]


def keep_sum(near, far, got):
    count, width = got.shape[0] // 2, got.shape[1]

    def kernel(a, b, c, own, give, a_v, b_v, c_v, o_v, sems):
        copies = Copies(sems)
        loads = [copies.start(r.at[0 : 2 * count, :], v) for r, v in ((a, a_v), (b, b_v), (c, c_v))]
        for copy in loads:
            copy.wait()
        total = a_v[...].astype(F32) + b_v[...].astype(F32) + c_v[...].astype(F32)
        o_v[...] = total[0:count, :]
        a_v[0:count, :] = total[count:, :].astype(BF16)
        stores = [copies.start(o_v, own), copies.start(a_v.at[0:count, :], give)]
        for copy in stores:
            copy.wait()

    scratch = [pltpu.VMEM((2 * count, width), BF16)] * 3 + [pltpu.VMEM((count, width), F32)]
    return call(
        kernel,
        "keep",
        [(near, ANY), (far, ANY), (got, ANY)],
        [(shaped((count, width), F32), ANY), (shaped((count, width)), ANY)],
        scratch + [pltpu.SemaphoreType.DMA((5,))],
    )


def joint_kernel(*refs):
    ins, (total, dense, raw, wide, sems) = refs[:4], refs[4:]
    shard, slot, _ = place_of()
    owned = total.shape[0]
    part = dense.shape[0] // SPLIT
    copies = Copies(sems)
    loads = [copies.start(ref.at[0:owned, :], raw.at[j]) for j, ref in enumerate(ins)]
    stores = []
    for j in range(4):
        loads[j].wait()
        wide[j] = raw[j].astype(F32)
        at = slot ^ (0, 2, 1, 3)[j]
        for i in range(3):
            where = i * (total.shape[1] // 3) + (shard * SPLIT + at) * part
            cols = pl.ds(pl.multiple_of(where, part), part)
            stores.append(copies.start(wide.at[j, :, i * part : (i + 1) * part], total.at[:, cols]))
        each = raw.shape[2] - 3 * part
        for i in range(owned // part):
            source = wide.at[j, i * part : (i + 1) * part, 3 * part :]
            target = dense.at[span(at, part), i * each : (i + 1) * each]
            stores.append(copies.start(source, target))
    for copy in stores:
        copy.wait()


def other_kernel(*refs):
    own, ins, refs = refs[:4], refs[4:8], refs[9:]
    total, qkv_o, in_o, out_o, dense_o, g1, b1, g2, b2, raw, wide, edge, flat, joint, in_b, sems = refs
    shard, slot, _ = place_of()
    owned = total.shape[0]
    width = total.shape[1] // 3
    part = raw.shape[2] // 3
    hidden = in_o.shape[0] // SPLIT
    copies = Copies(sems)
    edges = [copies.start(ref.at[owned:, 0 : 3 * part], edge.at[j]) for j, ref in enumerate(own)]
    loads = [copies.start(ref, raw.at[j]) for j, ref in enumerate(ins)]
    stores = []
    for j in range(4):
        loads[j].wait()
        wide[j] = raw[j].astype(F32)
        at = slot ^ (0, 2, 1, 3)[j]
        for i in range(3):
            where = i * width + ((1 - shard) * SPLIT + at) * part
            cols = pl.ds(pl.multiple_of(where, part), part)
            source = wide.at[j, 0:owned, i * part : (i + 1) * part]
            stores.append(copies.start(source, total.at[:, cols]))
    for copy in edges:
        copy.wait()
    mine = [edge[j].astype(F32) for j in range(4)]
    theirs = [wide[j, owned:, :] for j in range(4)]
    every = sum(mine) + sum(theirs)
    per = -(-width // (3 * part))
    for i, vectors in enumerate(((g1,), (b1,), (g2,), (b2,), (out_o, dense_o))):
        flat[...] = jnp.concatenate([every[i * per + k : i * per + k + 1] for k in range(per)], axis=1)[:, 0:width]
        for ref in vectors:
            ref[...] = flat[:, span(shard, owned)].reshape(owned)
    row = 5 * per
    long = -(-hidden // (3 * part))
    for j in range(4):
        at = slot ^ (0, 2, 1, 3)[j]
        sums = jnp.concatenate([mine[j][row + k : row + k + 1] for k in range(long)], axis=1)
        in_b[:, span(at, hidden)] = sums[:, 0:hidden]
        for values, group in ((mine[j], shard), (theirs[j], 1 - shard)):
            for i in range(3):
                piece = values[row + long : row + long + 1, i * part : (i + 1) * part]
                joint[i : i + 1, span(group * SPLIT + at, part)] = piece
    thirds = [joint[i : i + 1, k * owned : (k + 1) * owned] for i in range(3) for k in range(2)]
    for i in range(3):
        third = jnp.where(shard == 0, thirds[i], thirds[3 + i])
        qkv_o[i * owned : (i + 1) * owned] = third.reshape(owned)
    in_o[...] = in_b[...].reshape(in_o.shape)
    for copy in stores:
        copy.wait()


def finish_kernel(length, tok, cot, own, got, params, result, grad_tokens):
    rows, width = tok.shape
    live = lax.broadcasted_iota(jnp.int32, (rows, width), 0) < length[0]
    values = tok[...].astype(F32)
    mixed = own[:, 0:width] + got[:, 0:width].astype(F32) + params[3:4, :] + params[4:5, :]
    result[...] = (values + jnp.where(live, mixed, 0.0)).astype(BF16)
    centre = values - jnp.mean(values, axis=-1, keepdims=True)
    root = lax.rsqrt(jnp.mean(centre * centre, axis=-1, keepdims=True) + 1e-05)
    hat = centre * root
    inner = own[:, width:] + got[:, width:].astype(F32)
    inner = inner - jnp.mean(inner, axis=-1, keepdims=True) - hat * jnp.mean(inner * hat, axis=-1, keepdims=True)
    grad_tokens[...] = (cot[...].astype(F32) + inner * root).astype(BF16)


def turn_tables(seq_rows, columns):
    half = ROT // 2
    inverse = np.float32(10000.0) ** (-(2.0 * np.arange(half, dtype=np.float32)) / np.float32(ROT))
    angles = np.arange(seq_rows, dtype=np.float32)[:, None] * inverse.astype(np.float32)[None, :]
    cosine = np.ones((seq_rows, HEAD_DIM), np.float32)
    low = np.zeros((seq_rows, HEAD_DIM), np.float32)
    high = np.zeros((seq_rows, HEAD_DIM), np.float32)
    cosine[:, :half] = cosine[:, half:ROT] = np.cos(angles)
    low[:, :half] = -np.sin(angles)
    high[:, half:ROT] = np.sin(angles)
    return [jnp.asarray(np.tile(t, (1, columns // HEAD_DIM))) for t in (cosine, low, high)]


ORDER = (
    "far", "mob", "moa", "coa", "fold", "tja", "mia", "mib", "cob", "poa",
    "xoa", "cia", "tjb", "pob", "keep", "xob", "cib", "mja", "pia", "xia",
    "sob", "soa", "mjb", "pib", "xib", "loa", "cja", "sia", "lob", "pja",
    "cjb", "xja", "sib", "pjb", "xjb", "lia", "lib", "sja", "end", "sjb",
    "lja",
)


def make_pairs(mesh):
    reps = mesh.shape["rep"]

    def swap_rep(values, bit):
        return lax.ppermute(values, "rep", [(i, i ^ bit) for i in range(reps)])

    def swap_shard(values):
        return lax.ppermute(values, "shard", [(0, 1), (1, 0)])

    def line_permute(values, pairs):
        pairs = [(a * SPLIT + i, b * SPLIT + i) for a, b in pairs for i in range(SPLIT)]
        return lax.ppermute(values, "rep", pairs)

    def after(value, other):
        return lax.optimization_barrier((value, other))[0]

    def on_device(
        tokens, cotangent, lengths, qkv_weight, qkv_bias, dense_weight, dense_bias, in_weight,
        in_bias, out_weight, out_bias, norm1_gain, norm1_bias, norm2_gain, norm2_bias,
    ):
        seq_rows, width = tokens.shape
        owned = width // 2
        hidden = in_weight.shape[1]
        part_f, part_h = hidden // GROUP, width // GROUP
        rows = GROUP * seq_rows
        halves = [qkv_bias, dense_bias, out_bias, norm1_gain, norm1_bias, norm2_gain, norm2_bias]
        packed, branch_sum, in_b, in_give, qkv_give = call(
            pack_kernel,
            "pack",
            [(lengths, SCALAR)]
            + [(a, ANY) for a in [tokens, cotangent, in_bias, *halves, in_weight, qkv_weight]],
            [
                (shaped((2 * seq_rows + TAIL, width)), WHOLE),
                (shaped((1, width), F32), WHOLE),
                (shaped((1, part_f), F32), WHOLE),
                (shaped((owned, part_f)), WHOLE),
                (shaped((owned, 3 * part_h)), WHOLE),
            ],
            [pltpu.VMEM((seq_rows, width), BF16)] * 2
            + [pltpu.VMEM(v.shape, BF16) for v in [in_bias, *halves]]
            + [pltpu.SemaphoreType.DMA((14,))],
        )
        beside = swap_rep(packed, 2)
        across = swap_shard(packed)
        beyond = swap_rep(after(across, beside), 2)
        in_got = swap_shard(in_give)
        qkv_got = swap_shard(qkv_give)
        pieces = [packed, across, beside, after(beyond, in_got)]
        pieces += [swap_rep(v, 1) for v in pieces]

        normed, xhat, active, grad_before, branch, out_all, in_mine, in_theirs, params, lens, in_sum = call(
            hidden_kernel,
            "hidden",
            [(p, ANY) for p in pieces]
            + [(in_weight, ANY), (in_got, ANY), (out_weight, ANY), (in_b, WHOLE)],
            [
                (shaped((rows, width)), ANY),
                (shaped((rows, width)), ANY),
                (shaped((rows, part_f)), ANY),
                (shaped((rows, part_f)), ANY),
                (shaped((rows, width)), ANY),
                (shaped((part_f, width)), ANY),
                (shaped((owned, part_f)), ANY),
                (shaped((owned, part_f)), ANY),
                (shaped((TAIL, width), F32), WHOLE),
                (shaped((GROUP * 8, 128), F32), WHOLE),
                (shaped((1, part_f), F32), WHOLE),
            ],
            [
                pltpu.VMEM((rows, width), BF16),
                pltpu.VMEM((rows, width), BF16),
                pltpu.VMEM((GROUP, TAIL, width), BF16),
                pltpu.VMEM((width, part_f), BF16),
                pltpu.VMEM((part_f, width), BF16),
                pltpu.VMEM((rows, width), BF16),
                pltpu.VMEM((rows, width), BF16),
                pltpu.VMEM((rows, width), BF16),
                pltpu.VMEM((rows, part_f), BF16),
                pltpu.VMEM((rows, part_f), F32),
                pltpu.VMEM((rows, part_f), BF16),
                pltpu.VMEM((part_f, width), BF16),
                pltpu.VMEM((owned, part_f), BF16),
                pltpu.VMEM((owned, part_f), BF16),
                pltpu.SemaphoreType.DMA((3 * GROUP + 3 + 9,)),
            ],
        )
        in_other = swap_shard(in_theirs)

        blocks = [normed, branch, active, grad_before, xhat, lens]
        whole = [qkv_weight, qkv_got, dense_weight, out_weight, in_weight, in_got, params]
        tables = turn_tables(seq_rows, part_h)
        sizes = (width, part_h, part_f)
        line = lax.axis_index("rep") // SPLIT
        inner_line = (line == 1) | (line == 2)
        last = [params]

        def then(value):
            return after(value, last[0])

        def did(value):
            last[0] = value
            return value

        def added(left, right):
            total = (left.astype(F32) + right.astype(F32)).astype(BF16)
            return did(lax.optimization_barrier(total))

        def meet(chunk):
            return added(then(chunk), line_permute(chunk, [(0, 1), (3, 2)]))

        def cross(near):
            return added(then(near), line_permute(near, [(1, 2), (2, 1)]))

        def spread(both):
            got = line_permute(both, [(1, 0), (2, 3)])
            return did(jnp.where(inner_line, then(both), got))

        half_f = (hidden // 2, width)
        wide = 3 * part_h
        here = lambda slot, shard: shard * SPLIT + slot
        there = lambda slot, shard: (1 - shard) * SPLIT + slot
        goes = {
            "oa": ("out", half_f, part_f // 2, lambda slot, shard: 2 * slot, 0),
            "ob": ("out", half_f, part_f // 2, lambda slot, shard: 2 * slot + 1, 0),
            "ia": ("in", (owned, hidden), part_f, here, 1),
            "ib": ("in", (owned, hidden), part_f, there, 1),
        }
        totals = {"out": None, "in": None}

        far, near, joint_a, joint_theirs = attention(
            blocks, whole, tables, [in_sum, branch_sum], seq_rows, sizes
        )
        did(joint_a)
        got = line_permute(out_all, [(0, 1), (3, 2)])
        half = part_f // 2
        state = {"oa": (out_all[:half], got[:half]), "ob": (out_all[half:], got[half:])}
        state |= {"ia": in_mine, "ib": in_other, "ja": joint_a}
        state["jb"] = swap_shard(joint_theirs)
        for token in ORDER:
            what, name = token[0], token[1:]
            held = state.get(name)
            if what == "t":
                state[name] = then(held)
            elif what == "m":
                state[name] = added(then(held[0]), held[1]) if name[0] == "o" else meet(held)
            elif what == "c":
                state[name] = cross(held)
            elif what == "p":
                state[name] = spread(held)
            elif what == "x":
                state[name] = [held, swap_rep(then(held), 2)]
            elif what == "s":
                state[name] = held + [swap_rep(then(v), 1) for v in held]
            elif what == "l" and name in goes:
                kind, *how = goes[name]
                totals[kind] = did(placed(totals[kind], [then(held[0])] + held[1:], *how))
            elif token == "lja":
                total_qkv, total_dense = call(
                    joint_kernel,
                    "place_joint",
                    [(then(held[0]), ANY)] + [(a, ANY) for a in held[1:]],
                    [(shaped((owned, 3 * width), F32), ANY), (shaped((owned, width), F32), ANY)],
                    [
                        pltpu.VMEM((4, owned, held[0].shape[1]), BF16),
                        pltpu.VMEM((4, owned, held[0].shape[1]), F32),
                        pltpu.SemaphoreType.DMA((4 * (4 + owned // part_h),)),
                    ],
                )
                did(total_dense)
            elif token == "far":
                far = swap_rep(then(far), 1)
            elif token == "fold":
                give = swap_rep(did(fold(then(near), far, 2 * seq_rows)), 2)
            elif token == "keep":
                keep, give = keep_sum(then(near), far, give)
                did(keep)
                give = swap_shard(give)
            elif token == "end":
                result, grad_tokens = call(
                    finish_kernel,
                    "finish",
                    [(then(lengths), SCALAR)]
                    + [(a, WHOLE) for a in (tokens, cotangent, keep, give, params)],
                    [(shaped((seq_rows, width)), WHOLE)] * 2,
                )
                did(result)
        total_out, total_in = totals["out"], totals["in"]
        joint_a, joint_b = state["ja"], state["jb"]
        sizes = [3 * owned, hidden // 2] + 6 * [owned]
        total_qkv, *vectors = pl.pallas_call(
            other_kernel,
            out_shape=[shaped(total_qkv.shape, F32)] + [shaped((n,), F32) for n in sizes],
            in_specs=[ANY] * 9,
            out_specs=[ANY] + [WHOLE] * 8,
            scratch_shapes=[
                pltpu.VMEM((4, owned + VECTORS, wide), BF16),
                pltpu.VMEM((4, owned + VECTORS, wide), F32),
                pltpu.VMEM((4, VECTORS, wide), BF16),
                pltpu.VMEM((1, width), F32),
                pltpu.VMEM((3, width), F32),
                pltpu.VMEM((1, hidden // 2), F32),
                pltpu.SemaphoreType.DMA((20,)),
            ],
            input_output_aliases={8: 0},
            compiler_params=pltpu.CompilerParams(vmem_limit_bytes=LIMIT),
            cost_estimate=SMALL,
            name="place_other",
        )(*joint_a, *joint_b, total_qkv)
        qkv_b, in_b, out_b, dense_b, g1, b1, g2, b2 = vectors
        return (
            result, grad_tokens, total_qkv, qkv_b, total_dense, dense_b, total_in, in_b, total_out, out_b,
            g1, b1, g2, b2,
        )

    return on_device


def solution(mesh):
    rows = P(("rep", "shard"), None)
    vector = P("shard")
    matrix = P("shard", None)
    weights = (matrix, vector)
    in_specs = (rows, rows, P(("rep", "shard"))) + 4 * weights + 4 * (vector,)
    out_specs = (rows, rows) + 4 * weights + 4 * (vector,)
    paired = mesh.shape["shard"] == 2 and mesh.shape["rep"] == SPLIT * LINES
    body = make_pairs(mesh) if paired else make(mesh)
    return jax.shard_map(body, mesh=mesh, in_specs=in_specs, out_specs=out_specs, check_vma=False)
```

```python
import jax
import jax.numpy as jnp
import numpy as np
from jax import lax
from jax.experimental import pallas as pl
from jax.experimental.pallas import tpu as pltpu
from jax.sharding import PartitionSpec as P

HEAD_DIM = 64
ROT = 16
F32 = jnp.float32
BF16 = jnp.bfloat16
EXTRA = 16


def rotary(values, turn):
    seq_rows = values.shape[-2]
    half = ROT // 2
    inverse = 10000.0 ** (-(2.0 * jnp.arange(half).astype(F32)) / ROT)
    angles = jnp.arange(seq_rows).astype(F32)[:, None] * inverse[None, :]
    cosine = jnp.cos(angles)
    sine = jnp.sin(angles) * turn
    first = values[..., :half]
    second = values[..., half:ROT]
    return jnp.concatenate(
        [first * cosine - second * sine, second * cosine + first * sine, values[..., ROT:]],
        axis=-1,
    )


def dot(left, right):
    return jnp.dot(left, right, preferred_element_type=F32)


def dot_nt(left, right):
    return lax.dot_general(left, right, (((1,), (1,)), ((), ())), preferred_element_type=F32)


def dot_tn(left, right):
    return lax.dot_general(left, right, (((0,), (0,)), ((), ())), preferred_element_type=F32)


def plan(mesh_shape, heads):
    shards, reps = mesh_shape["shard"], mesh_shape["rep"]
    split = 1
    while split < 4 and reps % (2 * split) == 0 and heads % (2 * split * shards) == 0:
        split *= 2
    return shards, reps, split


def make(mesh):
    def on_device(
        tokens,
        cotangent,
        lengths,
        qkv_weight,
        qkv_bias,
        dense_weight,
        dense_bias,
        in_weight,
        in_bias,
        out_weight,
        out_bias,
        norm1_gain,
        norm1_bias,
        norm2_gain,
        norm2_bias,
    ):
        seq_rows, width = tokens.shape
        heads = width // HEAD_DIM
        shards, reps, split = plan(dict(mesh.shape), heads)
        lines = reps // split
        group = shards * split
        owned = width // shards
        hidden = in_weight.shape[1]
        part_f = hidden // group
        part_h = width // group
        own_heads = part_h // HEAD_DIM
        shard = lax.axis_index("shard")
        rep = lax.axis_index("rep")
        slot = lax.rem(rep, split)
        line = rep // split
        block = shard * split + slot
        bits = []
        bit = split // 2
        while bit:
            bits.append(bit)
            bit //= 2

        def swap_rep(values, bit):
            return lax.ppermute(values, "rep", [(i, i ^ bit) for i in range(reps)])

        def swap_shard(values):
            return lax.ppermute(values, "shard", [(0, 1), (1, 0)])

        def gather_shard(values):
            if shards == 1:
                return values
            if shards == 2:
                return jnp.concatenate([values, swap_shard(values)], axis=0)
            return lax.all_gather(values, "shard", axis=0, tiled=True)

        def gather_rep(values):
            for bit in bits:
                values = jnp.concatenate([values, swap_rep(values, bit)], axis=0)
            return values

        def scatter_sum(values):
            for bit in reversed(bits):
                half = values.shape[0] // 2
                values = values[:half] + swap_rep(values[half:].astype(BF16), bit).astype(F32)
            if shards == 2:
                half = values.shape[0] // 2
                values = values[:half] + swap_shard(values[half:].astype(BF16)).astype(F32)
            elif shards > 2:
                values = lax.psum_scatter(
                    values.astype(BF16), "shard", scatter_dimension=0, tiled=True
                ).astype(F32)
            return values

        def ordered(mine, other, flag, axis):
            first = jnp.where(flag, other, mine)
            second = jnp.where(flag, mine, other)
            return jnp.concatenate([first, second], axis=axis)

        def columns_of(weight, parts, size):
            rows = weight.shape[0]
            cut = weight.reshape(rows, parts, group, size)

            def piece(at):
                return lax.dynamic_slice_in_dim(cut, at, 1, 2).reshape(rows, parts * size)

            if shards == 1:
                return piece(block)
            if shards == 2:
                other = swap_shard(piece((1 - shard) * split + slot))
                return ordered(piece(block), other, shard == 1, 0)
            picked = jnp.stack([piece(s * split + slot) for s in range(shards)], axis=0)
            return lax.all_to_all(picked, "shard", 0, 0, tiled=True).reshape(
                rows * shards, parts * size
            )

        def rows_exchange(grad):
            if shards == 1:
                return [grad]
            if shards == 2:
                mine = lax.dynamic_slice_in_dim(grad, shard * owned, owned, 0)
                other = swap_shard(lax.dynamic_slice_in_dim(grad, (1 - shard) * owned, owned, 0))
                return [jnp.where(shard == 1, other, mine), jnp.where(shard == 1, mine, other)]
            got = lax.all_to_all(grad, "shard", 0, 0, tiled=True)
            return [got[s * owned : (s + 1) * owned] for s in range(shards)]

        length = lengths[0]
        live = (jnp.arange(seq_rows) < length).astype(F32)[:, None]
        branch = (live * cotangent.astype(F32)).astype(BF16)
        halves = [dense_bias, out_bias, norm1_gain, norm1_bias, norm2_gain, norm2_bias]
        params = jnp.concatenate([qkv_bias] + halves)
        params = jnp.pad(params, (0, 8 * width - params.shape[0])).reshape(8, width)
        length_rows = jnp.broadcast_to(length.astype(BF16), (EXTRA - 8, width))
        packed = jnp.concatenate([tokens, params, length_rows], axis=0)
        packed = gather_shard(packed)
        branch_all = gather_shard(branch)
        in_w = columns_of(in_weight, 1, part_f)
        packed_all = gather_rep(packed).reshape(group, seq_rows + EXTRA, width)
        branch_all = gather_rep(branch_all)
        qkv_w = columns_of(qkv_weight, 3, part_h)

        by_shard = packed.reshape(shards, seq_rows + EXTRA, width)[:, seq_rows : seq_rows + 8]
        by_shard = by_shard.reshape(shards, 8 * width)
        if shards == 2:
            by_shard = jnp.where(shard == 1, by_shard[::-1], by_shard)

        def whole(at, size):
            return by_shard[:, at : at + size].reshape(shards * size).astype(F32)

        qkv_b = whole(0, 3 * owned)
        at = 3 * owned
        full = []
        for _ in halves:
            full.append(whole(at, owned))
            at += owned
        dense_b, out_b, gain_one, shift_one, gain_two, shift_two = full
        all_lengths = packed_all[:, seq_rows + 8, 0].astype(jnp.int32)
        rows = group * seq_rows
        values = packed_all[:, :seq_rows].reshape(rows, width).astype(F32)

        centre = values - jnp.mean(values, axis=-1, keepdims=True)
        spread = jnp.mean(centre * centre, axis=-1, keepdims=True)
        root = lax.rsqrt(spread + 1e-05)
        xhat = centre * root
        normed = (xhat * gain_one + shift_one).astype(BF16)
        normed_two = (xhat * gain_two + shift_two).astype(BF16)

        out_w = lax.dynamic_slice_in_dim(out_weight, slot * part_f, part_f, 0)
        in_b = lax.dynamic_slice_in_dim(in_bias, slot * part_f, part_f, 0).astype(F32)
        before = dot(normed_two, in_w) + in_b
        cdf = 0.5 * (1.0 + lax.erf(before * (0.5**0.5)))
        active = (before * cdf).astype(BF16)
        slope = cdf + before * jnp.exp(-0.5 * before * before) * 0.3989422804014327
        grad_before = (dot_nt(branch_all, out_w) * slope).astype(BF16)
        grad_out_w = dot_tn(active, branch_all).astype(BF16)
        grad_in_w = dot_tn(normed_two, grad_before).astype(BF16)
        grad_two = dot_nt(grad_before, in_w)

        scaling = HEAD_DIM ** (-0.5)
        bias = lax.dynamic_slice_in_dim(qkv_b.reshape(3, group, part_h), block, 1, 1)
        joint = dot(normed, qkv_w) + bias.reshape(3 * part_h)
        split_joint = joint.reshape(group, seq_rows, 3, own_heads, HEAD_DIM).transpose(2, 0, 3, 1, 4)
        query = rotary(split_joint[0], 1.0).astype(BF16)
        keys = rotary(split_joint[1], 1.0).astype(BF16)
        vals = split_joint[2].astype(BF16)
        position = jnp.arange(seq_rows)
        allowed = (position[None, :] <= position[:, None])[None] & (
            position[None, None, :] < all_lengths[:, None, None]
        )
        scores = jnp.einsum("bhpd,bhqd->bhpq", query, keys, preferred_element_type=F32) * scaling
        scores = jnp.where(allowed[:, None], scores, -1e30)
        raised = jnp.exp(scores - jnp.max(scores, axis=-1, keepdims=True))
        exact = raised / jnp.sum(raised, axis=-1, keepdims=True)
        probs = exact.astype(BF16)
        context = jnp.einsum("bhpq,bhqd->bhpd", probs, vals, preferred_element_type=F32)
        context = context.astype(BF16).transpose(0, 2, 1, 3).reshape(rows, part_h)
        dense_w = lax.dynamic_slice_in_dim(dense_weight, slot * part_h, part_h, 0)
        mixed = scatter_sum(dot(active, out_w) + dot(context, dense_w))
        result = (tokens.astype(F32) + live * (mixed + dense_b + out_b)).astype(BF16)

        grad_context = dot_nt(branch_all, dense_w).astype(BF16)
        grad_dense_w = dot_tn(context, branch_all).astype(BF16)
        grad_context = grad_context.reshape(group, seq_rows, own_heads, HEAD_DIM).transpose(0, 2, 1, 3)
        grad_probs = jnp.einsum(
            "bhpd,bhqd->bhpq", grad_context, vals, preferred_element_type=F32
        )
        grad_vals = jnp.einsum("bhpq,bhpd->bhqd", probs, grad_context, preferred_element_type=F32)
        grad_scores = (
            exact * (grad_probs - jnp.sum(grad_probs * exact, axis=-1, keepdims=True))
        ).astype(BF16)
        grad_query = jnp.einsum("bhpq,bhqd->bhpd", grad_scores, keys, preferred_element_type=F32)
        grad_keys = jnp.einsum("bhpq,bhpd->bhqd", grad_scores, query, preferred_element_type=F32)
        grad_joint = jnp.stack(
            [rotary(grad_query * scaling, -1.0), rotary(grad_keys * scaling, -1.0), grad_vals]
        ).astype(BF16)
        grad_joint = grad_joint.transpose(1, 3, 0, 2, 4).reshape(rows, 3 * part_h)
        grad_qkv_w = dot_tn(normed, grad_joint).astype(BF16)
        grad_one = dot_nt(grad_joint, qkv_w)

        inner = scatter_sum(grad_one * gain_one + grad_two * gain_two)
        own_xhat = xhat[:seq_rows] if shards <= 2 else None
        if own_xhat is None:
            own_xhat = lax.dynamic_slice_in_dim(xhat, shard * seq_rows, seq_rows, 0)
            own_root = lax.dynamic_slice_in_dim(root, shard * seq_rows, seq_rows, 0)
        else:
            own_root = root[:seq_rows]
        inner = (
            inner
            - jnp.mean(inner, axis=-1, keepdims=True)
            - own_xhat * jnp.mean(inner * own_xhat, axis=-1, keepdims=True)
        ) * own_root
        grad_tokens = (cotangent.astype(F32) + inner).astype(BF16)

        in_sum = jnp.sum(grad_before.astype(F32), axis=0)
        qkv_sum = jnp.sum(grad_joint.astype(F32), axis=0).reshape(3, 1, part_h)
        vectors = jnp.concatenate(
            [
                jnp.sum(grad_one * xhat, axis=0),
                jnp.sum(grad_one, axis=0),
                jnp.sum(grad_two * xhat, axis=0),
                jnp.sum(grad_two, axis=0),
                jnp.sum(branch.astype(F32), axis=0),
                lax.dynamic_update_slice_in_dim(jnp.zeros((hidden,), F32), in_sum, block * part_f, 0),
                lax.dynamic_update_slice_in_dim(
                    jnp.zeros((3, group, part_h), F32), qkv_sum, block, 1
                ).reshape(3 * width),
            ]
        )
        vectors = lax.psum(vectors, ("rep", "shard"))

        def own_part(at, size):
            piece = size // shards
            return lax.dynamic_slice_in_dim(vectors, at + shard * piece, piece, 0)

        in_parts = rows_exchange(grad_in_w)
        qkv_parts = rows_exchange(grad_qkv_w)
        chunks = [grad_out_w] + in_parts + [grad_dense_w] + qkv_parts
        if lines == 4:
            inner_line = (line == 1) | (line == 2)

            def line_permute(values, pairs):
                return lax.ppermute(
                    values,
                    "rep",
                    [(a * split + i, b * split + i) for a, b in pairs for i in range(split)],
                )

            summed = []
            for chunk in chunks:
                got = line_permute(chunk, [(0, 1), (3, 2)])
                near = lax.optimization_barrier((chunk.astype(F32) + got.astype(F32)).astype(BF16))
                got = line_permute(near, [(1, 2), (2, 1)])
                both = lax.optimization_barrier((near.astype(F32) + got.astype(F32)).astype(BF16))
                got = line_permute(both, [(1, 0), (2, 3)])
                summed.append(jnp.where(inner_line, both, got))
        else:
            groups = [[a * split + i for a in range(lines)] for i in range(split)]
            summed = [lax.psum(c, "rep", axis_index_groups=groups) for c in chunks]

        def gather_slots(values):
            values = values[None]
            for bit in reversed(bits):
                values = ordered(values, swap_rep(values, bit), (slot & bit) != 0, 0)
            return values

        summed = [gather_slots(c) for c in summed]
        total_out = summed[0].reshape(split * part_f, width).astype(F32)
        total_in = jnp.stack(summed[1 : 1 + shards])
        total_in = total_in.transpose(2, 0, 1, 3).reshape(owned, hidden).astype(F32)
        total_dense = summed[1 + shards].reshape(split * part_h, width).astype(F32)
        total_qkv = jnp.stack(summed[2 + shards :]).reshape(shards, split, owned, 3, part_h)
        total_qkv = total_qkv.transpose(2, 3, 0, 1, 4).reshape(owned, 3 * width).astype(F32)
        at_in = 5 * width
        at_qkv = at_in + hidden
        out_sum = own_part(4 * width, width)
        return (
            result,
            grad_tokens,
            total_qkv,
            own_part(at_qkv, 3 * width),
            total_dense,
            out_sum,
            total_in,
            own_part(at_in, hidden),
            total_out,
            out_sum,
            own_part(0, width),
            own_part(width, width),
            own_part(2 * width, width),
            own_part(3 * width, width),
        )

    return on_device


GROUP = 8
SPLIT = 4
LINES = 4
TAIL = 16
VECTORS = 32
ANY = pl.BlockSpec(memory_space=pltpu.HBM)
FREE = pl.BlockSpec(memory_space=pl.ANY)
SCALAR = pl.BlockSpec(memory_space=pltpu.SMEM)
WHOLE = pl.BlockSpec(memory_space=pltpu.VMEM)
LIMIT = 63 * 2**20
COST = pl.CostEstimate(flops=10**12, bytes_accessed=10**9, transcendentals=0)
SMALL = pl.CostEstimate(flops=10**6, bytes_accessed=0, transcendentals=0)


def shaped(shape, dtype=BF16):
    return jax.ShapeDtypeStruct(shape, dtype)


def call(kernel, name, ins, outs, scratch=()):
    return pl.pallas_call(
        kernel,
        out_shape=[shape for shape, _ in outs],
        in_specs=[spec for _, spec in ins],
        out_specs=[spec for _, spec in outs],
        scratch_shapes=list(scratch),
        compiler_params=pltpu.CompilerParams(vmem_limit_bytes=LIMIT if name in ("pack", "hidden") else LIMIT // 3),
        cost_estimate=COST if name == "hidden" else SMALL,
        name=name,
    )(*[array for array, _ in ins])


class Copies:
    def __init__(self, sems):
        self.sems, self.used = sems, 0

    def make(self, source, target):
        self.used += 1
        return pltpu.make_async_copy(source, target, self.sems.at[self.used - 1])

    def start(self, source, target):
        copy = self.make(source, target)
        copy.start()
        return copy


def place_of():
    shard = lax.axis_index("shard")
    slot = lax.rem(lax.axis_index("rep"), SPLIT)
    return shard, slot, shard * SPLIT + slot


def span(at, size):
    if isinstance(at, int):
        return pl.ds(at * size, size)
    return pl.ds(pl.multiple_of(at * size, size), size)


def pack_kernel(length, tok, cot, in_bias, qb, db, ob, g1, b1, g2, b2, in_weight, qkv_weight,
                packed, total, in_b, in_give, qkv_give, tok_v, cot_v, ib_v, qb_v, *rest):
    vecs, sems = rest[:-1], rest[-1]
    shard, slot, _ = place_of()
    twin = (1 - shard) * SPLIT + slot
    rows, width = tok_v.shape
    owned = vecs[0].shape[0]
    part_f, part_h = in_give.shape[1], qkv_give.shape[1] // 3
    copies = Copies(sems)
    first = [copies.start(tok, tok_v), copies.start(cot, cot_v), copies.start(in_bias, ib_v)]
    first.append(copies.start(qb, qb_v))
    first += [copies.start(a, b) for a, b in zip((db, ob, g1, b1, g2, b2), vecs)]
    given = [copies.start(in_weight.at[:, span(twin, part_f)], in_give)]
    for i in range(3):
        cols = pl.ds(pl.multiple_of(i * width + twin * part_h, part_h), part_h)
        target = qkv_give.at[:, i * part_h : (i + 1) * part_h]
        given.append(copies.start(qkv_weight.at[:, cols], target))
    for copy in first:
        copy.wait()
    live = lax.broadcasted_iota(jnp.int32, (rows, width), 0) < length[0]
    kept = jnp.where(live, cot_v[...].astype(F32), 0.0)
    packed[rows + TAIL :, :] = kept.astype(BF16)
    total[...] = jnp.sum(kept, axis=0, keepdims=True)
    packed[0:rows, :] = tok_v[...]
    whole = qb_v[...].astype(F32).reshape(1, 3 * owned)
    lines = [whole[:, i * owned : (i + 1) * owned] for i in range(3)]
    lines += [ref[...].astype(F32).reshape(1, owned) for ref in vecs]
    lines.append(jnp.full((TAIL - 9, owned), length[0].astype(F32)))
    packed[rows : rows + TAIL, 0:owned] = jnp.concatenate(lines, axis=0).astype(BF16)
    packed[rows : rows + TAIL, owned:width] = jnp.zeros((TAIL, width - owned), BF16)
    bias = ib_v[...].astype(F32).reshape(1, SPLIT * part_f)
    in_b[...] = sum(
        jnp.where(slot == i, bias[:, i * part_f : (i + 1) * part_f], 0.0) for i in range(SPLIT)
    )
    for copy in given:
        copy.wait()


def hidden_kernel(*refs):
    pieces, refs = refs[:GROUP], refs[GROUP:]
    (in_weight, in_got, out_weight, in_b, normed_o, xhat_o, active_o, grad_o, branch_o, out_o,
     own_o, other_o, params, lens, in_sum, every, branch, tails, w_full, out_w, normed, normed_two,
     xhat, active, slope, grad_before, grad_out, own, other, sems) = refs
    shard, slot, block = place_of()
    rows = pieces[0].shape[0] - TAIL >> 1
    owned, part = in_got.shape
    copies = Copies(sems)
    edge = [copies.start(p.at[rows : rows + TAIL, :], tails.at[i]) for i, p in enumerate(pieces)]
    first = [copies.start(p.at[0:rows, :], every.at[i * rows : (i + 1) * rows, :]) for i, p in enumerate(pieces)]
    first.append(copies.start(in_weight.at[:, span(block, part)], w_full.at[span(shard, owned), :]))
    first.append(copies.start(in_got, w_full.at[span(1 - shard, owned), :]))
    late = [copies.start(p.at[rows + TAIL :, :], branch.at[i * rows : (i + 1) * rows, :]) for i, p in enumerate(pieces)]
    late.append(copies.start(out_weight.at[span(slot, part), :], out_w))
    for copy in edge:
        copy.wait()
    params[:, span(shard, owned)] = tails[0, :, 0:owned].astype(F32)
    params[:, span(1 - shard, owned)] = tails[1, :, 0:owned].astype(F32)
    for i in range(GROUP):
        lens[i * 8 : (i + 1) * 8, :] = tails[i, :, 0:128].astype(F32)[8:]
    g1, b1, g2, b2 = (params[i : i + 1, :] for i in range(5, 9))
    for copy in first:
        copy.wait()
    step = 256

    def forward(i, carry):
        at = span(i, step)
        values = every[at, :].astype(F32)
        centre = values - jnp.mean(values, axis=-1, keepdims=True)
        spread = jnp.mean(centre * centre, axis=-1, keepdims=True)
        hat = centre * lax.rsqrt(spread + 1e-05)
        xhat[at, :] = hat.astype(BF16)
        normed[at, :] = (hat * g1 + b1).astype(BF16)
        two = (hat * g2 + b2).astype(BF16)
        normed_two[at, :] = two
        before = dot(two, w_full[...]) + in_b[...]
        cdf = 0.5 * (1.0 + lax.erf(before * (0.5**0.5)))
        active[at, :] = (before * cdf).astype(BF16)
        slope[at, :] = cdf + before * jnp.exp(-0.5 * before * before) * 0.3989422804014327
        return carry

    for i in range(GROUP * rows // step):
        forward(i, 0)
    done = [copies.start(normed, normed_o), copies.start(xhat, xhat_o), copies.start(active, active_o)]
    for copy in late:
        copy.wait()
    done.append(copies.start(branch, branch_o))

    def out_grad(j, carry):
        grad_out[span(j, step), :] = dot_tn(active[:, span(j, step)], branch[...]).astype(BF16)
        return carry

    lax.fori_loop(0, part // step, out_grad, 0)
    done.append(copies.start(grad_out, out_o))
    in_sum[...] = jnp.zeros_like(in_sum)

    def back(i, carry):
        at = span(i, step)
        grad = (dot_nt(branch[at, :], out_w[...]) * slope[at, :]).astype(BF16)
        grad_before[at, :] = grad
        in_sum[...] += jnp.sum(grad.astype(F32), axis=0, keepdims=True)
        return carry

    for i in range(GROUP * rows // step):
        back(i, 0)
    done.append(copies.start(grad_before, grad_o))
    for ref, target, where in ((other, other_o, 1 - shard), (own, own_o, shard)):

        def weight(j, carry, ref=ref, where=where):
            cols = span(where * (owned // step) + j, step)
            ref[span(j, step), :] = dot_tn(normed_two[:, cols], grad_before[...]).astype(BF16)
            return carry

        lax.fori_loop(0, owned // step, weight, 0)
        done.append(copies.start(ref, target))
    for copy in done:
        copy.wait()


def turn(values, tables, back):
    cosine, low, high = tables
    width = values.shape[1]
    ahead = pltpu.roll(values, width - ROT // 2, 1)
    behind = pltpu.roll(values, ROT // 2, 1)
    moved = ahead * low + behind * high
    return values * cosine - moved if back else values * cosine + moved


def attention_kernel(
    normed, branch, active, grad_before, xhat, lens, qkv_weight, qkv_got, dense_weight, out_weight,
    in_weight, in_got, params, cosine, low, high, in_sum, own_sum, far, near, mine_o, theirs_o,
    acc, dense, sums, jsum, vectors, w_full, dense_w, out_w, in_w, sems,
):
    shard, slot, block = place_of()
    rows, width = normed.shape
    part = dense_w.shape[0]
    owned, hidden = in_got.shape
    step = pl.program_id(0)

    copies = Copies(sems)
    mine, theirs = span(shard, owned), span(1 - shard, owned)
    early = [copies.make(qkv_got, w_full.at[theirs, :])]
    for i in range(3):
        cols = pl.ds(pl.multiple_of(i * width + block * part, part), part)
        target = w_full.at[mine, i * part : (i + 1) * part]
        early.append(copies.make(qkv_weight.at[:, cols], target))
    early.append(copies.make(dense_weight.at[span(slot, part), :], dense_w))
    late = [copies.make(out_weight.at[span(slot, hidden), :], out_w)]
    late.append(copies.make(in_weight.at[:, span(block, hidden)], in_w.at[mine, :]))
    late.append(copies.make(in_got, in_w.at[theirs, :]))

    @pl.when(step == 0)
    def _():
        for copy in early + late:
            copy.start()
        for ref in (acc, dense, sums, jsum):
            ref[...] = jnp.zeros_like(ref)
        for copy in early:
            copy.wait()

    scaling = HEAD_DIM**-0.5
    biases = []
    for i in range(3):
        at = i * width + block * part
        inside = lax.rem(at, 3 * owned)
        col = at // (3 * owned) * owned + lax.rem(inside, owned)
        cols = pl.ds(pl.multiple_of(col, part), part)
        biases.append(
            sum(jnp.where(inside // owned == r, params[r : r + 1, cols], 0.0) for r in range(3))
        )
    joint = dot(normed[...], w_full[...]) + jnp.concatenate(biases, axis=1)
    grad_context = dot_nt(branch[...], dense_w[...]).astype(BF16)
    seq = cosine.shape[0]
    tables = (cosine[...], low[...], high[...])
    at_p = lax.broadcasted_iota(jnp.int32, (seq, seq), 0)
    at_q = lax.broadcasted_iota(jnp.int32, (seq, seq), 1)
    head_of = lax.broadcasted_iota(jnp.int32, (seq, part), 1) // HEAD_DIM

    def apart(values):
        zero = jnp.zeros_like(values)
        return jnp.concatenate(
            [jnp.where(head_of == h, values, zero) for h in range(part // HEAD_DIM)], axis=0
        )

    def together(values):
        total = values[0:seq]
        for h in range(1, part // HEAD_DIM):
            total = jnp.where(head_of == h, values[h * seq : (h + 1) * seq], total)
        return total

    contexts, grads = [], []
    for one in range(rows // seq):
        at = slice(one * seq, (one + 1) * seq)
        query = turn(joint[at, 0:part], tables, False).astype(BF16)
        keys = turn(joint[at, part : 2 * part], tables, False).astype(BF16)
        vals = joint[at, 2 * part :].astype(BF16)
        allowed = (at_q <= at_p) & (at_q.astype(F32) < lens[8 * one + 7 : 8 * one + 8, :])
        gc = grad_context[at, :]
        keys_apart, vals_apart = apart(keys), apart(vals)
        scores = dot_nt(query, keys_apart) * scaling
        heads = range(part // HEAD_DIM)
        exact = []
        for head in heads:
            masked = jnp.where(allowed, scores[:, head * seq : (head + 1) * seq], -1e30)
            raised = jnp.exp(masked - jnp.max(masked, axis=-1, keepdims=True))
            exact.append(raised / jnp.sum(raised, axis=-1, keepdims=True))
        probs = jnp.concatenate(exact, axis=1).astype(BF16)
        contexts.append(dot(probs, vals_apart).astype(BF16))
        grad_probs = dot_nt(gc, vals_apart)
        grad_vals = together(dot_tn(probs, gc))
        grad_scores = []
        for head in heads:
            grad = grad_probs[:, head * seq : (head + 1) * seq]
            mean = jnp.sum(grad * exact[head], axis=-1, keepdims=True)
            grad_scores.append((exact[head] * (grad - mean)).astype(BF16))
        grad_scores = jnp.concatenate(grad_scores, axis=1)
        grad_query = turn(dot(grad_scores, keys_apart) * scaling, tables, True)
        grad_keys = turn(together(dot_tn(grad_scores, query)) * scaling, tables, True)
        grads.append(jnp.concatenate([grad_query, grad_keys, grad_vals], axis=1).astype(BF16))
    ctx = jnp.concatenate(contexts, axis=0)
    grad = jnp.concatenate(grads, axis=0)
    jsum[...] += jnp.sum(grad.astype(F32), axis=0, keepdims=True)
    acc[...] += dot_tn(normed[...], grad)
    dense[...] += dot_tn(ctx, branch[...])

    @pl.when(step == 0)
    def _():
        for copy in late:
            copy.wait()

    mixed = (dot(active[...], out_w[...]) + dot(ctx, dense_w[...])).astype(BF16)
    hat = xhat[...].astype(F32)
    one = dot_nt(grad, w_full[...])
    sums[0:1, :] += jnp.sum(one * hat, axis=0, keepdims=True)
    sums[1:2, :] += jnp.sum(one, axis=0, keepdims=True)
    two = dot_nt(grad_before[...], in_w[...])
    sums[2:3, :] += jnp.sum(two * hat, axis=0, keepdims=True)
    sums[3:4, :] += jnp.sum(two, axis=0, keepdims=True)
    inner = (one * params[5:6, :] + two * params[7:8, :]).astype(BF16)
    for ref, here in ((far, step < 2), (near, step >= 2)):

        @pl.when(here)
        def _(ref=ref):
            ref[:, 0:width] = mixed
            ref[:, width:] = inner

    @pl.when(step == pl.num_programs(0) - 1)
    def _():
        wide = 3 * part
        vectors[...] = jnp.zeros_like(vectors)
        row = 0
        for source in [sums[i : i + 1, :] for i in range(4)] + [own_sum[...], in_sum[...], jsum[...]]:
            for at in range(0, source.shape[1], wide):
                piece = source[:, at : at + wide]
                vectors[row : row + 1, 0 : piece.shape[1]] = piece
                row += 1
        for ref, which in ((mine_o, shard), (theirs_o, 1 - shard)):
            ref[0:owned, 0:wide] = acc[span(which, owned), :].astype(BF16)
            ref[owned:, 0:wide] = vectors[...].astype(BF16)
        each = width * part // owned
        for i in range(owned // part):
            cols = slice(i * each, (i + 1) * each)
            mine_o[i * part : (i + 1) * part, wide:] = dense[:, cols].astype(BF16)
        mine_o[owned:, wide:] = jnp.zeros((VECTORS, each), BF16)


def attention(blocks, whole, tables, small, seq_rows, sizes):
    width, part, hidden = sizes
    rows, steps = 2 * seq_rows, 4
    owned, wide = width // 2, 3 * part

    def block(array, height):
        return pl.BlockSpec((height, array.shape[1]), lambda i: ((i + 2) % 4, 0))

    def full(shape):
        return pl.BlockSpec(shape, lambda i: (0, 0))

    outer = pl.BlockSpec((rows, 2 * width), lambda i: (jnp.minimum(i, 1), 0))
    inner = pl.BlockSpec((rows, 2 * width), lambda i: (jnp.maximum(i - 2, 0), 0))
    mine = (owned + VECTORS, wide + width * part // owned)
    theirs = (owned + VECTORS, wide)
    half = shaped((2 * rows, 2 * width))
    args = [*blocks, *whole, *tables, *small]
    specs = [block(a, h) for a, h in zip(blocks, [rows] * 5 + [16])]
    specs += [ANY, FREE, ANY, ANY, ANY, FREE] + [full(a.shape) for a in [whole[6], *tables, *small]]
    sums = [(width, wide), (part, width), (8, width), (1, wide), (VECTORS, wide)]
    weights = [(width, wide), (part, width), (hidden, width), (width, hidden)]
    return pl.pallas_call(
        attention_kernel,
        grid=(steps,),
        out_shape=[half, half, shaped(mine), shaped(theirs)],
        in_specs=specs,
        out_specs=[outer, inner, full(mine), full(theirs)],
        scratch_shapes=[pltpu.VMEM(s, F32) for s in sums]
        + [pltpu.VMEM(s, BF16) for s in weights]
        + [pltpu.SemaphoreType.DMA((8,))],
        compiler_params=pltpu.CompilerParams(vmem_limit_bytes=LIMIT),
        cost_estimate=COST,
        name="attention",
    )(*args)


def placed(held, pieces, shape, size, where, parts=1):
    count = len(pieces)
    per = shape[1] // max(parts, 1)
    height = pieces[0].shape[0] if parts else size
    held_shape = (count, height, pieces[0].shape[1])

    def kernel(*refs):
        ins, (out, raw, wide, sems) = refs[:count], refs[-4:]
        shard, slot, _ = place_of()
        copies = Copies(sems)
        loads = [copies.start(ref.at[0:height, :], raw.at[j]) for j, ref in enumerate(ins)]
        stores = []
        for j in range(count):
            loads[j].wait()
            wide[j] = raw[j].astype(F32)
            at = where(slot ^ (0, 2, 1, 3)[j], shard)
            if parts == 0:
                stores.append(copies.start(wide.at[j], out.at[span(at, size), :]))
            for i in range(parts):
                cols = pl.ds(pl.multiple_of(i * per + at * size, size), size)
                source = wide.at[j, :, i * size : (i + 1) * size]
                stores.append(copies.start(source, out.at[:, cols]))
        for copy in stores:
            copy.wait()

    args = list(pieces) + ([] if held is None else [held])
    return pl.pallas_call(
        kernel,
        in_specs=[pl.BlockSpec(memory_space=pl.ANY)] * len(args),
        out_specs=pl.BlockSpec(memory_space=pl.ANY),
        out_shape=shaped(shape, F32),
        scratch_shapes=[
            pltpu.VMEM(held_shape, BF16),
            pltpu.VMEM(held_shape, F32),
            pltpu.SemaphoreType.DMA((count * (1 + max(parts, 1)),)),
        ],
        input_output_aliases={} if held is None else {count: 0},
        compiler_params=pltpu.CompilerParams(vmem_limit_bytes=LIMIT // 2),
        cost_estimate=SMALL,
        name="place",
    )(*args)


def fold(left, right, rows=None, name="fold"):
    count = rows or left.shape[0]
    shape = (count, left.shape[1])

    def kernel(a, b, out, a_v, b_v, sems):
        copies = Copies(sems)
        first = copies.start(a.at[a.shape[0] - count :, :], a_v)
        second = copies.start(b.at[b.shape[0] - count :, :], b_v)
        first.wait()
        second.wait()
        a_v[...] = (a_v[...].astype(F32) + b_v[...].astype(F32)).astype(BF16)
        copies.start(a_v, out).wait()

    scratch = [pltpu.VMEM(shape, BF16)] * 2 + [pltpu.SemaphoreType.DMA((3,))]
    return call(kernel, name, [(left, FREE), (right, FREE)], [(shaped(shape), FREE)], scratch)[0]


def keep_sum(near, far, got):
    count, width = got.shape[0] // 2, got.shape[1]

    def kernel(a, b, c, own, give, a_v, b_v, c_v, o_v, sems):
        copies = Copies(sems)
        loads = [copies.start(r.at[0 : 2 * count, :], v) for r, v in ((a, a_v), (b, b_v), (c, c_v))]
        for copy in loads:
            copy.wait()
        total = a_v[...].astype(F32) + b_v[...].astype(F32) + c_v[...].astype(F32)
        o_v[...] = total[0:count, :]
        a_v[0:count, :] = total[count:, :].astype(BF16)
        stores = [copies.start(o_v, own), copies.start(a_v.at[0:count, :], give)]
        for copy in stores:
            copy.wait()

    scratch = [pltpu.VMEM((2 * count, width), BF16)] * 3 + [pltpu.VMEM((count, width), F32)]
    return call(
        kernel,
        "keep",
        [(near, FREE), (far, FREE), (got, FREE)],
        [(shaped((count, width), F32), ANY), (shaped((count, width)), ANY)],
        scratch + [pltpu.SemaphoreType.DMA((5,))],
    )


def joint_kernel(*refs):
    ins, (total, dense, raw, wide, sems) = refs[:4], refs[4:]
    shard, slot, _ = place_of()
    owned = total.shape[0]
    part = dense.shape[0] // SPLIT
    copies = Copies(sems)
    loads = [copies.start(ref.at[0:owned, :], raw.at[j]) for j, ref in enumerate(ins)]
    stores = []
    for j in range(4):
        loads[j].wait()
        wide[j] = raw[j].astype(F32)
        at = slot ^ (0, 2, 1, 3)[j]
        for i in range(3):
            where = i * (total.shape[1] // 3) + (shard * SPLIT + at) * part
            cols = pl.ds(pl.multiple_of(where, part), part)
            stores.append(copies.start(wide.at[j, :, i * part : (i + 1) * part], total.at[:, cols]))
        each = raw.shape[2] - 3 * part
        for i in range(owned // part):
            source = wide.at[j, i * part : (i + 1) * part, 3 * part :]
            target = dense.at[span(at, part), i * each : (i + 1) * each]
            stores.append(copies.start(source, target))
    for copy in stores:
        copy.wait()


def other_kernel(*refs):
    own, ins, refs = refs[:4], refs[4:8], refs[9:]
    total, qkv_o, in_o, out_o, dense_o, g1, b1, g2, b2, raw, wide, edge, flat, joint, in_b, sems = refs
    shard, slot, _ = place_of()
    owned = total.shape[0]
    width = total.shape[1] // 3
    part = raw.shape[2] // 3
    hidden = in_o.shape[0] // SPLIT
    copies = Copies(sems)
    edges = [copies.start(ref.at[owned:, 0 : 3 * part], edge.at[j]) for j, ref in enumerate(own)]
    loads = [copies.start(ref, raw.at[j]) for j, ref in enumerate(ins)]
    stores = []
    for j in range(4):
        loads[j].wait()
        wide[j] = raw[j].astype(F32)
        at = slot ^ (0, 2, 1, 3)[j]
        for i in range(3):
            where = i * width + ((1 - shard) * SPLIT + at) * part
            cols = pl.ds(pl.multiple_of(where, part), part)
            source = wide.at[j, 0:owned, i * part : (i + 1) * part]
            stores.append(copies.start(source, total.at[:, cols]))
    for copy in edges:
        copy.wait()
    mine = [edge[j].astype(F32) for j in range(4)]
    theirs = [wide[j, owned:, :] for j in range(4)]
    every = sum(mine) + sum(theirs)
    per = -(-width // (3 * part))
    for i, vectors in enumerate(((g1,), (b1,), (g2,), (b2,), (out_o, dense_o))):
        flat[...] = jnp.concatenate([every[i * per + k : i * per + k + 1] for k in range(per)], axis=1)[:, 0:width]
        for ref in vectors:
            ref[...] = flat[:, span(shard, owned)].reshape(owned)
    row = 5 * per
    long = -(-hidden // (3 * part))
    for j in range(4):
        at = slot ^ (0, 2, 1, 3)[j]
        sums = jnp.concatenate([mine[j][row + k : row + k + 1] for k in range(long)], axis=1)
        in_b[:, span(at, hidden)] = sums[:, 0:hidden]
        for values, group in ((mine[j], shard), (theirs[j], 1 - shard)):
            for i in range(3):
                piece = values[row + long : row + long + 1, i * part : (i + 1) * part]
                joint[i : i + 1, span(group * SPLIT + at, part)] = piece
    thirds = [joint[i : i + 1, k * owned : (k + 1) * owned] for i in range(3) for k in range(2)]
    for i in range(3):
        third = jnp.where(shard == 0, thirds[i], thirds[3 + i])
        qkv_o[i * owned : (i + 1) * owned] = third.reshape(owned)
    in_o[...] = in_b[...].reshape(in_o.shape)
    for copy in stores:
        copy.wait()


def finish_kernel(length, tok, cot, own, got, params, result, grad_tokens):
    rows, width = tok.shape
    live = lax.broadcasted_iota(jnp.int32, (rows, width), 0) < length[0]
    values = tok[...].astype(F32)
    mixed = own[:, 0:width] + got[:, 0:width].astype(F32) + params[3:4, :] + params[4:5, :]
    result[...] = (values + jnp.where(live, mixed, 0.0)).astype(BF16)
    centre = values - jnp.mean(values, axis=-1, keepdims=True)
    root = lax.rsqrt(jnp.mean(centre * centre, axis=-1, keepdims=True) + 1e-05)
    hat = centre * root
    inner = own[:, width:] + got[:, width:].astype(F32)
    inner = inner - jnp.mean(inner, axis=-1, keepdims=True) - hat * jnp.mean(inner * hat, axis=-1, keepdims=True)
    grad_tokens[...] = (cot[...].astype(F32) + inner * root).astype(BF16)


def turn_tables(seq_rows, columns):
    half = ROT // 2
    inverse = np.float32(10000.0) ** (-(2.0 * np.arange(half, dtype=np.float32)) / np.float32(ROT))
    angles = np.arange(seq_rows, dtype=np.float32)[:, None] * inverse.astype(np.float32)[None, :]
    cosine = np.ones((seq_rows, HEAD_DIM), np.float32)
    low = np.zeros((seq_rows, HEAD_DIM), np.float32)
    high = np.zeros((seq_rows, HEAD_DIM), np.float32)
    cosine[:, :half] = cosine[:, half:ROT] = np.cos(angles)
    low[:, :half] = -np.sin(angles)
    high[:, half:ROT] = np.sin(angles)
    return [jnp.asarray(np.tile(t, (1, columns // HEAD_DIM))) for t in (cosine, low, high)]


ORDER = (
    "far", "moa", "mob", "coa", "mia", "fold", "poa", "mib", "xoa", "cob",
    "tjb", "cia", "pob", "xob", "keep", "soa", "cib", "mja", "pia", "xia",
    "mjb", "pib", "loa", "sob", "sia", "cja", "xib", "lob", "cjb", "pja",
    "sib", "xja", "lia", "pjb", "lib", "sja", "xjb", "end", "sjb", "lja",
)


def make_pairs(mesh):
    reps = mesh.shape["rep"]

    def swap_rep(values, bit):
        return lax.ppermute(values, "rep", [(i, i ^ bit) for i in range(reps)])

    def swap_shard(values):
        return lax.ppermute(values, "shard", [(0, 1), (1, 0)])

    def line_permute(values, pairs):
        pairs = [(a * SPLIT + i, b * SPLIT + i) for a, b in pairs for i in range(SPLIT)]
        return lax.ppermute(values, "rep", pairs)

    def after(value, other):
        return lax.optimization_barrier((value, other))[0]

    def on_device(
        tokens, cotangent, lengths, qkv_weight, qkv_bias, dense_weight, dense_bias, in_weight,
        in_bias, out_weight, out_bias, norm1_gain, norm1_bias, norm2_gain, norm2_bias,
    ):
        seq_rows, width = tokens.shape
        owned = width // 2
        hidden = in_weight.shape[1]
        part_f, part_h = hidden // GROUP, width // GROUP
        rows = GROUP * seq_rows
        halves = [qkv_bias, dense_bias, out_bias, norm1_gain, norm1_bias, norm2_gain, norm2_bias]
        packed, branch_sum, in_b, in_give, qkv_give = call(
            pack_kernel,
            "pack",
            [(lengths, SCALAR)]
            + [(a, ANY) for a in [tokens, cotangent, in_bias, *halves, in_weight, qkv_weight]],
            [
                (shaped((2 * seq_rows + TAIL, width)), WHOLE),
                (shaped((1, width), F32), WHOLE),
                (shaped((1, part_f), F32), WHOLE),
                (shaped((owned, part_f)), WHOLE),
                (shaped((owned, 3 * part_h)), WHOLE),
            ],
            [pltpu.VMEM((seq_rows, width), BF16)] * 2
            + [pltpu.VMEM(v.shape, BF16) for v in [in_bias, *halves]]
            + [pltpu.SemaphoreType.DMA((14,))],
        )
        beside = swap_rep(packed, 2)
        across = swap_shard(packed)
        beyond = swap_rep(after(across, beside), 2)
        in_got = swap_shard(in_give)
        qkv_got = swap_shard(qkv_give)
        pieces = [packed, across, beside, after(beyond, in_got)]
        pieces += [swap_rep(v, 1) for v in pieces]

        normed, xhat, active, grad_before, branch, out_all, in_mine, in_theirs, params, lens, in_sum = call(
            hidden_kernel,
            "hidden",
            [(p, FREE) for p in pieces]
            + [(in_weight, ANY), (in_got, FREE), (out_weight, ANY), (in_b, WHOLE)],
            [
                (shaped((rows, width)), ANY),
                (shaped((rows, width)), ANY),
                (shaped((rows, part_f)), ANY),
                (shaped((rows, part_f)), ANY),
                (shaped((rows, width)), ANY),
                (shaped((part_f, width)), ANY),
                (shaped((owned, part_f)), ANY),
                (shaped((owned, part_f)), ANY),
                (shaped((TAIL, width), F32), WHOLE),
                (shaped((GROUP * 8, 128), F32), WHOLE),
                (shaped((1, part_f), F32), WHOLE),
            ],
            [
                pltpu.VMEM((rows, width), BF16),
                pltpu.VMEM((rows, width), BF16),
                pltpu.VMEM((GROUP, TAIL, width), BF16),
                pltpu.VMEM((width, part_f), BF16),
                pltpu.VMEM((part_f, width), BF16),
                pltpu.VMEM((rows, width), BF16),
                pltpu.VMEM((rows, width), BF16),
                pltpu.VMEM((rows, width), BF16),
                pltpu.VMEM((rows, part_f), BF16),
                pltpu.VMEM((rows, part_f), F32),
                pltpu.VMEM((rows, part_f), BF16),
                pltpu.VMEM((part_f, width), BF16),
                pltpu.VMEM((owned, part_f), BF16),
                pltpu.VMEM((owned, part_f), BF16),
                pltpu.SemaphoreType.DMA((3 * GROUP + 3 + 9,)),
            ],
        )
        in_other = swap_shard(in_theirs)

        blocks = [normed, branch, active, grad_before, xhat, lens]
        whole = [qkv_weight, qkv_got, dense_weight, out_weight, in_weight, in_got, params]
        tables = turn_tables(seq_rows, part_h)
        sizes = (width, part_h, part_f)
        line = lax.axis_index("rep") // SPLIT
        inner_line = (line == 1) | (line == 2)
        last = [params]

        def then(value):
            return after(value, last[0])

        def did(value):
            last[0] = value
            return value

        def added(left, right):
            total = (left.astype(F32) + right.astype(F32)).astype(BF16)
            return did(lax.optimization_barrier(total))

        def meet(chunk):
            return added(then(chunk), line_permute(chunk, [(0, 1), (3, 2)]))

        def cross(near):
            return added(then(near), line_permute(near, [(1, 2), (2, 1)]))

        def spread(both):
            got = line_permute(both, [(1, 0), (2, 3)])
            return did(jnp.where(inner_line, then(both), got))

        half_f = (hidden // 2, width)
        wide = 3 * part_h
        here = lambda slot, shard: shard * SPLIT + slot
        there = lambda slot, shard: (1 - shard) * SPLIT + slot
        goes = {
            "oa": ("out", half_f, part_f // 2, lambda slot, shard: 2 * slot, 0),
            "ob": ("out", half_f, part_f // 2, lambda slot, shard: 2 * slot + 1, 0),
            "ia": ("in", (owned, hidden), part_f, here, 1),
            "ib": ("in", (owned, hidden), part_f, there, 1),
        }
        totals = {"out": None, "in": None}

        far, near, joint_a, joint_theirs = attention(
            blocks, whole, tables, [in_sum, branch_sum], seq_rows, sizes
        )
        did(joint_a)
        got = line_permute(out_all, [(0, 1), (3, 2)])
        got = after(got, in_other)
        half = part_f // 2
        state = {"oa": (out_all[:half], got[:half]), "ob": (out_all[half:], got[half:])}
        state |= {"ia": in_mine, "ib": in_other, "ja": joint_a}
        state["jb"] = swap_shard(joint_theirs)
        for token in ORDER:
            what, name = token[0], token[1:]
            held = state.get(name)
            if what == "t":
                state[name] = then(held)
            elif what == "m":
                state[name] = added(then(held[0]), held[1]) if name[0] == "o" else meet(held)
            elif what == "c":
                state[name] = cross(held)
            elif what == "p":
                state[name] = spread(held)
            elif what == "x":
                state[name] = [held, swap_rep(then(held), 2)]
            elif what == "s":
                state[name] = held + [swap_rep(then(v), 1) for v in held]
            elif what == "l" and name in goes:
                kind, *how = goes[name]
                totals[kind] = did(placed(totals[kind], [then(held[0])] + held[1:], *how))
            elif token == "lja":
                total_qkv, total_dense = call(
                    joint_kernel,
                    "place_joint",
                    [(then(held[0]), FREE)] + [(a, FREE) for a in held[1:]],
                    [(shaped((owned, 3 * width), F32), ANY), (shaped((owned, width), F32), ANY)],
                    [
                        pltpu.VMEM((4, owned, held[0].shape[1]), BF16),
                        pltpu.VMEM((4, owned, held[0].shape[1]), F32),
                        pltpu.SemaphoreType.DMA((4 * (4 + owned // part_h),)),
                    ],
                )
                did(total_dense)
            elif token == "far":
                far = swap_rep(then(far), 1)
            elif token == "fold":
                give = swap_rep(did(fold(then(near), far, 2 * seq_rows)), 2)
            elif token == "keep":
                keep, give = keep_sum(then(near), far, give)
                did(keep)
                give = swap_shard(give)
            elif token == "end":
                result, grad_tokens = call(
                    finish_kernel,
                    "finish",
                    [(then(lengths), SCALAR)]
                    + [(a, WHOLE) for a in (tokens, cotangent, keep, give, params)],
                    [(shaped((seq_rows, width)), WHOLE)] * 2,
                )
                did(result)
        total_out, total_in = totals["out"], totals["in"]
        joint_a, joint_b = state["ja"], state["jb"]
        sizes = [3 * owned, hidden // 2] + 6 * [owned]
        total_qkv, *vectors = pl.pallas_call(
            other_kernel,
            out_shape=[shaped(total_qkv.shape, F32)] + [shaped((n,), F32) for n in sizes],
            in_specs=[FREE] * 9,
            out_specs=[FREE] + [WHOLE] * 8,
            scratch_shapes=[
                pltpu.VMEM((4, owned + VECTORS, wide), BF16),
                pltpu.VMEM((4, owned + VECTORS, wide), F32),
                pltpu.VMEM((4, VECTORS, wide), BF16),
                pltpu.VMEM((1, width), F32),
                pltpu.VMEM((3, width), F32),
                pltpu.VMEM((1, hidden // 2), F32),
                pltpu.SemaphoreType.DMA((20,)),
            ],
            input_output_aliases={8: 0},
            compiler_params=pltpu.CompilerParams(vmem_limit_bytes=LIMIT // 3),
            cost_estimate=SMALL,
            name="place_other",
        )(*joint_a, *joint_b, total_qkv)
        qkv_b, in_b, out_b, dense_b, g1, b1, g2, b2 = vectors
        return (
            result, grad_tokens, total_qkv, qkv_b, total_dense, dense_b, total_in, in_b, total_out, out_b,
            g1, b1, g2, b2,
        )

    return on_device


def solution(mesh):
    rows = P(("rep", "shard"), None)
    vector = P("shard")
    matrix = P("shard", None)
    weights = (matrix, vector)
    in_specs = (rows, rows, P(("rep", "shard"))) + 4 * weights + 4 * (vector,)
    out_specs = (rows, rows) + 4 * weights + 4 * (vector,)
    paired = mesh.shape["shard"] == 2 and mesh.shape["rep"] == SPLIT * LINES
    body = make_pairs(mesh) if paired else make(mesh)
    return jax.shard_map(body, mesh=mesh, in_specs=in_specs, out_specs=out_specs, check_vma=False)
```

```python
import jax
import jax.numpy as jnp
import numpy as np
from jax import lax
from jax.experimental import pallas as pl
from jax.experimental.pallas import tpu as pltpu
from jax.sharding import PartitionSpec as P

HEAD_DIM = 64
ROT = 16
F32 = jnp.float32
BF16 = jnp.bfloat16
EXTRA = 16


def rotary(values, turn):
    seq_rows = values.shape[-2]
    half = ROT // 2
    inverse = 10000.0 ** (-(2.0 * jnp.arange(half).astype(F32)) / ROT)
    angles = jnp.arange(seq_rows).astype(F32)[:, None] * inverse[None, :]
    cosine = jnp.cos(angles)
    sine = jnp.sin(angles) * turn
    first = values[..., :half]
    second = values[..., half:ROT]
    return jnp.concatenate(
        [first * cosine - second * sine, second * cosine + first * sine, values[..., ROT:]],
        axis=-1,
    )


def dot(left, right):
    return jnp.dot(left, right, preferred_element_type=F32)


def dot_nt(left, right):
    return lax.dot_general(left, right, (((1,), (1,)), ((), ())), preferred_element_type=F32)


def dot_tn(left, right):
    return lax.dot_general(left, right, (((0,), (0,)), ((), ())), preferred_element_type=F32)


def plan(mesh_shape, heads):
    shards, reps = mesh_shape["shard"], mesh_shape["rep"]
    split = 1
    while split < 4 and reps % (2 * split) == 0 and heads % (2 * split * shards) == 0:
        split *= 2
    return shards, reps, split


def make(mesh):
    def on_device(
        tokens,
        cotangent,
        lengths,
        qkv_weight,
        qkv_bias,
        dense_weight,
        dense_bias,
        in_weight,
        in_bias,
        out_weight,
        out_bias,
        norm1_gain,
        norm1_bias,
        norm2_gain,
        norm2_bias,
    ):
        seq_rows, width = tokens.shape
        heads = width // HEAD_DIM
        shards, reps, split = plan(dict(mesh.shape), heads)
        lines = reps // split
        group = shards * split
        owned = width // shards
        hidden = in_weight.shape[1]
        part_f = hidden // group
        part_h = width // group
        own_heads = part_h // HEAD_DIM
        shard = lax.axis_index("shard")
        rep = lax.axis_index("rep")
        slot = lax.rem(rep, split)
        line = rep // split
        block = shard * split + slot
        bits = []
        bit = split // 2
        while bit:
            bits.append(bit)
            bit //= 2

        def swap_rep(values, bit):
            return lax.ppermute(values, "rep", [(i, i ^ bit) for i in range(reps)])

        def swap_shard(values):
            return lax.ppermute(values, "shard", [(0, 1), (1, 0)])

        def gather_shard(values):
            if shards == 1:
                return values
            if shards == 2:
                return jnp.concatenate([values, swap_shard(values)], axis=0)
            return lax.all_gather(values, "shard", axis=0, tiled=True)

        def gather_rep(values):
            for bit in bits:
                values = jnp.concatenate([values, swap_rep(values, bit)], axis=0)
            return values

        def scatter_sum(values):
            for bit in reversed(bits):
                half = values.shape[0] // 2
                values = values[:half] + swap_rep(values[half:].astype(BF16), bit).astype(F32)
            if shards == 2:
                half = values.shape[0] // 2
                values = values[:half] + swap_shard(values[half:].astype(BF16)).astype(F32)
            elif shards > 2:
                values = lax.psum_scatter(
                    values.astype(BF16), "shard", scatter_dimension=0, tiled=True
                ).astype(F32)
            return values

        def ordered(mine, other, flag, axis):
            first = jnp.where(flag, other, mine)
            second = jnp.where(flag, mine, other)
            return jnp.concatenate([first, second], axis=axis)

        def columns_of(weight, parts, size):
            rows = weight.shape[0]
            cut = weight.reshape(rows, parts, group, size)

            def piece(at):
                return lax.dynamic_slice_in_dim(cut, at, 1, 2).reshape(rows, parts * size)

            if shards == 1:
                return piece(block)
            if shards == 2:
                other = swap_shard(piece((1 - shard) * split + slot))
                return ordered(piece(block), other, shard == 1, 0)
            picked = jnp.stack([piece(s * split + slot) for s in range(shards)], axis=0)
            return lax.all_to_all(picked, "shard", 0, 0, tiled=True).reshape(
                rows * shards, parts * size
            )

        def rows_exchange(grad):
            if shards == 1:
                return [grad]
            if shards == 2:
                mine = lax.dynamic_slice_in_dim(grad, shard * owned, owned, 0)
                other = swap_shard(lax.dynamic_slice_in_dim(grad, (1 - shard) * owned, owned, 0))
                return [jnp.where(shard == 1, other, mine), jnp.where(shard == 1, mine, other)]
            got = lax.all_to_all(grad, "shard", 0, 0, tiled=True)
            return [got[s * owned : (s + 1) * owned] for s in range(shards)]

        length = lengths[0]
        live = (jnp.arange(seq_rows) < length).astype(F32)[:, None]
        branch = (live * cotangent.astype(F32)).astype(BF16)
        halves = [dense_bias, out_bias, norm1_gain, norm1_bias, norm2_gain, norm2_bias]
        params = jnp.concatenate([qkv_bias] + halves)
        params = jnp.pad(params, (0, 8 * width - params.shape[0])).reshape(8, width)
        length_rows = jnp.broadcast_to(length.astype(BF16), (EXTRA - 8, width))
        packed = jnp.concatenate([tokens, params, length_rows], axis=0)
        packed = gather_shard(packed)
        branch_all = gather_shard(branch)
        in_w = columns_of(in_weight, 1, part_f)
        packed_all = gather_rep(packed).reshape(group, seq_rows + EXTRA, width)
        branch_all = gather_rep(branch_all)
        qkv_w = columns_of(qkv_weight, 3, part_h)

        by_shard = packed.reshape(shards, seq_rows + EXTRA, width)[:, seq_rows : seq_rows + 8]
        by_shard = by_shard.reshape(shards, 8 * width)
        if shards == 2:
            by_shard = jnp.where(shard == 1, by_shard[::-1], by_shard)

        def whole(at, size):
            return by_shard[:, at : at + size].reshape(shards * size).astype(F32)

        qkv_b = whole(0, 3 * owned)
        at = 3 * owned
        full = []
        for _ in halves:
            full.append(whole(at, owned))
            at += owned
        dense_b, out_b, gain_one, shift_one, gain_two, shift_two = full
        all_lengths = packed_all[:, seq_rows + 8, 0].astype(jnp.int32)
        rows = group * seq_rows
        values = packed_all[:, :seq_rows].reshape(rows, width).astype(F32)

        centre = values - jnp.mean(values, axis=-1, keepdims=True)
        spread = jnp.mean(centre * centre, axis=-1, keepdims=True)
        root = lax.rsqrt(spread + 1e-05)
        xhat = centre * root
        normed = (xhat * gain_one + shift_one).astype(BF16)
        normed_two = (xhat * gain_two + shift_two).astype(BF16)

        out_w = lax.dynamic_slice_in_dim(out_weight, slot * part_f, part_f, 0)
        in_b = lax.dynamic_slice_in_dim(in_bias, slot * part_f, part_f, 0).astype(F32)
        before = dot(normed_two, in_w) + in_b
        cdf = 0.5 * (1.0 + lax.erf(before * (0.5**0.5)))
        active = (before * cdf).astype(BF16)
        slope = cdf + before * jnp.exp(-0.5 * before * before) * 0.3989422804014327
        grad_before = (dot_nt(branch_all, out_w) * slope).astype(BF16)
        grad_out_w = dot_tn(active, branch_all).astype(BF16)
        grad_in_w = dot_tn(normed_two, grad_before).astype(BF16)
        grad_two = dot_nt(grad_before, in_w)

        scaling = HEAD_DIM ** (-0.5)
        bias = lax.dynamic_slice_in_dim(qkv_b.reshape(3, group, part_h), block, 1, 1)
        joint = dot(normed, qkv_w) + bias.reshape(3 * part_h)
        split_joint = joint.reshape(group, seq_rows, 3, own_heads, HEAD_DIM).transpose(2, 0, 3, 1, 4)
        query = rotary(split_joint[0], 1.0).astype(BF16)
        keys = rotary(split_joint[1], 1.0).astype(BF16)
        vals = split_joint[2].astype(BF16)
        position = jnp.arange(seq_rows)
        allowed = (position[None, :] <= position[:, None])[None] & (
            position[None, None, :] < all_lengths[:, None, None]
        )
        scores = jnp.einsum("bhpd,bhqd->bhpq", query, keys, preferred_element_type=F32) * scaling
        scores = jnp.where(allowed[:, None], scores, -1e30)
        raised = jnp.exp(scores - jnp.max(scores, axis=-1, keepdims=True))
        exact = raised / jnp.sum(raised, axis=-1, keepdims=True)
        probs = exact.astype(BF16)
        context = jnp.einsum("bhpq,bhqd->bhpd", probs, vals, preferred_element_type=F32)
        context = context.astype(BF16).transpose(0, 2, 1, 3).reshape(rows, part_h)
        dense_w = lax.dynamic_slice_in_dim(dense_weight, slot * part_h, part_h, 0)
        mixed = scatter_sum(dot(active, out_w) + dot(context, dense_w))
        result = (tokens.astype(F32) + live * (mixed + dense_b + out_b)).astype(BF16)

        grad_context = dot_nt(branch_all, dense_w).astype(BF16)
        grad_dense_w = dot_tn(context, branch_all).astype(BF16)
        grad_context = grad_context.reshape(group, seq_rows, own_heads, HEAD_DIM).transpose(0, 2, 1, 3)
        grad_probs = jnp.einsum(
            "bhpd,bhqd->bhpq", grad_context, vals, preferred_element_type=F32
        )
        grad_vals = jnp.einsum("bhpq,bhpd->bhqd", probs, grad_context, preferred_element_type=F32)
        grad_scores = (
            exact * (grad_probs - jnp.sum(grad_probs * exact, axis=-1, keepdims=True))
        ).astype(BF16)
        grad_query = jnp.einsum("bhpq,bhqd->bhpd", grad_scores, keys, preferred_element_type=F32)
        grad_keys = jnp.einsum("bhpq,bhpd->bhqd", grad_scores, query, preferred_element_type=F32)
        grad_joint = jnp.stack(
            [rotary(grad_query * scaling, -1.0), rotary(grad_keys * scaling, -1.0), grad_vals]
        ).astype(BF16)
        grad_joint = grad_joint.transpose(1, 3, 0, 2, 4).reshape(rows, 3 * part_h)
        grad_qkv_w = dot_tn(normed, grad_joint).astype(BF16)
        grad_one = dot_nt(grad_joint, qkv_w)

        inner = scatter_sum(grad_one * gain_one + grad_two * gain_two)
        own_xhat = xhat[:seq_rows] if shards <= 2 else None
        if own_xhat is None:
            own_xhat = lax.dynamic_slice_in_dim(xhat, shard * seq_rows, seq_rows, 0)
            own_root = lax.dynamic_slice_in_dim(root, shard * seq_rows, seq_rows, 0)
        else:
            own_root = root[:seq_rows]
        inner = (
            inner
            - jnp.mean(inner, axis=-1, keepdims=True)
            - own_xhat * jnp.mean(inner * own_xhat, axis=-1, keepdims=True)
        ) * own_root
        grad_tokens = (cotangent.astype(F32) + inner).astype(BF16)

        in_sum = jnp.sum(grad_before.astype(F32), axis=0)
        qkv_sum = jnp.sum(grad_joint.astype(F32), axis=0).reshape(3, 1, part_h)
        vectors = jnp.concatenate(
            [
                jnp.sum(grad_one * xhat, axis=0),
                jnp.sum(grad_one, axis=0),
                jnp.sum(grad_two * xhat, axis=0),
                jnp.sum(grad_two, axis=0),
                jnp.sum(branch.astype(F32), axis=0),
                lax.dynamic_update_slice_in_dim(jnp.zeros((hidden,), F32), in_sum, block * part_f, 0),
                lax.dynamic_update_slice_in_dim(
                    jnp.zeros((3, group, part_h), F32), qkv_sum, block, 1
                ).reshape(3 * width),
            ]
        )
        vectors = lax.psum(vectors, ("rep", "shard"))

        def own_part(at, size):
            piece = size // shards
            return lax.dynamic_slice_in_dim(vectors, at + shard * piece, piece, 0)

        in_parts = rows_exchange(grad_in_w)
        qkv_parts = rows_exchange(grad_qkv_w)
        chunks = [grad_out_w] + in_parts + [grad_dense_w] + qkv_parts
        if lines == 4:
            inner_line = (line == 1) | (line == 2)

            def line_permute(values, pairs):
                return lax.ppermute(
                    values,
                    "rep",
                    [(a * split + i, b * split + i) for a, b in pairs for i in range(split)],
                )

            summed = []
            for chunk in chunks:
                got = line_permute(chunk, [(0, 1), (3, 2)])
                near = lax.optimization_barrier((chunk.astype(F32) + got.astype(F32)).astype(BF16))
                got = line_permute(near, [(1, 2), (2, 1)])
                both = lax.optimization_barrier((near.astype(F32) + got.astype(F32)).astype(BF16))
                got = line_permute(both, [(1, 0), (2, 3)])
                summed.append(jnp.where(inner_line, both, got))
        else:
            groups = [[a * split + i for a in range(lines)] for i in range(split)]
            summed = [lax.psum(c, "rep", axis_index_groups=groups) for c in chunks]

        def gather_slots(values):
            values = values[None]
            for bit in reversed(bits):
                values = ordered(values, swap_rep(values, bit), (slot & bit) != 0, 0)
            return values

        summed = [gather_slots(c) for c in summed]
        total_out = summed[0].reshape(split * part_f, width).astype(F32)
        total_in = jnp.stack(summed[1 : 1 + shards])
        total_in = total_in.transpose(2, 0, 1, 3).reshape(owned, hidden).astype(F32)
        total_dense = summed[1 + shards].reshape(split * part_h, width).astype(F32)
        total_qkv = jnp.stack(summed[2 + shards :]).reshape(shards, split, owned, 3, part_h)
        total_qkv = total_qkv.transpose(2, 3, 0, 1, 4).reshape(owned, 3 * width).astype(F32)
        at_in = 5 * width
        at_qkv = at_in + hidden
        out_sum = own_part(4 * width, width)
        return (
            result,
            grad_tokens,
            total_qkv,
            own_part(at_qkv, 3 * width),
            total_dense,
            out_sum,
            total_in,
            own_part(at_in, hidden),
            total_out,
            out_sum,
            own_part(0, width),
            own_part(width, width),
            own_part(2 * width, width),
            own_part(3 * width, width),
        )

    return on_device


GROUP = 8
SPLIT = 4
LINES = 4
TAIL = 16
VECTORS = 32
ANY = pl.BlockSpec(memory_space=pltpu.HBM)
FREE = pl.BlockSpec(memory_space=pl.ANY)
SCALAR = pl.BlockSpec(memory_space=pltpu.SMEM)
WHOLE = pl.BlockSpec(memory_space=pltpu.VMEM)
LIMIT = 63 * 2**20
COST = pl.CostEstimate(flops=10**12, bytes_accessed=10**9, transcendentals=0)
SMALL = pl.CostEstimate(flops=10**6, bytes_accessed=0, transcendentals=0)


def shaped(shape, dtype=BF16):
    return jax.ShapeDtypeStruct(shape, dtype)


def call(kernel, name, ins, outs, scratch=()):
    return pl.pallas_call(
        kernel,
        out_shape=[shape for shape, _ in outs],
        in_specs=[spec for _, spec in ins],
        out_specs=[spec for _, spec in outs],
        scratch_shapes=list(scratch),
        compiler_params=pltpu.CompilerParams(
            vmem_limit_bytes=LIMIT if name in ("pack", "hidden") else LIMIT // 3
        ),
        cost_estimate=COST if name == "hidden" else SMALL,
        name=name,
    )(*[array for array, _ in ins])


class Copies:
    def __init__(self, sems):
        self.sems, self.used = sems, 0

    def make(self, source, target):
        self.used += 1
        return pltpu.make_async_copy(source, target, self.sems.at[self.used - 1])

    def start(self, source, target):
        copy = self.make(source, target)
        copy.start()
        return copy


def place_of():
    shard = lax.axis_index("shard")
    slot = lax.rem(lax.axis_index("rep"), SPLIT)
    return shard, slot, shard * SPLIT + slot


def span(at, size):
    if isinstance(at, int):
        return pl.ds(at * size, size)
    return pl.ds(pl.multiple_of(at * size, size), size)


def pack_kernel(length, tok, cot, in_bias, qb, db, ob, g1, b1, g2, b2, in_weight, qkv_weight,
                packed, total, in_b, in_give, qkv_give, tok_v, cot_v, ib_v, qb_v, *rest):
    vecs, sems = rest[:-1], rest[-1]
    shard, slot, _ = place_of()
    twin = (1 - shard) * SPLIT + slot
    rows, width = tok_v.shape
    owned = vecs[0].shape[0]
    part_f, part_h = in_give.shape[1], qkv_give.shape[1] // 3
    copies = Copies(sems)
    first = [copies.start(tok, tok_v), copies.start(cot, cot_v), copies.start(in_bias, ib_v)]
    first.append(copies.start(qb, qb_v))
    first += [copies.start(a, b) for a, b in zip((db, ob, g1, b1, g2, b2), vecs)]
    given = [copies.start(in_weight.at[:, span(twin, part_f)], in_give)]
    for i in range(3):
        cols = pl.ds(pl.multiple_of(i * width + twin * part_h, part_h), part_h)
        target = qkv_give.at[:, i * part_h : (i + 1) * part_h]
        given.append(copies.start(qkv_weight.at[:, cols], target))
    for copy in first:
        copy.wait()
    live = lax.broadcasted_iota(jnp.int32, (rows, width), 0) < length[0]
    kept = jnp.where(live, cot_v[...].astype(F32), 0.0)
    packed[rows + TAIL :, :] = kept.astype(BF16)
    total[...] = jnp.sum(kept, axis=0, keepdims=True)
    packed[0:rows, :] = tok_v[...]
    whole = qb_v[...].astype(F32).reshape(1, 3 * owned)
    lines = [whole[:, i * owned : (i + 1) * owned] for i in range(3)]
    lines += [ref[...].astype(F32).reshape(1, owned) for ref in vecs]
    lines.append(jnp.full((TAIL - 9, owned), length[0].astype(F32)))
    packed[rows : rows + TAIL, 0:owned] = jnp.concatenate(lines, axis=0).astype(BF16)
    packed[rows : rows + TAIL, owned:width] = jnp.zeros((TAIL, width - owned), BF16)
    bias = ib_v[...].astype(F32).reshape(1, SPLIT * part_f)
    in_b[...] = sum(
        jnp.where(slot == i, bias[:, i * part_f : (i + 1) * part_f], 0.0) for i in range(SPLIT)
    )
    for copy in given:
        copy.wait()


def hidden_kernel(*refs):
    pieces, refs = refs[:GROUP], refs[GROUP:]
    (in_weight, in_got, out_weight, in_b, normed_o, xhat_o, active_o, grad_o, branch_o, out_o,
     own_o, other_o, params, lens, in_sum, every, branch, tails, w_full, out_w, normed, normed_two,
     xhat, active, slope, grad_before, grad_out, own, other, sems) = refs
    shard, slot, block = place_of()
    rows = pieces[0].shape[0] - TAIL >> 1
    owned, part = in_got.shape
    copies = Copies(sems)
    edge = [copies.start(p.at[rows : rows + TAIL, :], tails.at[i]) for i, p in enumerate(pieces)]
    first = [copies.start(p.at[0:rows, :], every.at[i * rows : (i + 1) * rows, :]) for i, p in enumerate(pieces)]
    first.append(copies.start(in_weight.at[:, span(block, part)], w_full.at[span(shard, owned), :]))
    first.append(copies.start(in_got, w_full.at[span(1 - shard, owned), :]))
    late = [copies.start(p.at[rows + TAIL :, :], branch.at[i * rows : (i + 1) * rows, :]) for i, p in enumerate(pieces)]
    late.append(copies.start(out_weight.at[span(slot, part), :], out_w))
    for copy in edge:
        copy.wait()
    params[:, span(shard, owned)] = tails[0, :, 0:owned].astype(F32)
    params[:, span(1 - shard, owned)] = tails[1, :, 0:owned].astype(F32)
    for i in range(GROUP):
        lens[i * 8 : (i + 1) * 8, :] = tails[i, :, 0:128].astype(F32)[8:]
    g1, b1, g2, b2 = (params[i : i + 1, :] for i in range(5, 9))
    for copy in first:
        copy.wait()
    step = 256

    def forward(i, carry):
        at = span(i, step)
        values = every[at, :].astype(F32)
        centre = values - jnp.mean(values, axis=-1, keepdims=True)
        spread = jnp.mean(centre * centre, axis=-1, keepdims=True)
        hat = centre * lax.rsqrt(spread + 1e-05)
        xhat[at, :] = hat.astype(BF16)
        normed[at, :] = (hat * g1 + b1).astype(BF16)
        two = (hat * g2 + b2).astype(BF16)
        normed_two[at, :] = two
        before = dot(two, w_full[...]) + in_b[...]
        cdf = 0.5 * (1.0 + lax.erf(before * (0.5**0.5)))
        active[at, :] = (before * cdf).astype(BF16)
        slope[at, :] = cdf + before * jnp.exp(-0.5 * before * before) * 0.3989422804014327
        return carry

    for i in range(GROUP * rows // step):
        forward(i, 0)
    done = [copies.start(normed, normed_o), copies.start(xhat, xhat_o), copies.start(active, active_o)]
    for copy in late:
        copy.wait()
    done.append(copies.start(branch, branch_o))

    def out_grad(j, carry):
        grad_out[span(j, step), :] = dot_tn(active[:, span(j, step)], branch[...]).astype(BF16)
        return carry

    lax.fori_loop(0, part // step, out_grad, 0)
    done.append(copies.start(grad_out, out_o))
    in_sum[...] = jnp.zeros_like(in_sum)

    def back(i, carry):
        at = span(i, step)
        grad = (dot_nt(branch[at, :], out_w[...]) * slope[at, :]).astype(BF16)
        grad_before[at, :] = grad
        in_sum[...] += jnp.sum(grad.astype(F32), axis=0, keepdims=True)
        return carry

    for i in range(GROUP * rows // step):
        back(i, 0)
    done.append(copies.start(grad_before, grad_o))
    for ref, target, where in ((other, other_o, 1 - shard), (own, own_o, shard)):

        def weight(j, carry, ref=ref, where=where):
            cols = span(where * (owned // step) + j, step)
            ref[span(j, step), :] = dot_tn(normed_two[:, cols], grad_before[...]).astype(BF16)
            return carry

        lax.fori_loop(0, owned // step, weight, 0)
        done.append(copies.start(ref, target))
    for copy in done:
        copy.wait()


def turn(values, tables, back):
    cosine, low, high = tables
    width = values.shape[1]
    ahead = pltpu.roll(values, width - ROT // 2, 1)
    behind = pltpu.roll(values, ROT // 2, 1)
    moved = ahead * low + behind * high
    return values * cosine - moved if back else values * cosine + moved


def attention_kernel(
    normed, branch, active, grad_before, xhat, lens, qkv_weight, qkv_got, dense_weight, out_weight,
    in_weight, in_got, params, cosine, low, high, in_sum, own_sum, far, near, mine_o, theirs_o,
    acc, dense, sums, jsum, vectors, w_full, dense_w, out_w, in_w, sems,
):
    shard, slot, block = place_of()
    rows, width = normed.shape
    part = dense_w.shape[0]
    owned, hidden = in_got.shape
    step = pl.program_id(0)

    copies = Copies(sems)
    mine, theirs = span(shard, owned), span(1 - shard, owned)
    early = [copies.make(qkv_got, w_full.at[theirs, :])]
    for i in range(3):
        cols = pl.ds(pl.multiple_of(i * width + block * part, part), part)
        target = w_full.at[mine, i * part : (i + 1) * part]
        early.append(copies.make(qkv_weight.at[:, cols], target))
    early.append(copies.make(dense_weight.at[span(slot, part), :], dense_w))
    late = [copies.make(out_weight.at[span(slot, hidden), :], out_w)]
    late.append(copies.make(in_weight.at[:, span(block, hidden)], in_w.at[mine, :]))
    late.append(copies.make(in_got, in_w.at[theirs, :]))

    @pl.when(step == 0)
    def _():
        for copy in early + late:
            copy.start()
        for ref in (acc, dense, sums, jsum):
            ref[...] = jnp.zeros_like(ref)
        for copy in early:
            copy.wait()

    scaling = HEAD_DIM**-0.5
    biases = []
    for i in range(3):
        at = i * width + block * part
        inside = lax.rem(at, 3 * owned)
        col = at // (3 * owned) * owned + lax.rem(inside, owned)
        cols = pl.ds(pl.multiple_of(col, part), part)
        biases.append(
            sum(jnp.where(inside // owned == r, params[r : r + 1, cols], 0.0) for r in range(3))
        )
    joint = dot(normed[...], w_full[...]) + jnp.concatenate(biases, axis=1)
    grad_context = dot_nt(branch[...], dense_w[...]).astype(BF16)
    seq = cosine.shape[0]
    tables = (cosine[...], low[...], high[...])
    at_p = lax.broadcasted_iota(jnp.int32, (seq, seq), 0)
    at_q = lax.broadcasted_iota(jnp.int32, (seq, seq), 1)
    head_of = lax.broadcasted_iota(jnp.int32, (seq, part), 1) // HEAD_DIM

    def apart(values):
        zero = jnp.zeros_like(values)
        return jnp.concatenate(
            [jnp.where(head_of == h, values, zero) for h in range(part // HEAD_DIM)], axis=0
        )

    def together(values):
        total = values[0:seq]
        for h in range(1, part // HEAD_DIM):
            total = jnp.where(head_of == h, values[h * seq : (h + 1) * seq], total)
        return total

    contexts, grads = [], []
    for one in range(rows // seq):
        at = slice(one * seq, (one + 1) * seq)
        query = turn(joint[at, 0:part], tables, False).astype(BF16)
        keys = turn(joint[at, part : 2 * part], tables, False).astype(BF16)
        vals = joint[at, 2 * part :].astype(BF16)
        allowed = (at_q <= at_p) & (at_q.astype(F32) < lens[8 * one + 7 : 8 * one + 8, :])
        gc = grad_context[at, :]
        keys_apart, vals_apart = apart(keys), apart(vals)
        scores = dot_nt(query, keys_apart) * scaling
        heads = range(part // HEAD_DIM)
        exact = []
        for head in heads:
            masked = jnp.where(allowed, scores[:, head * seq : (head + 1) * seq], -1e30)
            raised = jnp.exp(masked - jnp.max(masked, axis=-1, keepdims=True))
            exact.append(raised / jnp.sum(raised, axis=-1, keepdims=True))
        probs = jnp.concatenate(exact, axis=1).astype(BF16)
        contexts.append(dot(probs, vals_apart).astype(BF16))
        grad_probs = dot_nt(gc, vals_apart)
        grad_vals = together(dot_tn(probs, gc))
        grad_scores = []
        for head in heads:
            grad = grad_probs[:, head * seq : (head + 1) * seq]
            mean = jnp.sum(grad * exact[head], axis=-1, keepdims=True)
            grad_scores.append((exact[head] * (grad - mean)).astype(BF16))
        grad_scores = jnp.concatenate(grad_scores, axis=1)
        grad_query = turn(dot(grad_scores, keys_apart) * scaling, tables, True)
        grad_keys = turn(together(dot_tn(grad_scores, query)) * scaling, tables, True)
        grads.append(jnp.concatenate([grad_query, grad_keys, grad_vals], axis=1).astype(BF16))
    ctx = jnp.concatenate(contexts, axis=0)
    grad = jnp.concatenate(grads, axis=0)
    jsum[...] += jnp.sum(grad.astype(F32), axis=0, keepdims=True)
    acc[...] += dot_tn(normed[...], grad)
    dense[...] += dot_tn(ctx, branch[...])

    @pl.when(step == 0)
    def _():
        for copy in late:
            copy.wait()

    mixed = (dot(active[...], out_w[...]) + dot(ctx, dense_w[...])).astype(BF16)
    hat = xhat[...].astype(F32)
    one = dot_nt(grad, w_full[...])
    sums[0:1, :] += jnp.sum(one * hat, axis=0, keepdims=True)
    sums[1:2, :] += jnp.sum(one, axis=0, keepdims=True)
    two = dot_nt(grad_before[...], in_w[...])
    sums[2:3, :] += jnp.sum(two * hat, axis=0, keepdims=True)
    sums[3:4, :] += jnp.sum(two, axis=0, keepdims=True)
    inner = (one * params[5:6, :] + two * params[7:8, :]).astype(BF16)
    for ref, here in ((far, step < 2), (near, step >= 2)):

        @pl.when(here)
        def _(ref=ref):
            ref[:, 0:width] = mixed
            ref[:, width:] = inner

    @pl.when(step == pl.num_programs(0) - 1)
    def _():
        wide = 3 * part
        vectors[...] = jnp.zeros_like(vectors)
        row = 0
        for source in [sums[i : i + 1, :] for i in range(4)] + [own_sum[...], in_sum[...], jsum[...]]:
            for at in range(0, source.shape[1], wide):
                piece = source[:, at : at + wide]
                vectors[row : row + 1, 0 : piece.shape[1]] = piece
                row += 1
        for ref, which in ((mine_o, shard), (theirs_o, 1 - shard)):
            ref[0:owned, 0:wide] = acc[span(which, owned), :].astype(BF16)
            ref[owned:, 0:wide] = vectors[...].astype(BF16)
        each = width * part // owned
        for i in range(owned // part):
            cols = slice(i * each, (i + 1) * each)
            mine_o[i * part : (i + 1) * part, wide:] = dense[:, cols].astype(BF16)
        mine_o[owned:, wide:] = jnp.zeros((VECTORS, each), BF16)


def attention(blocks, whole, tables, small, seq_rows, sizes):
    width, part, hidden = sizes
    rows, steps = 2 * seq_rows, 4
    owned, wide = width // 2, 3 * part

    def block(array, height):
        return pl.BlockSpec((height, array.shape[1]), lambda i: ((i + 2) % 4, 0))

    def full(shape):
        return pl.BlockSpec(shape, lambda i: (0, 0))

    outer = pl.BlockSpec((rows, 2 * width), lambda i: (jnp.minimum(i, 1), 0))
    inner = pl.BlockSpec((rows, 2 * width), lambda i: (jnp.maximum(i - 2, 0), 0))
    mine = (owned + VECTORS, wide + width * part // owned)
    theirs = (owned + VECTORS, wide)
    half = shaped((2 * rows, 2 * width))
    args = [*blocks, *whole, *tables, *small]
    specs = [block(a, h) for a, h in zip(blocks, [rows] * 5 + [16])]
    specs += [ANY, FREE, ANY, ANY, ANY, FREE] + [full(a.shape) for a in [whole[6], *tables, *small]]
    sums = [(width, wide), (part, width), (8, width), (1, wide), (VECTORS, wide)]
    weights = [(width, wide), (part, width), (hidden, width), (width, hidden)]
    return pl.pallas_call(
        attention_kernel,
        grid=(steps,),
        out_shape=[half, half, shaped(mine), shaped(theirs)],
        in_specs=specs,
        out_specs=[outer, inner, full(mine), full(theirs)],
        scratch_shapes=[pltpu.VMEM(s, F32) for s in sums]
        + [pltpu.VMEM(s, BF16) for s in weights]
        + [pltpu.SemaphoreType.DMA((8,))],
        compiler_params=pltpu.CompilerParams(vmem_limit_bytes=LIMIT),
        cost_estimate=COST,
        name="attention",
    )(*args)


def placed(held, pieces, shape, size, where, parts=1):
    count = len(pieces)
    per = shape[1] // max(parts, 1)
    height = pieces[0].shape[0] if parts else size
    held_shape = (count, height, pieces[0].shape[1])

    def kernel(*refs):
        ins, (out, raw, wide, sems) = refs[:count], refs[-4:]
        shard, slot, _ = place_of()
        copies = Copies(sems)
        loads = [copies.start(ref.at[0:height, :], raw.at[j]) for j, ref in enumerate(ins)]
        stores = []
        for j in range(count):
            loads[j].wait()
            wide[j] = raw[j].astype(F32)
            at = where(slot ^ (0, 2, 1, 3)[j], shard)
            if parts == 0:
                stores.append(copies.start(wide.at[j], out.at[span(at, size), :]))
            for i in range(parts):
                cols = pl.ds(pl.multiple_of(i * per + at * size, size), size)
                source = wide.at[j, :, i * size : (i + 1) * size]
                stores.append(copies.start(source, out.at[:, cols]))
        for copy in stores:
            copy.wait()

    args = list(pieces) + ([] if held is None else [held])
    return pl.pallas_call(
        kernel,
        in_specs=[pl.BlockSpec(memory_space=pl.ANY)] * len(args),
        out_specs=pl.BlockSpec(memory_space=pl.ANY),
        out_shape=shaped(shape, F32),
        scratch_shapes=[
            pltpu.VMEM(held_shape, BF16),
            pltpu.VMEM(held_shape, F32),
            pltpu.SemaphoreType.DMA((count * (1 + max(parts, 1)),)),
        ],
        input_output_aliases={} if held is None else {count: 0},
        compiler_params=pltpu.CompilerParams(vmem_limit_bytes=LIMIT // 2),
        cost_estimate=SMALL,
        name="place",
    )(*args)


def fold(left, right, rows=None, name="fold"):
    count = rows or left.shape[0]
    shape = (count, left.shape[1])

    def kernel(a, b, out, a_v, b_v, sems):
        copies = Copies(sems)
        first = copies.start(a.at[a.shape[0] - count :, :], a_v)
        second = copies.start(b.at[b.shape[0] - count :, :], b_v)
        first.wait()
        second.wait()
        a_v[...] = (a_v[...].astype(F32) + b_v[...].astype(F32)).astype(BF16)
        copies.start(a_v, out).wait()

    scratch = [pltpu.VMEM(shape, BF16)] * 2 + [pltpu.SemaphoreType.DMA((3,))]
    return call(kernel, name, [(left, FREE), (right, FREE)], [(shaped(shape), FREE)], scratch)[0]


def keep_sum(near, far, got):
    count, width = got.shape[0] // 2, got.shape[1]

    def kernel(a, b, c, own, give, a_v, b_v, c_v, o_v, sems):
        copies = Copies(sems)
        loads = [copies.start(r.at[0 : 2 * count, :], v) for r, v in ((a, a_v), (b, b_v), (c, c_v))]
        for copy in loads:
            copy.wait()
        total = a_v[...].astype(F32) + b_v[...].astype(F32) + c_v[...].astype(F32)
        o_v[...] = total[0:count, :]
        a_v[0:count, :] = total[count:, :].astype(BF16)
        stores = [copies.start(o_v, own), copies.start(a_v.at[0:count, :], give)]
        for copy in stores:
            copy.wait()

    scratch = [pltpu.VMEM((2 * count, width), BF16)] * 3 + [pltpu.VMEM((count, width), F32)]
    return call(
        kernel,
        "keep",
        [(near, FREE), (far, FREE), (got, FREE)],
        [(shaped((count, width), F32), ANY), (shaped((count, width)), ANY)],
        scratch + [pltpu.SemaphoreType.DMA((5,))],
    )


def joint_kernel(*refs):
    ins, (total, dense, raw, wide, sems) = refs[:4], refs[4:]
    shard, slot, _ = place_of()
    owned = total.shape[0]
    part = dense.shape[0] // SPLIT
    copies = Copies(sems)
    loads = [copies.start(ref.at[0:owned, :], raw.at[j]) for j, ref in enumerate(ins)]
    stores = []
    for j in range(4):
        loads[j].wait()
        wide[j] = raw[j].astype(F32)
        at = slot ^ (0, 2, 1, 3)[j]
        for i in range(3):
            where = i * (total.shape[1] // 3) + (shard * SPLIT + at) * part
            cols = pl.ds(pl.multiple_of(where, part), part)
            stores.append(copies.start(wide.at[j, :, i * part : (i + 1) * part], total.at[:, cols]))
        each = raw.shape[2] - 3 * part
        for i in range(owned // part):
            source = wide.at[j, i * part : (i + 1) * part, 3 * part :]
            target = dense.at[span(at, part), i * each : (i + 1) * each]
            stores.append(copies.start(source, target))
    for copy in stores:
        copy.wait()


def other_kernel(*refs):
    own, ins, refs = refs[:4], refs[4:8], refs[9:]
    total, qkv_o, in_o, out_o, dense_o, g1, b1, g2, b2, raw, wide, edge, flat, joint, in_b, sems = refs
    shard, slot, _ = place_of()
    owned = total.shape[0]
    width = total.shape[1] // 3
    part = raw.shape[2] // 3
    hidden = in_o.shape[0] // SPLIT
    copies = Copies(sems)
    edges = [copies.start(ref.at[owned:, 0 : 3 * part], edge.at[j]) for j, ref in enumerate(own)]
    loads = [copies.start(ref, raw.at[j]) for j, ref in enumerate(ins)]
    stores = []
    for j in range(4):
        loads[j].wait()
        wide[j] = raw[j].astype(F32)
        at = slot ^ (0, 2, 1, 3)[j]
        for i in range(3):
            where = i * width + ((1 - shard) * SPLIT + at) * part
            cols = pl.ds(pl.multiple_of(where, part), part)
            source = wide.at[j, 0:owned, i * part : (i + 1) * part]
            stores.append(copies.start(source, total.at[:, cols]))
    for copy in edges:
        copy.wait()
    mine = [edge[j].astype(F32) for j in range(4)]
    theirs = [wide[j, owned:, :] for j in range(4)]
    every = sum(mine) + sum(theirs)
    per = -(-width // (3 * part))
    for i, vectors in enumerate(((g1,), (b1,), (g2,), (b2,), (out_o, dense_o))):
        flat[...] = jnp.concatenate([every[i * per + k : i * per + k + 1] for k in range(per)], axis=1)[:, 0:width]
        for ref in vectors:
            ref[...] = flat[:, span(shard, owned)].reshape(owned)
    row = 5 * per
    long = -(-hidden // (3 * part))
    for j in range(4):
        at = slot ^ (0, 2, 1, 3)[j]
        sums = jnp.concatenate([mine[j][row + k : row + k + 1] for k in range(long)], axis=1)
        in_b[:, span(at, hidden)] = sums[:, 0:hidden]
        for values, group in ((mine[j], shard), (theirs[j], 1 - shard)):
            for i in range(3):
                piece = values[row + long : row + long + 1, i * part : (i + 1) * part]
                joint[i : i + 1, span(group * SPLIT + at, part)] = piece
    thirds = [joint[i : i + 1, k * owned : (k + 1) * owned] for i in range(3) for k in range(2)]
    for i in range(3):
        third = jnp.where(shard == 0, thirds[i], thirds[3 + i])
        qkv_o[i * owned : (i + 1) * owned] = third.reshape(owned)
    in_o[...] = in_b[...].reshape(in_o.shape)
    for copy in stores:
        copy.wait()


def finish_kernel(length, tok, cot, own, got, params, result, grad_tokens):
    rows, width = tok.shape
    live = lax.broadcasted_iota(jnp.int32, (rows, width), 0) < length[0]
    values = tok[...].astype(F32)
    mixed = own[:, 0:width] + got[:, 0:width].astype(F32) + params[3:4, :] + params[4:5, :]
    result[...] = (values + jnp.where(live, mixed, 0.0)).astype(BF16)
    centre = values - jnp.mean(values, axis=-1, keepdims=True)
    root = lax.rsqrt(jnp.mean(centre * centre, axis=-1, keepdims=True) + 1e-05)
    hat = centre * root
    inner = own[:, width:] + got[:, width:].astype(F32)
    inner = inner - jnp.mean(inner, axis=-1, keepdims=True) - hat * jnp.mean(inner * hat, axis=-1, keepdims=True)
    grad_tokens[...] = (cot[...].astype(F32) + inner * root).astype(BF16)


def turn_tables(seq_rows, columns):
    half = ROT // 2
    inverse = np.float32(10000.0) ** (-(2.0 * np.arange(half, dtype=np.float32)) / np.float32(ROT))
    angles = np.arange(seq_rows, dtype=np.float32)[:, None] * inverse.astype(np.float32)[None, :]
    cosine = np.ones((seq_rows, HEAD_DIM), np.float32)
    low = np.zeros((seq_rows, HEAD_DIM), np.float32)
    high = np.zeros((seq_rows, HEAD_DIM), np.float32)
    cosine[:, :half] = cosine[:, half:ROT] = np.cos(angles)
    low[:, :half] = -np.sin(angles)
    high[:, half:ROT] = np.sin(angles)
    return [jnp.asarray(np.tile(t, (1, columns // HEAD_DIM))) for t in (cosine, low, high)]


ORDER = (
    "far", "moa", "mob", "coa", "mia", "fold", "poa", "mib", "cob", "tjb",
    "cia", "pob", "xoa", "xob", "keep", "soa", "cib", "mja", "pia", "xia",
    "pib", "loa", "sob", "cja", "sia", "mjb", "xib", "sib", "lob", "cjb",
    "pja", "xja", "lia", "pjb", "sja", "lib", "xjb", "end", "sjb", "lja",
)


def make_pairs(mesh):
    reps = mesh.shape["rep"]

    def swap_rep(values, bit):
        return lax.ppermute(values, "rep", [(i, i ^ bit) for i in range(reps)])

    def swap_shard(values):
        return lax.ppermute(values, "shard", [(0, 1), (1, 0)])

    def line_permute(values, pairs):
        pairs = [(a * SPLIT + i, b * SPLIT + i) for a, b in pairs for i in range(SPLIT)]
        return lax.ppermute(values, "rep", pairs)

    def after(value, other):
        return lax.optimization_barrier((value, other))[0]

    def on_device(
        tokens, cotangent, lengths, qkv_weight, qkv_bias, dense_weight, dense_bias, in_weight,
        in_bias, out_weight, out_bias, norm1_gain, norm1_bias, norm2_gain, norm2_bias,
    ):
        seq_rows, width = tokens.shape
        owned = width // 2
        hidden = in_weight.shape[1]
        part_f, part_h = hidden // GROUP, width // GROUP
        rows = GROUP * seq_rows
        halves = [qkv_bias, dense_bias, out_bias, norm1_gain, norm1_bias, norm2_gain, norm2_bias]
        packed, branch_sum, in_b, in_give, qkv_give = call(
            pack_kernel,
            "pack",
            [(lengths, SCALAR)]
            + [(a, ANY) for a in [tokens, cotangent, in_bias, *halves, in_weight, qkv_weight]],
            [
                (shaped((2 * seq_rows + TAIL, width)), WHOLE),
                (shaped((1, width), F32), WHOLE),
                (shaped((1, part_f), F32), WHOLE),
                (shaped((owned, part_f)), WHOLE),
                (shaped((owned, 3 * part_h)), WHOLE),
            ],
            [pltpu.VMEM((seq_rows, width), BF16)] * 2
            + [pltpu.VMEM(v.shape, BF16) for v in [in_bias, *halves]]
            + [pltpu.SemaphoreType.DMA((14,))],
        )
        beside = swap_rep(packed, 2)
        across = swap_shard(packed)
        beyond = swap_rep(after(across, beside), 2)
        in_got = swap_shard(in_give)
        qkv_got = swap_shard(qkv_give)
        pieces = [packed, across, beside, after(beyond, in_got)]
        pieces += [swap_rep(v, 1) for v in pieces]

        normed, xhat, active, grad_before, branch, out_all, in_mine, in_theirs, params, lens, in_sum = call(
            hidden_kernel,
            "hidden",
            [(p, FREE) for p in pieces]
            + [(in_weight, ANY), (in_got, FREE), (out_weight, ANY), (in_b, WHOLE)],
            [
                (shaped((rows, width)), ANY),
                (shaped((rows, width)), ANY),
                (shaped((rows, part_f)), ANY),
                (shaped((rows, part_f)), ANY),
                (shaped((rows, width)), ANY),
                (shaped((part_f, width)), ANY),
                (shaped((owned, part_f)), ANY),
                (shaped((owned, part_f)), ANY),
                (shaped((TAIL, width), F32), WHOLE),
                (shaped((GROUP * 8, 128), F32), WHOLE),
                (shaped((1, part_f), F32), WHOLE),
            ],
            [
                pltpu.VMEM((rows, width), BF16),
                pltpu.VMEM((rows, width), BF16),
                pltpu.VMEM((GROUP, TAIL, width), BF16),
                pltpu.VMEM((width, part_f), BF16),
                pltpu.VMEM((part_f, width), BF16),
                pltpu.VMEM((rows, width), BF16),
                pltpu.VMEM((rows, width), BF16),
                pltpu.VMEM((rows, width), BF16),
                pltpu.VMEM((rows, part_f), BF16),
                pltpu.VMEM((rows, part_f), F32),
                pltpu.VMEM((rows, part_f), BF16),
                pltpu.VMEM((part_f, width), BF16),
                pltpu.VMEM((owned, part_f), BF16),
                pltpu.VMEM((owned, part_f), BF16),
                pltpu.SemaphoreType.DMA((3 * GROUP + 3 + 9,)),
            ],
        )
        in_other = swap_shard(in_theirs)

        blocks = [normed, branch, active, grad_before, xhat, lens]
        whole = [qkv_weight, qkv_got, dense_weight, out_weight, in_weight, in_got, params]
        tables = turn_tables(seq_rows, part_h)
        sizes = (width, part_h, part_f)
        line = lax.axis_index("rep") // SPLIT
        inner_line = (line == 1) | (line == 2)
        last = [params]

        def then(value):
            return after(value, last[0])

        def did(value):
            last[0] = value
            return value

        def added(left, right):
            total = (left.astype(F32) + right.astype(F32)).astype(BF16)
            return did(lax.optimization_barrier(total))

        def meet(chunk):
            return added(then(chunk), line_permute(chunk, [(0, 1), (3, 2)]))

        def cross(near):
            return added(then(near), line_permute(near, [(1, 2), (2, 1)]))

        def spread(both):
            got = line_permute(both, [(1, 0), (2, 3)])
            return did(jnp.where(inner_line, then(both), got))

        half_f = (hidden // 2, width)
        wide = 3 * part_h
        here = lambda slot, shard: shard * SPLIT + slot
        there = lambda slot, shard: (1 - shard) * SPLIT + slot
        goes = {
            "oa": ("out", half_f, part_f // 2, lambda slot, shard: 2 * slot, 0),
            "ob": ("out", half_f, part_f // 2, lambda slot, shard: 2 * slot + 1, 0),
            "ia": ("in", (owned, hidden), part_f, here, 1),
            "ib": ("in", (owned, hidden), part_f, there, 1),
        }
        totals = {"out": None, "in": None}

        far, near, joint_a, joint_theirs = attention(
            blocks, whole, tables, [in_sum, branch_sum], seq_rows, sizes
        )
        did(joint_a)
        got = line_permute(out_all, [(0, 1), (3, 2)])
        got = after(got, in_other)
        half = part_f // 2
        state = {"oa": slice(0, half), "ob": slice(half, part_f), "ia": in_mine, "ib": in_other, "ja": joint_a}
        state["jb"] = swap_shard(joint_theirs)
        for token in ORDER:
            what, name = token[0], token[1:]
            held = state.get(name)
            if what == "t":
                state[name] = then(held)
            elif what == "m":
                whole = name[0] == "o"
                state[name] = added(then(out_all)[held], got[held]) if whole else meet(held)
            elif what == "c":
                state[name] = cross(held)
            elif what == "p":
                state[name] = spread(held)
            elif what == "x":
                state[name] = [held, swap_rep(then(held), 2)]
            elif what == "s":
                state[name] = held + [swap_rep(then(v), 1) for v in held]
            elif what == "l" and name in goes:
                kind, *how = goes[name]
                totals[kind] = did(placed(totals[kind], [then(held[0])] + held[1:], *how))
            elif token == "lja":
                total_qkv, total_dense = call(
                    joint_kernel,
                    "place_joint",
                    [(then(held[0]), FREE)] + [(a, FREE) for a in held[1:]],
                    [(shaped((owned, 3 * width), F32), ANY), (shaped((owned, width), F32), ANY)],
                    [
                        pltpu.VMEM((4, owned, held[0].shape[1]), BF16),
                        pltpu.VMEM((4, owned, held[0].shape[1]), F32),
                        pltpu.SemaphoreType.DMA((4 * (4 + owned // part_h),)),
                    ],
                )
                did(total_dense)
            elif token == "far":
                far = swap_rep(then(far), 1)
            elif token == "fold":
                give = swap_rep(did(fold(then(near), far, 2 * seq_rows)), 2)
            elif token == "keep":
                keep, give = keep_sum(then(near), far, give)
                did(keep)
                give = swap_shard(give)
            elif token == "end":
                result, grad_tokens = call(
                    finish_kernel,
                    "finish",
                    [(then(lengths), SCALAR)]
                    + [(a, WHOLE) for a in (tokens, cotangent, keep, give, params)],
                    [(shaped((seq_rows, width)), WHOLE)] * 2,
                )
                did(result)
        total_out, total_in = totals["out"], totals["in"]
        joint_a, joint_b = state["ja"], state["jb"]
        sizes = [3 * owned, hidden // 2] + 6 * [owned]
        total_qkv, *vectors = pl.pallas_call(
            other_kernel,
            out_shape=[shaped(total_qkv.shape, F32)] + [shaped((n,), F32) for n in sizes],
            in_specs=[FREE] * 9,
            out_specs=[FREE] + [WHOLE] * 8,
            scratch_shapes=[
                pltpu.VMEM((4, owned + VECTORS, wide), BF16),
                pltpu.VMEM((4, owned + VECTORS, wide), F32),
                pltpu.VMEM((4, VECTORS, wide), BF16),
                pltpu.VMEM((1, width), F32),
                pltpu.VMEM((3, width), F32),
                pltpu.VMEM((1, hidden // 2), F32),
                pltpu.SemaphoreType.DMA((20,)),
            ],
            input_output_aliases={8: 0},
            compiler_params=pltpu.CompilerParams(vmem_limit_bytes=LIMIT // 3),
            cost_estimate=SMALL,
            name="place_other",
        )(*joint_a, *joint_b, total_qkv)
        qkv_b, in_b, out_b, dense_b, g1, b1, g2, b2 = vectors
        return (
            result, grad_tokens, total_qkv, qkv_b, total_dense, dense_b, total_in, in_b, total_out, out_b,
            g1, b1, g2, b2,
        )

    return on_device


def solution(mesh):
    rows = P(("rep", "shard"), None)
    vector = P("shard")
    matrix = P("shard", None)
    weights = (matrix, vector)
    in_specs = (rows, rows, P(("rep", "shard"))) + 4 * weights + 4 * (vector,)
    out_specs = (rows, rows) + 4 * weights + 4 * (vector,)
    paired = mesh.shape["shard"] == 2 and mesh.shape["rep"] == SPLIT * LINES
    body = make_pairs(mesh) if paired else make(mesh)
    return jax.shard_map(body, mesh=mesh, in_specs=in_specs, out_specs=out_specs, check_vma=False)
```

```python
import jax
import jax.numpy as jnp
import numpy as np
from jax import lax
from jax.experimental import pallas as pl
from jax.experimental.pallas import tpu as pltpu
from jax.sharding import PartitionSpec as P

HEAD_DIM = 64
ROT = 16
F32 = jnp.float32
BF16 = jnp.bfloat16
EXTRA = 16


def rotary(values, turn):
    seq_rows = values.shape[-2]
    half = ROT // 2
    inverse = 10000.0 ** (-(2.0 * jnp.arange(half).astype(F32)) / ROT)
    angles = jnp.arange(seq_rows).astype(F32)[:, None] * inverse[None, :]
    cosine = jnp.cos(angles)
    sine = jnp.sin(angles) * turn
    first = values[..., :half]
    second = values[..., half:ROT]
    return jnp.concatenate(
        [first * cosine - second * sine, second * cosine + first * sine, values[..., ROT:]],
        axis=-1,
    )


def dot(left, right):
    return jnp.dot(left, right, preferred_element_type=F32)


def dot_nt(left, right):
    return lax.dot_general(left, right, (((1,), (1,)), ((), ())), preferred_element_type=F32)


def dot_tn(left, right):
    return lax.dot_general(left, right, (((0,), (0,)), ((), ())), preferred_element_type=F32)


def plan(mesh_shape, heads):
    shards, reps = mesh_shape["shard"], mesh_shape["rep"]
    split = 1
    while split < 4 and reps % (2 * split) == 0 and heads % (2 * split * shards) == 0:
        split *= 2
    return shards, reps, split


def make(mesh):
    def on_device(
        tokens,
        cotangent,
        lengths,
        qkv_weight,
        qkv_bias,
        dense_weight,
        dense_bias,
        in_weight,
        in_bias,
        out_weight,
        out_bias,
        norm1_gain,
        norm1_bias,
        norm2_gain,
        norm2_bias,
    ):
        seq_rows, width = tokens.shape
        heads = width // HEAD_DIM
        shards, reps, split = plan(dict(mesh.shape), heads)
        lines = reps // split
        group = shards * split
        owned = width // shards
        hidden = in_weight.shape[1]
        part_f = hidden // group
        part_h = width // group
        own_heads = part_h // HEAD_DIM
        shard = lax.axis_index("shard")
        rep = lax.axis_index("rep")
        slot = lax.rem(rep, split)
        line = rep // split
        block = shard * split + slot
        bits = []
        bit = split // 2
        while bit:
            bits.append(bit)
            bit //= 2

        def swap_rep(values, bit):
            return lax.ppermute(values, "rep", [(i, i ^ bit) for i in range(reps)])

        def swap_shard(values):
            return lax.ppermute(values, "shard", [(0, 1), (1, 0)])

        def gather_shard(values):
            if shards == 1:
                return values
            if shards == 2:
                return jnp.concatenate([values, swap_shard(values)], axis=0)
            return lax.all_gather(values, "shard", axis=0, tiled=True)

        def gather_rep(values):
            for bit in bits:
                values = jnp.concatenate([values, swap_rep(values, bit)], axis=0)
            return values

        def scatter_sum(values):
            for bit in reversed(bits):
                half = values.shape[0] // 2
                values = values[:half] + swap_rep(values[half:].astype(BF16), bit).astype(F32)
            if shards == 2:
                half = values.shape[0] // 2
                values = values[:half] + swap_shard(values[half:].astype(BF16)).astype(F32)
            elif shards > 2:
                values = lax.psum_scatter(
                    values.astype(BF16), "shard", scatter_dimension=0, tiled=True
                ).astype(F32)
            return values

        def ordered(mine, other, flag, axis):
            first = jnp.where(flag, other, mine)
            second = jnp.where(flag, mine, other)
            return jnp.concatenate([first, second], axis=axis)

        def columns_of(weight, parts, size):
            rows = weight.shape[0]
            cut = weight.reshape(rows, parts, group, size)

            def piece(at):
                return lax.dynamic_slice_in_dim(cut, at, 1, 2).reshape(rows, parts * size)

            if shards == 1:
                return piece(block)
            if shards == 2:
                other = swap_shard(piece((1 - shard) * split + slot))
                return ordered(piece(block), other, shard == 1, 0)
            picked = jnp.stack([piece(s * split + slot) for s in range(shards)], axis=0)
            return lax.all_to_all(picked, "shard", 0, 0, tiled=True).reshape(
                rows * shards, parts * size
            )

        def rows_exchange(grad):
            if shards == 1:
                return [grad]
            if shards == 2:
                mine = lax.dynamic_slice_in_dim(grad, shard * owned, owned, 0)
                other = swap_shard(lax.dynamic_slice_in_dim(grad, (1 - shard) * owned, owned, 0))
                return [jnp.where(shard == 1, other, mine), jnp.where(shard == 1, mine, other)]
            got = lax.all_to_all(grad, "shard", 0, 0, tiled=True)
            return [got[s * owned : (s + 1) * owned] for s in range(shards)]

        length = lengths[0]
        live = (jnp.arange(seq_rows) < length).astype(F32)[:, None]
        branch = (live * cotangent.astype(F32)).astype(BF16)
        halves = [dense_bias, out_bias, norm1_gain, norm1_bias, norm2_gain, norm2_bias]
        params = jnp.concatenate([qkv_bias] + halves)
        params = jnp.pad(params, (0, 8 * width - params.shape[0])).reshape(8, width)
        length_rows = jnp.broadcast_to(length.astype(BF16), (EXTRA - 8, width))
        packed = jnp.concatenate([tokens, params, length_rows], axis=0)
        packed = gather_shard(packed)
        branch_all = gather_shard(branch)
        in_w = columns_of(in_weight, 1, part_f)
        packed_all = gather_rep(packed).reshape(group, seq_rows + EXTRA, width)
        branch_all = gather_rep(branch_all)
        qkv_w = columns_of(qkv_weight, 3, part_h)

        by_shard = packed.reshape(shards, seq_rows + EXTRA, width)[:, seq_rows : seq_rows + 8]
        by_shard = by_shard.reshape(shards, 8 * width)
        if shards == 2:
            by_shard = jnp.where(shard == 1, by_shard[::-1], by_shard)

        def whole(at, size):
            return by_shard[:, at : at + size].reshape(shards * size).astype(F32)

        qkv_b = whole(0, 3 * owned)
        at = 3 * owned
        full = []
        for _ in halves:
            full.append(whole(at, owned))
            at += owned
        dense_b, out_b, gain_one, shift_one, gain_two, shift_two = full
        all_lengths = packed_all[:, seq_rows + 8, 0].astype(jnp.int32)
        rows = group * seq_rows
        values = packed_all[:, :seq_rows].reshape(rows, width).astype(F32)

        centre = values - jnp.mean(values, axis=-1, keepdims=True)
        spread = jnp.mean(centre * centre, axis=-1, keepdims=True)
        root = lax.rsqrt(spread + 1e-05)
        xhat = centre * root
        normed = (xhat * gain_one + shift_one).astype(BF16)
        normed_two = (xhat * gain_two + shift_two).astype(BF16)

        out_w = lax.dynamic_slice_in_dim(out_weight, slot * part_f, part_f, 0)
        in_b = lax.dynamic_slice_in_dim(in_bias, slot * part_f, part_f, 0).astype(F32)
        before = dot(normed_two, in_w) + in_b
        cdf = 0.5 * (1.0 + lax.erf(before * (0.5**0.5)))
        active = (before * cdf).astype(BF16)
        slope = cdf + before * jnp.exp(-0.5 * before * before) * 0.3989422804014327
        grad_before = (dot_nt(branch_all, out_w) * slope).astype(BF16)
        grad_out_w = dot_tn(active, branch_all).astype(BF16)
        grad_in_w = dot_tn(normed_two, grad_before).astype(BF16)
        grad_two = dot_nt(grad_before, in_w)

        scaling = HEAD_DIM ** (-0.5)
        bias = lax.dynamic_slice_in_dim(qkv_b.reshape(3, group, part_h), block, 1, 1)
        joint = dot(normed, qkv_w) + bias.reshape(3 * part_h)
        split_joint = joint.reshape(group, seq_rows, 3, own_heads, HEAD_DIM).transpose(2, 0, 3, 1, 4)
        query = rotary(split_joint[0], 1.0).astype(BF16)
        keys = rotary(split_joint[1], 1.0).astype(BF16)
        vals = split_joint[2].astype(BF16)
        position = jnp.arange(seq_rows)
        allowed = (position[None, :] <= position[:, None])[None] & (
            position[None, None, :] < all_lengths[:, None, None]
        )
        scores = jnp.einsum("bhpd,bhqd->bhpq", query, keys, preferred_element_type=F32) * scaling
        scores = jnp.where(allowed[:, None], scores, -1e30)
        raised = jnp.exp(scores - jnp.max(scores, axis=-1, keepdims=True))
        exact = raised / jnp.sum(raised, axis=-1, keepdims=True)
        probs = exact.astype(BF16)
        context = jnp.einsum("bhpq,bhqd->bhpd", probs, vals, preferred_element_type=F32)
        context = context.astype(BF16).transpose(0, 2, 1, 3).reshape(rows, part_h)
        dense_w = lax.dynamic_slice_in_dim(dense_weight, slot * part_h, part_h, 0)
        mixed = scatter_sum(dot(active, out_w) + dot(context, dense_w))
        result = (tokens.astype(F32) + live * (mixed + dense_b + out_b)).astype(BF16)

        grad_context = dot_nt(branch_all, dense_w).astype(BF16)
        grad_dense_w = dot_tn(context, branch_all).astype(BF16)
        grad_context = grad_context.reshape(group, seq_rows, own_heads, HEAD_DIM).transpose(0, 2, 1, 3)
        grad_probs = jnp.einsum(
            "bhpd,bhqd->bhpq", grad_context, vals, preferred_element_type=F32
        )
        grad_vals = jnp.einsum("bhpq,bhpd->bhqd", probs, grad_context, preferred_element_type=F32)
        grad_scores = (
            exact * (grad_probs - jnp.sum(grad_probs * exact, axis=-1, keepdims=True))
        ).astype(BF16)
        grad_query = jnp.einsum("bhpq,bhqd->bhpd", grad_scores, keys, preferred_element_type=F32)
        grad_keys = jnp.einsum("bhpq,bhpd->bhqd", grad_scores, query, preferred_element_type=F32)
        grad_joint = jnp.stack(
            [rotary(grad_query * scaling, -1.0), rotary(grad_keys * scaling, -1.0), grad_vals]
        ).astype(BF16)
        grad_joint = grad_joint.transpose(1, 3, 0, 2, 4).reshape(rows, 3 * part_h)
        grad_qkv_w = dot_tn(normed, grad_joint).astype(BF16)
        grad_one = dot_nt(grad_joint, qkv_w)

        inner = scatter_sum(grad_one * gain_one + grad_two * gain_two)
        own_xhat = xhat[:seq_rows] if shards <= 2 else None
        if own_xhat is None:
            own_xhat = lax.dynamic_slice_in_dim(xhat, shard * seq_rows, seq_rows, 0)
            own_root = lax.dynamic_slice_in_dim(root, shard * seq_rows, seq_rows, 0)
        else:
            own_root = root[:seq_rows]
        inner = (
            inner
            - jnp.mean(inner, axis=-1, keepdims=True)
            - own_xhat * jnp.mean(inner * own_xhat, axis=-1, keepdims=True)
        ) * own_root
        grad_tokens = (cotangent.astype(F32) + inner).astype(BF16)

        in_sum = jnp.sum(grad_before.astype(F32), axis=0)
        qkv_sum = jnp.sum(grad_joint.astype(F32), axis=0).reshape(3, 1, part_h)
        vectors = jnp.concatenate(
            [
                jnp.sum(grad_one * xhat, axis=0),
                jnp.sum(grad_one, axis=0),
                jnp.sum(grad_two * xhat, axis=0),
                jnp.sum(grad_two, axis=0),
                jnp.sum(branch.astype(F32), axis=0),
                lax.dynamic_update_slice_in_dim(jnp.zeros((hidden,), F32), in_sum, block * part_f, 0),
                lax.dynamic_update_slice_in_dim(
                    jnp.zeros((3, group, part_h), F32), qkv_sum, block, 1
                ).reshape(3 * width),
            ]
        )
        vectors = lax.psum(vectors, ("rep", "shard"))

        def own_part(at, size):
            piece = size // shards
            return lax.dynamic_slice_in_dim(vectors, at + shard * piece, piece, 0)

        in_parts = rows_exchange(grad_in_w)
        qkv_parts = rows_exchange(grad_qkv_w)
        chunks = [grad_out_w] + in_parts + [grad_dense_w] + qkv_parts
        if lines == 4:
            inner_line = (line == 1) | (line == 2)

            def line_permute(values, pairs):
                return lax.ppermute(
                    values,
                    "rep",
                    [(a * split + i, b * split + i) for a, b in pairs for i in range(split)],
                )

            summed = []
            for chunk in chunks:
                got = line_permute(chunk, [(0, 1), (3, 2)])
                near = lax.optimization_barrier((chunk.astype(F32) + got.astype(F32)).astype(BF16))
                got = line_permute(near, [(1, 2), (2, 1)])
                both = lax.optimization_barrier((near.astype(F32) + got.astype(F32)).astype(BF16))
                got = line_permute(both, [(1, 0), (2, 3)])
                summed.append(jnp.where(inner_line, both, got))
        else:
            groups = [[a * split + i for a in range(lines)] for i in range(split)]
            summed = [lax.psum(c, "rep", axis_index_groups=groups) for c in chunks]

        def gather_slots(values):
            values = values[None]
            for bit in reversed(bits):
                values = ordered(values, swap_rep(values, bit), (slot & bit) != 0, 0)
            return values

        summed = [gather_slots(c) for c in summed]
        total_out = summed[0].reshape(split * part_f, width).astype(F32)
        total_in = jnp.stack(summed[1 : 1 + shards])
        total_in = total_in.transpose(2, 0, 1, 3).reshape(owned, hidden).astype(F32)
        total_dense = summed[1 + shards].reshape(split * part_h, width).astype(F32)
        total_qkv = jnp.stack(summed[2 + shards :]).reshape(shards, split, owned, 3, part_h)
        total_qkv = total_qkv.transpose(2, 3, 0, 1, 4).reshape(owned, 3 * width).astype(F32)
        at_in = 5 * width
        at_qkv = at_in + hidden
        out_sum = own_part(4 * width, width)
        return (
            result,
            grad_tokens,
            total_qkv,
            own_part(at_qkv, 3 * width),
            total_dense,
            out_sum,
            total_in,
            own_part(at_in, hidden),
            total_out,
            out_sum,
            own_part(0, width),
            own_part(width, width),
            own_part(2 * width, width),
            own_part(3 * width, width),
        )

    return on_device


GROUP = 8
SPLIT = 4
LINES = 4
TAIL = 16
VECTORS = 32
ANY = pl.BlockSpec(memory_space=pltpu.HBM)
FREE = pl.BlockSpec(memory_space=pl.ANY)
SCALAR = pl.BlockSpec(memory_space=pltpu.SMEM)
WHOLE = pl.BlockSpec(memory_space=pltpu.VMEM)
LIMIT = 63 * 2**20
COST = pl.CostEstimate(flops=10**12, bytes_accessed=10**9, transcendentals=0)
SMALL = pl.CostEstimate(flops=10**6, bytes_accessed=0, transcendentals=0)


def shaped(shape, dtype=BF16):
    return jax.ShapeDtypeStruct(shape, dtype)


def call(kernel, name, ins, outs, scratch=()):
    return pl.pallas_call(
        kernel,
        out_shape=[shape for shape, _ in outs],
        in_specs=[spec for _, spec in ins],
        out_specs=[spec for _, spec in outs],
        scratch_shapes=list(scratch),
        compiler_params=pltpu.CompilerParams(
            vmem_limit_bytes=LIMIT if name in ("pack", "hidden") else LIMIT // 3
        ),
        cost_estimate=COST if name == "hidden" else SMALL,
        name=name,
    )(*[array for array, _ in ins])


class Copies:
    def __init__(self, sems):
        self.sems, self.used = sems, 0

    def make(self, source, target):
        self.used += 1
        return pltpu.make_async_copy(source, target, self.sems.at[self.used - 1])

    def start(self, source, target):
        copy = self.make(source, target)
        copy.start()
        return copy


def place_of():
    shard = lax.axis_index("shard")
    slot = lax.rem(lax.axis_index("rep"), SPLIT)
    return shard, slot, shard * SPLIT + slot


def span(at, size):
    if isinstance(at, int):
        return pl.ds(at * size, size)
    return pl.ds(pl.multiple_of(at * size, size), size)


def pack_kernel(length, tok, cot, in_bias, qb, db, ob, g1, b1, g2, b2, in_weight, qkv_weight,
                packed, total, in_b, in_give, qkv_give, tok_v, cot_v, ib_v, qb_v, *rest):
    vecs, sems = rest[:-1], rest[-1]
    shard, slot, _ = place_of()
    twin = (1 - shard) * SPLIT + slot
    rows, width = tok_v.shape
    owned = vecs[0].shape[0]
    part_f, part_h = in_give.shape[1], qkv_give.shape[1] // 3
    copies = Copies(sems)
    first = [copies.start(tok, tok_v), copies.start(cot, cot_v), copies.start(in_bias, ib_v)]
    first.append(copies.start(qb, qb_v))
    first += [copies.start(a, b) for a, b in zip((db, ob, g1, b1, g2, b2), vecs)]
    given = [copies.start(in_weight.at[:, span(twin, part_f)], in_give)]
    for i in range(3):
        cols = pl.ds(pl.multiple_of(i * width + twin * part_h, part_h), part_h)
        target = qkv_give.at[:, i * part_h : (i + 1) * part_h]
        given.append(copies.start(qkv_weight.at[:, cols], target))
    for copy in first:
        copy.wait()
    live = lax.broadcasted_iota(jnp.int32, (rows, width), 0) < length[0]
    kept = jnp.where(live, cot_v[...].astype(F32), 0.0)
    packed[rows + TAIL :, :] = kept.astype(BF16)
    total[...] = jnp.sum(kept, axis=0, keepdims=True)
    packed[0:rows, :] = tok_v[...]
    whole = qb_v[...].astype(F32).reshape(1, 3 * owned)
    lines = [whole[:, i * owned : (i + 1) * owned] for i in range(3)]
    lines += [ref[...].astype(F32).reshape(1, owned) for ref in vecs]
    lines.append(jnp.full((TAIL - 9, owned), length[0].astype(F32)))
    packed[rows : rows + TAIL, 0:owned] = jnp.concatenate(lines, axis=0).astype(BF16)
    packed[rows : rows + TAIL, owned:width] = jnp.zeros((TAIL, width - owned), BF16)
    bias = ib_v[...].astype(F32).reshape(1, SPLIT * part_f)
    in_b[...] = sum(
        jnp.where(slot == i, bias[:, i * part_f : (i + 1) * part_f], 0.0) for i in range(SPLIT)
    )
    for copy in given:
        copy.wait()


def hidden_kernel(*refs):
    pieces, refs = refs[:GROUP], refs[GROUP:]
    (in_weight, in_got, out_weight, in_b, normed_o, xhat_o, active_o, grad_o, branch_o, out_o,
     own_o, other_o, params, lens, in_sum, every, branch, tails, w_full, out_w, normed, normed_two,
     xhat, active, slope, grad_before, grad_out, own, other, sems) = refs
    shard, slot, block = place_of()
    rows = pieces[0].shape[0] - TAIL >> 1
    owned, part = in_got.shape
    copies = Copies(sems)
    edge = [copies.start(p.at[rows : rows + TAIL, :], tails.at[i]) for i, p in enumerate(pieces)]
    first = [copies.start(p.at[0:rows, :], every.at[i * rows : (i + 1) * rows, :]) for i, p in enumerate(pieces)]
    first.append(copies.start(in_weight.at[:, span(block, part)], w_full.at[span(shard, owned), :]))
    first.append(copies.start(in_got, w_full.at[span(1 - shard, owned), :]))
    late = [copies.start(p.at[rows + TAIL :, :], branch.at[i * rows : (i + 1) * rows, :]) for i, p in enumerate(pieces)]
    late.append(copies.start(out_weight.at[span(slot, part), :], out_w))
    for copy in edge:
        copy.wait()
    params[:, span(shard, owned)] = tails[0, :, 0:owned].astype(F32)
    params[:, span(1 - shard, owned)] = tails[1, :, 0:owned].astype(F32)
    for i in range(GROUP):
        lens[i * 8 : (i + 1) * 8, :] = tails[i, :, 0:128].astype(F32)[8:]
    g1, b1, g2, b2 = (params[i : i + 1, :] for i in range(5, 9))
    for copy in first:
        copy.wait()
    step = 256

    def forward(i, carry):
        at = span(i, step)
        values = every[at, :].astype(F32)
        centre = values - jnp.mean(values, axis=-1, keepdims=True)
        spread = jnp.mean(centre * centre, axis=-1, keepdims=True)
        hat = centre * lax.rsqrt(spread + 1e-05)
        xhat[at, :] = hat.astype(BF16)
        normed[at, :] = (hat * g1 + b1).astype(BF16)
        two = (hat * g2 + b2).astype(BF16)
        normed_two[at, :] = two
        before = dot(two, w_full[...]) + in_b[...]
        cdf = 0.5 * (1.0 + lax.erf(before * (0.5**0.5)))
        active[at, :] = (before * cdf).astype(BF16)
        slope[at, :] = cdf + before * jnp.exp(-0.5 * before * before) * 0.3989422804014327
        return carry

    for i in range(GROUP * rows // step):
        forward(i, 0)
    done = [copies.start(normed, normed_o), copies.start(xhat, xhat_o), copies.start(active, active_o)]
    for copy in late:
        copy.wait()
    done.append(copies.start(branch, branch_o))

    def out_grad(j, carry):
        grad_out[span(j, step), :] = dot_tn(active[:, span(j, step)], branch[...]).astype(BF16)
        return carry

    lax.fori_loop(0, part // step, out_grad, 0)
    done.append(copies.start(grad_out, out_o))
    in_sum[...] = jnp.zeros_like(in_sum)

    def back(i, carry):
        at = span(i, step)
        grad = (dot_nt(branch[at, :], out_w[...]) * slope[at, :]).astype(BF16)
        grad_before[at, :] = grad
        in_sum[...] += jnp.sum(grad.astype(F32), axis=0, keepdims=True)
        return carry

    for i in range(GROUP * rows // step):
        back(i, 0)
    done.append(copies.start(grad_before, grad_o))
    for ref, target, where in ((other, other_o, 1 - shard), (own, own_o, shard)):

        def weight(j, carry, ref=ref, where=where):
            cols = span(where * (owned // step) + j, step)
            ref[span(j, step), :] = dot_tn(normed_two[:, cols], grad_before[...]).astype(BF16)
            return carry

        lax.fori_loop(0, owned // step, weight, 0)
        done.append(copies.start(ref, target))
    for copy in done:
        copy.wait()


def turn(values, tables, back):
    cosine, low, high = tables
    width = values.shape[1]
    ahead = pltpu.roll(values, width - ROT // 2, 1)
    behind = pltpu.roll(values, ROT // 2, 1)
    moved = ahead * low + behind * high
    return values * cosine - moved if back else values * cosine + moved


def attention_kernel(
    normed, branch, active, grad_before, xhat, lens, qkv_weight, qkv_got, dense_weight, out_weight,
    in_weight, in_got, params, cosine, low, high, in_sum, own_sum, far, near, mine_o, theirs_o,
    acc, dense, sums, jsum, vectors, w_full, dense_w, out_w, in_w, sems,
):
    shard, slot, block = place_of()
    rows, width = normed.shape
    part = dense_w.shape[0]
    owned, hidden = in_got.shape
    step = pl.program_id(0)

    copies = Copies(sems)
    mine, theirs = span(shard, owned), span(1 - shard, owned)
    early = [copies.make(qkv_got, w_full.at[theirs, :])]
    for i in range(3):
        cols = pl.ds(pl.multiple_of(i * width + block * part, part), part)
        target = w_full.at[mine, i * part : (i + 1) * part]
        early.append(copies.make(qkv_weight.at[:, cols], target))
    early.append(copies.make(dense_weight.at[span(slot, part), :], dense_w))
    late = [copies.make(out_weight.at[span(slot, hidden), :], out_w)]
    late.append(copies.make(in_weight.at[:, span(block, hidden)], in_w.at[mine, :]))
    late.append(copies.make(in_got, in_w.at[theirs, :]))

    @pl.when(step == 0)
    def _():
        for copy in early + late:
            copy.start()
        for ref in (acc, dense, sums, jsum):
            ref[...] = jnp.zeros_like(ref)
        for copy in early:
            copy.wait()

    scaling = HEAD_DIM**-0.5
    biases = []
    for i in range(3):
        at = i * width + block * part
        inside = lax.rem(at, 3 * owned)
        col = at // (3 * owned) * owned + lax.rem(inside, owned)
        cols = pl.ds(pl.multiple_of(col, part), part)
        biases.append(
            sum(jnp.where(inside // owned == r, params[r : r + 1, cols], 0.0) for r in range(3))
        )
    joint = dot(normed[...], w_full[...]) + jnp.concatenate(biases, axis=1)
    grad_context = dot_nt(branch[...], dense_w[...]).astype(BF16)
    seq = cosine.shape[0]
    tables = (cosine[...], low[...], high[...])
    at_p = lax.broadcasted_iota(jnp.int32, (seq, seq), 0)
    at_q = lax.broadcasted_iota(jnp.int32, (seq, seq), 1)
    head_of = lax.broadcasted_iota(jnp.int32, (seq, part), 1) // HEAD_DIM

    def apart(values):
        zero = jnp.zeros_like(values)
        return jnp.concatenate(
            [jnp.where(head_of == h, values, zero) for h in range(part // HEAD_DIM)], axis=0
        )

    def together(values):
        total = values[0:seq]
        for h in range(1, part // HEAD_DIM):
            total = jnp.where(head_of == h, values[h * seq : (h + 1) * seq], total)
        return total

    contexts, grads = [], []
    for one in range(rows // seq):
        at = slice(one * seq, (one + 1) * seq)
        query = turn(joint[at, 0:part], tables, False).astype(BF16)
        keys = turn(joint[at, part : 2 * part], tables, False).astype(BF16)
        vals = joint[at, 2 * part :].astype(BF16)
        allowed = (at_q <= at_p) & (at_q.astype(F32) < lens[8 * one + 7 : 8 * one + 8, :])
        gc = grad_context[at, :]
        keys_apart, vals_apart = apart(keys), apart(vals)
        scores = dot_nt(query, keys_apart) * scaling
        heads = range(part // HEAD_DIM)
        exact = []
        for head in heads:
            masked = jnp.where(allowed, scores[:, head * seq : (head + 1) * seq], -1e30)
            raised = jnp.exp(masked - jnp.max(masked, axis=-1, keepdims=True))
            exact.append(raised / jnp.sum(raised, axis=-1, keepdims=True))
        probs = jnp.concatenate(exact, axis=1).astype(BF16)
        contexts.append(dot(probs, vals_apart).astype(BF16))
        grad_probs = dot_nt(gc, vals_apart)
        grad_vals = together(dot_tn(probs, gc))
        grad_scores = []
        for head in heads:
            grad = grad_probs[:, head * seq : (head + 1) * seq]
            mean = jnp.sum(grad * exact[head], axis=-1, keepdims=True)
            grad_scores.append((exact[head] * (grad - mean)).astype(BF16))
        grad_scores = jnp.concatenate(grad_scores, axis=1)
        grad_query = turn(dot(grad_scores, keys_apart) * scaling, tables, True)
        grad_keys = turn(together(dot_tn(grad_scores, query)) * scaling, tables, True)
        grads.append(jnp.concatenate([grad_query, grad_keys, grad_vals], axis=1).astype(BF16))
    ctx = jnp.concatenate(contexts, axis=0)
    grad = jnp.concatenate(grads, axis=0)
    jsum[...] += jnp.sum(grad.astype(F32), axis=0, keepdims=True)
    acc[...] += dot_tn(normed[...], grad)
    dense[...] += dot_tn(ctx, branch[...])

    @pl.when(step == 0)
    def _():
        for copy in late:
            copy.wait()

    mixed = (dot(active[...], out_w[...]) + dot(ctx, dense_w[...])).astype(BF16)
    hat = xhat[...].astype(F32)
    one = dot_nt(grad, w_full[...])
    sums[0:1, :] += jnp.sum(one * hat, axis=0, keepdims=True)
    sums[1:2, :] += jnp.sum(one, axis=0, keepdims=True)
    two = dot_nt(grad_before[...], in_w[...])
    sums[2:3, :] += jnp.sum(two * hat, axis=0, keepdims=True)
    sums[3:4, :] += jnp.sum(two, axis=0, keepdims=True)
    inner = (one * params[5:6, :] + two * params[7:8, :]).astype(BF16)
    for ref, here in ((far, step < 2), (near, step >= 2)):

        @pl.when(here)
        def _(ref=ref):
            ref[:, 0:width] = mixed
            ref[:, width:] = inner

    @pl.when(step == pl.num_programs(0) - 1)
    def _():
        wide = 3 * part
        vectors[...] = jnp.zeros_like(vectors)
        row = 0
        for source in [sums[i : i + 1, :] for i in range(4)] + [own_sum[...], in_sum[...], jsum[...]]:
            for at in range(0, source.shape[1], wide):
                piece = source[:, at : at + wide]
                vectors[row : row + 1, 0 : piece.shape[1]] = piece
                row += 1
        for ref, which in ((mine_o, shard), (theirs_o, 1 - shard)):
            ref[0:owned, 0:wide] = acc[span(which, owned), :].astype(BF16)
            ref[owned:, 0:wide] = vectors[...].astype(BF16)
        each = width * part // owned
        for i in range(owned // part):
            cols = slice(i * each, (i + 1) * each)
            mine_o[i * part : (i + 1) * part, wide:] = dense[:, cols].astype(BF16)
        mine_o[owned:, wide:] = jnp.zeros((VECTORS, each), BF16)


def attention(blocks, whole, tables, small, seq_rows, sizes):
    width, part, hidden = sizes
    rows, steps = 2 * seq_rows, 4
    owned, wide = width // 2, 3 * part

    def block(array, height):
        return pl.BlockSpec((height, array.shape[1]), lambda i: ((i + 2) % 4, 0))

    def full(shape):
        return pl.BlockSpec(shape, lambda i: (0, 0))

    outer = pl.BlockSpec((rows, 2 * width), lambda i: (jnp.minimum(i, 1), 0))
    inner = pl.BlockSpec((rows, 2 * width), lambda i: (jnp.maximum(i - 2, 0), 0))
    mine = (owned + VECTORS, wide + width * part // owned)
    theirs = (owned + VECTORS, wide)
    half = shaped((2 * rows, 2 * width))
    args = [*blocks, *whole, *tables, *small]
    specs = [block(a, h) for a, h in zip(blocks, [rows] * 5 + [16])]
    specs += [ANY, FREE, ANY, ANY, ANY, FREE] + [full(a.shape) for a in [whole[6], *tables, *small]]
    sums = [(width, wide), (part, width), (8, width), (1, wide), (VECTORS, wide)]
    weights = [(width, wide), (part, width), (hidden, width), (width, hidden)]
    return pl.pallas_call(
        attention_kernel,
        grid=(steps,),
        out_shape=[half, half, shaped(mine), shaped(theirs)],
        in_specs=specs,
        out_specs=[outer, inner, full(mine), full(theirs)],
        scratch_shapes=[pltpu.VMEM(s, F32) for s in sums]
        + [pltpu.VMEM(s, BF16) for s in weights]
        + [pltpu.SemaphoreType.DMA((8,))],
        compiler_params=pltpu.CompilerParams(vmem_limit_bytes=LIMIT),
        cost_estimate=COST,
        name="attention",
    )(*args)


def placed(held, pieces, shape, size, where, parts=1):
    count = len(pieces)
    per = shape[1] // max(parts, 1)
    height = pieces[0].shape[0] if parts else size
    held_shape = (count, height, pieces[0].shape[1])

    def kernel(*refs):
        ins, (out, raw, wide, sems) = refs[:count], refs[-4:]
        shard, slot, _ = place_of()
        copies = Copies(sems)
        loads = [copies.start(ref.at[0:height, :], raw.at[j]) for j, ref in enumerate(ins)]
        stores = []
        for j in range(count):
            loads[j].wait()
            wide[j] = raw[j].astype(F32)
            at = where(slot ^ (0, 2, 1, 3)[j], shard)
            if parts == 0:
                stores.append(copies.start(wide.at[j], out.at[span(at, size), :]))
            for i in range(parts):
                cols = pl.ds(pl.multiple_of(i * per + at * size, size), size)
                source = wide.at[j, :, i * size : (i + 1) * size]
                stores.append(copies.start(source, out.at[:, cols]))
        for copy in stores:
            copy.wait()

    args = list(pieces) + ([] if held is None else [held])
    return pl.pallas_call(
        kernel,
        in_specs=[pl.BlockSpec(memory_space=pl.ANY)] * len(args),
        out_specs=pl.BlockSpec(memory_space=pl.ANY),
        out_shape=shaped(shape, F32),
        scratch_shapes=[
            pltpu.VMEM(held_shape, BF16),
            pltpu.VMEM(held_shape, F32),
            pltpu.SemaphoreType.DMA((count * (1 + max(parts, 1)),)),
        ],
        input_output_aliases={} if held is None else {count: 0},
        compiler_params=pltpu.CompilerParams(vmem_limit_bytes=LIMIT // 2),
        cost_estimate=SMALL,
        name="place",
    )(*args)


def fold(left, right, rows=None, name="fold"):
    count = rows or left.shape[0]
    shape = (count, left.shape[1])

    def kernel(a, b, out, a_v, b_v, sems):
        copies = Copies(sems)
        first = copies.start(a.at[a.shape[0] - count :, :], a_v)
        second = copies.start(b.at[b.shape[0] - count :, :], b_v)
        first.wait()
        second.wait()
        a_v[...] = (a_v[...].astype(F32) + b_v[...].astype(F32)).astype(BF16)
        copies.start(a_v, out).wait()

    scratch = [pltpu.VMEM(shape, BF16)] * 2 + [pltpu.SemaphoreType.DMA((3,))]
    return call(kernel, name, [(left, FREE), (right, FREE)], [(shaped(shape), FREE)], scratch)[0]


def keep_sum(near, far, got):
    count, width = got.shape[0] // 2, got.shape[1]

    def kernel(a, b, c, own, give, a_v, b_v, c_v, o_v, sems):
        copies = Copies(sems)
        loads = [copies.start(r.at[0 : 2 * count, :], v) for r, v in ((a, a_v), (b, b_v), (c, c_v))]
        for copy in loads:
            copy.wait()
        total = a_v[...].astype(F32) + b_v[...].astype(F32) + c_v[...].astype(F32)
        o_v[...] = total[0:count, :]
        a_v[0:count, :] = total[count:, :].astype(BF16)
        stores = [copies.start(o_v, own), copies.start(a_v.at[0:count, :], give)]
        for copy in stores:
            copy.wait()

    scratch = [pltpu.VMEM((2 * count, width), BF16)] * 3 + [pltpu.VMEM((count, width), F32)]
    return call(
        kernel,
        "keep",
        [(near, FREE), (far, FREE), (got, FREE)],
        [(shaped((count, width), F32), ANY), (shaped((count, width)), ANY)],
        scratch + [pltpu.SemaphoreType.DMA((5,))],
    )


def joint_kernel(*refs):
    ins, (total, dense, raw, wide, sems) = refs[:4], refs[4:]
    shard, slot, _ = place_of()
    owned = total.shape[0]
    part = dense.shape[0] // SPLIT
    copies = Copies(sems)
    loads = [copies.start(ref.at[0:owned, :], raw.at[j]) for j, ref in enumerate(ins)]
    stores = []
    for j in range(4):
        loads[j].wait()
        wide[j] = raw[j].astype(F32)
        at = slot ^ (0, 2, 1, 3)[j]
        for i in range(3):
            where = i * (total.shape[1] // 3) + (shard * SPLIT + at) * part
            cols = pl.ds(pl.multiple_of(where, part), part)
            stores.append(copies.start(wide.at[j, :, i * part : (i + 1) * part], total.at[:, cols]))
        each = raw.shape[2] - 3 * part
        for i in range(owned // part):
            source = wide.at[j, i * part : (i + 1) * part, 3 * part :]
            target = dense.at[span(at, part), i * each : (i + 1) * each]
            stores.append(copies.start(source, target))
    for copy in stores:
        copy.wait()


def other_kernel(*refs):
    own, ins, refs = refs[:4], refs[4:8], refs[9:]
    total, qkv_o, in_o, out_o, dense_o, g1, b1, g2, b2, raw, wide, edge, flat, joint, in_b, sems = refs
    shard, slot, _ = place_of()
    owned = total.shape[0]
    width = total.shape[1] // 3
    part = raw.shape[2] // 3
    hidden = in_o.shape[0] // SPLIT
    copies = Copies(sems)
    edges = [copies.start(ref.at[owned:, 0 : 3 * part], edge.at[j]) for j, ref in enumerate(own)]
    loads = [copies.start(ref, raw.at[j]) for j, ref in enumerate(ins)]
    stores = []
    for j in range(4):
        loads[j].wait()
        wide[j] = raw[j].astype(F32)
        at = slot ^ (0, 2, 1, 3)[j]
        for i in range(3):
            where = i * width + ((1 - shard) * SPLIT + at) * part
            cols = pl.ds(pl.multiple_of(where, part), part)
            source = wide.at[j, 0:owned, i * part : (i + 1) * part]
            stores.append(copies.start(source, total.at[:, cols]))
    for copy in edges:
        copy.wait()
    mine = [edge[j].astype(F32) for j in range(4)]
    theirs = [wide[j, owned:, :] for j in range(4)]
    every = sum(mine) + sum(theirs)
    per = -(-width // (3 * part))
    for i, vectors in enumerate(((g1,), (b1,), (g2,), (b2,), (out_o, dense_o))):
        flat[...] = jnp.concatenate([every[i * per + k : i * per + k + 1] for k in range(per)], axis=1)[:, 0:width]
        for ref in vectors:
            ref[...] = flat[:, span(shard, owned)].reshape(owned)
    row = 5 * per
    long = -(-hidden // (3 * part))
    for j in range(4):
        at = slot ^ (0, 2, 1, 3)[j]
        sums = jnp.concatenate([mine[j][row + k : row + k + 1] for k in range(long)], axis=1)
        in_b[:, span(at, hidden)] = sums[:, 0:hidden]
        for values, group in ((mine[j], shard), (theirs[j], 1 - shard)):
            for i in range(3):
                piece = values[row + long : row + long + 1, i * part : (i + 1) * part]
                joint[i : i + 1, span(group * SPLIT + at, part)] = piece
    thirds = [joint[i : i + 1, k * owned : (k + 1) * owned] for i in range(3) for k in range(2)]
    for i in range(3):
        third = jnp.where(shard == 0, thirds[i], thirds[3 + i])
        qkv_o[i * owned : (i + 1) * owned] = third.reshape(owned)
    in_o[...] = in_b[...].reshape(in_o.shape)
    for copy in stores:
        copy.wait()


def finish_kernel(length, tok, cot, own, got, params, result, grad_tokens):
    rows, width = tok.shape
    live = lax.broadcasted_iota(jnp.int32, (rows, width), 0) < length[0]
    values = tok[...].astype(F32)
    mixed = own[:, 0:width] + got[:, 0:width].astype(F32) + params[3:4, :] + params[4:5, :]
    result[...] = (values + jnp.where(live, mixed, 0.0)).astype(BF16)
    centre = values - jnp.mean(values, axis=-1, keepdims=True)
    root = lax.rsqrt(jnp.mean(centre * centre, axis=-1, keepdims=True) + 1e-05)
    hat = centre * root
    inner = own[:, width:] + got[:, width:].astype(F32)
    inner = inner - jnp.mean(inner, axis=-1, keepdims=True) - hat * jnp.mean(inner * hat, axis=-1, keepdims=True)
    grad_tokens[...] = (cot[...].astype(F32) + inner * root).astype(BF16)


def turn_tables(seq_rows, columns):
    half = ROT // 2
    inverse = np.float32(10000.0) ** (-(2.0 * np.arange(half, dtype=np.float32)) / np.float32(ROT))
    angles = np.arange(seq_rows, dtype=np.float32)[:, None] * inverse.astype(np.float32)[None, :]
    cosine = np.ones((seq_rows, HEAD_DIM), np.float32)
    low = np.zeros((seq_rows, HEAD_DIM), np.float32)
    high = np.zeros((seq_rows, HEAD_DIM), np.float32)
    cosine[:, :half] = cosine[:, half:ROT] = np.cos(angles)
    low[:, :half] = -np.sin(angles)
    high[:, half:ROT] = np.sin(angles)
    return [jnp.asarray(np.tile(t, (1, columns // HEAD_DIM))) for t in (cosine, low, high)]


ORDER = (
    "far", "moa", "mob", "coa", "mia", "fold", "poa", "mib", "cob", "tjb",
    "cia", "pob", "xoa", "xob", "keep", "soa", "cib", "mja", "pia", "xia",
    "pib", "loa", "sob", "cja", "sia", "mjb", "xib", "sib", "lob", "cjb",
    "pja", "xja", "end", "lia", "pjb", "sja", "lib", "xjb", "sjb", "lja",
)


def make_pairs(mesh):
    reps = mesh.shape["rep"]

    def swap_rep(values, bit):
        return lax.ppermute(values, "rep", [(i, i ^ bit) for i in range(reps)])

    def swap_shard(values):
        return lax.ppermute(values, "shard", [(0, 1), (1, 0)])

    def line_permute(values, pairs):
        pairs = [(a * SPLIT + i, b * SPLIT + i) for a, b in pairs for i in range(SPLIT)]
        return lax.ppermute(values, "rep", pairs)

    def after(value, other):
        return lax.optimization_barrier((value, other))[0]

    def on_device(
        tokens, cotangent, lengths, qkv_weight, qkv_bias, dense_weight, dense_bias, in_weight,
        in_bias, out_weight, out_bias, norm1_gain, norm1_bias, norm2_gain, norm2_bias,
    ):
        seq_rows, width = tokens.shape
        owned = width // 2
        hidden = in_weight.shape[1]
        part_f, part_h = hidden // GROUP, width // GROUP
        rows = GROUP * seq_rows
        halves = [qkv_bias, dense_bias, out_bias, norm1_gain, norm1_bias, norm2_gain, norm2_bias]
        packed, branch_sum, in_b, in_give, qkv_give = call(
            pack_kernel,
            "pack",
            [(lengths, SCALAR)]
            + [(a, ANY) for a in [tokens, cotangent, in_bias, *halves, in_weight, qkv_weight]],
            [
                (shaped((2 * seq_rows + TAIL, width)), WHOLE),
                (shaped((1, width), F32), WHOLE),
                (shaped((1, part_f), F32), WHOLE),
                (shaped((owned, part_f)), WHOLE),
                (shaped((owned, 3 * part_h)), WHOLE),
            ],
            [pltpu.VMEM((seq_rows, width), BF16)] * 2
            + [pltpu.VMEM(v.shape, BF16) for v in [in_bias, *halves]]
            + [pltpu.SemaphoreType.DMA((14,))],
        )
        beside = swap_rep(packed, 2)
        across = swap_shard(packed)
        beyond = swap_rep(after(across, beside), 2)
        in_got = swap_shard(in_give)
        qkv_got = swap_shard(qkv_give)
        pieces = [packed, across, beside, after(beyond, in_got)]
        pieces += [swap_rep(v, 1) for v in pieces]

        normed, xhat, active, grad_before, branch, out_all, in_mine, in_theirs, params, lens, in_sum = call(
            hidden_kernel,
            "hidden",
            [(p, FREE) for p in pieces]
            + [(in_weight, ANY), (in_got, FREE), (out_weight, ANY), (in_b, WHOLE)],
            [
                (shaped((rows, width)), ANY),
                (shaped((rows, width)), ANY),
                (shaped((rows, part_f)), ANY),
                (shaped((rows, part_f)), ANY),
                (shaped((rows, width)), ANY),
                (shaped((part_f, width)), ANY),
                (shaped((owned, part_f)), ANY),
                (shaped((owned, part_f)), ANY),
                (shaped((TAIL, width), F32), WHOLE),
                (shaped((GROUP * 8, 128), F32), WHOLE),
                (shaped((1, part_f), F32), WHOLE),
            ],
            [
                pltpu.VMEM((rows, width), BF16),
                pltpu.VMEM((rows, width), BF16),
                pltpu.VMEM((GROUP, TAIL, width), BF16),
                pltpu.VMEM((width, part_f), BF16),
                pltpu.VMEM((part_f, width), BF16),
                pltpu.VMEM((rows, width), BF16),
                pltpu.VMEM((rows, width), BF16),
                pltpu.VMEM((rows, width), BF16),
                pltpu.VMEM((rows, part_f), BF16),
                pltpu.VMEM((rows, part_f), F32),
                pltpu.VMEM((rows, part_f), BF16),
                pltpu.VMEM((part_f, width), BF16),
                pltpu.VMEM((owned, part_f), BF16),
                pltpu.VMEM((owned, part_f), BF16),
                pltpu.SemaphoreType.DMA((3 * GROUP + 3 + 9,)),
            ],
        )
        in_other = swap_shard(in_theirs)

        blocks = [normed, branch, active, grad_before, xhat, lens]
        whole = [qkv_weight, qkv_got, dense_weight, out_weight, in_weight, in_got, params]
        tables = turn_tables(seq_rows, part_h)
        sizes = (width, part_h, part_f)
        line = lax.axis_index("rep") // SPLIT
        inner_line = (line == 1) | (line == 2)
        last = [params]

        def then(value):
            return after(value, last[0])

        def did(value):
            last[0] = value
            return value

        def added(left, right):
            total = (left.astype(F32) + right.astype(F32)).astype(BF16)
            return did(lax.optimization_barrier(total))

        def meet(chunk):
            return added(then(chunk), line_permute(chunk, [(0, 1), (3, 2)]))

        def cross(near):
            return added(then(near), line_permute(near, [(1, 2), (2, 1)]))

        def spread(both):
            got = line_permute(both, [(1, 0), (2, 3)])
            return did(jnp.where(inner_line, then(both), got))

        half_f = (hidden // 2, width)
        wide = 3 * part_h
        here = lambda slot, shard: shard * SPLIT + slot
        there = lambda slot, shard: (1 - shard) * SPLIT + slot
        goes = {
            "oa": ("out", half_f, part_f // 2, lambda slot, shard: 2 * slot, 0),
            "ob": ("out", half_f, part_f // 2, lambda slot, shard: 2 * slot + 1, 0),
            "ia": ("in", (owned, hidden), part_f, here, 1),
            "ib": ("in", (owned, hidden), part_f, there, 1),
        }
        totals = {"out": None, "in": None}

        far, near, joint_a, joint_theirs = attention(
            blocks, whole, tables, [in_sum, branch_sum], seq_rows, sizes
        )
        did(joint_a)
        got = line_permute(out_all, [(0, 1), (3, 2)])
        got = after(got, in_other)
        half = part_f // 2
        state = {"oa": slice(0, half), "ob": slice(half, part_f), "ia": in_mine, "ib": in_other, "ja": joint_a}
        state["jb"] = swap_shard(joint_theirs)
        for token in ORDER:
            what, name = token[0], token[1:]
            held = state.get(name)
            if what == "t":
                state[name] = then(held)
            elif what == "m":
                whole = name[0] == "o"
                state[name] = added(then(out_all)[held], got[held]) if whole else meet(held)
            elif what == "c":
                state[name] = cross(held)
            elif what == "p":
                state[name] = spread(held)
            elif what == "x":
                state[name] = [held, swap_rep(then(held), 2)]
            elif what == "s":
                state[name] = held + [swap_rep(then(v), 1) for v in held]
            elif what == "l" and name in goes:
                kind, *how = goes[name]
                totals[kind] = did(placed(totals[kind], [then(held[0])] + held[1:], *how))
            elif token == "lja":
                total_qkv, total_dense = call(
                    joint_kernel,
                    "place_joint",
                    [(then(held[0]), FREE)] + [(a, FREE) for a in held[1:]],
                    [(shaped((owned, 3 * width), F32), ANY), (shaped((owned, width), F32), ANY)],
                    [
                        pltpu.VMEM((4, owned, held[0].shape[1]), BF16),
                        pltpu.VMEM((4, owned, held[0].shape[1]), F32),
                        pltpu.SemaphoreType.DMA((4 * (4 + owned // part_h),)),
                    ],
                )
                did(total_dense)
            elif token == "far":
                far = swap_rep(then(far), 1)
            elif token == "fold":
                give = swap_rep(did(fold(then(near), far, 2 * seq_rows)), 2)
            elif token == "keep":
                keep, give = keep_sum(then(near), far, give)
                did(keep)
                give = swap_shard(give)
            elif token == "end":
                result, grad_tokens = call(
                    finish_kernel,
                    "finish",
                    [(then(lengths), SCALAR)]
                    + [(a, WHOLE) for a in (tokens, cotangent, keep, give, params)],
                    [(shaped((seq_rows, width)), WHOLE)] * 2,
                )
                did(result)
        total_out, total_in = totals["out"], totals["in"]
        joint_a, joint_b = state["ja"], state["jb"]
        sizes = [3 * owned, hidden // 2] + 6 * [owned]
        total_qkv, *vectors = pl.pallas_call(
            other_kernel,
            out_shape=[shaped(total_qkv.shape, F32)] + [shaped((n,), F32) for n in sizes],
            in_specs=[FREE] * 9,
            out_specs=[FREE] + [WHOLE] * 8,
            scratch_shapes=[
                pltpu.VMEM((4, owned + VECTORS, wide), BF16),
                pltpu.VMEM((4, owned + VECTORS, wide), F32),
                pltpu.VMEM((4, VECTORS, wide), BF16),
                pltpu.VMEM((1, width), F32),
                pltpu.VMEM((3, width), F32),
                pltpu.VMEM((1, hidden // 2), F32),
                pltpu.SemaphoreType.DMA((20,)),
            ],
            input_output_aliases={8: 0},
            compiler_params=pltpu.CompilerParams(vmem_limit_bytes=LIMIT // 3),
            cost_estimate=SMALL,
            name="place_other",
        )(*joint_a, *joint_b, total_qkv)
        qkv_b, in_b, out_b, dense_b, g1, b1, g2, b2 = vectors
        return (
            result, grad_tokens, total_qkv, qkv_b, total_dense, dense_b, total_in, in_b, total_out, out_b,
            g1, b1, g2, b2,
        )

    return on_device


def solution(mesh):
    rows = P(("rep", "shard"), None)
    vector = P("shard")
    matrix = P("shard", None)
    weights = (matrix, vector)
    in_specs = (rows, rows, P(("rep", "shard"))) + 4 * weights + 4 * (vector,)
    out_specs = (rows, rows) + 4 * weights + 4 * (vector,)
    paired = mesh.shape["shard"] == 2 and mesh.shape["rep"] == SPLIT * LINES
    body = make_pairs(mesh) if paired else make(mesh)
    return jax.shard_map(body, mesh=mesh, in_specs=in_specs, out_specs=out_specs, check_vma=False)
```
